256 devices in a mesh: wide: 32 (over z, x), narrow: 8 (over y, core).
Axes of the slice: x: 4, y: 4, z: 8, core: 2. Of those that a mesh axis runs over, the one named last changes fastest.
Arguments:
- tractions: float32 [64, 16, 3, 256], P('wide', 'narrow'), may hold values from -6 to 6
- centers: float32 [64, 16, 3], P('wide', 'narrow'), may hold values from 0 to 272, as said below
- node_offsets: float32 [3, 256], replicated, may hold values from -3 to 3
- occupied: int32 [64, 16], P('wide', 'narrow'), may hold values from 0 to 1, as said below
- anchors: int32 [64, 16, 3], P('wide', 'narrow'), may hold values from 0 to 255, as said below
- near_list: int32 [64, 16, 2], P('wide', 'narrow'), may hold values from 0 to 1023, as said below
- contact_pairs: int32 [2, 8192], P(None, ('wide', 'narrow')), may hold values from 0 to 1023, as said below
- contact_gap: float32 [8192], P(('wide', 'narrow')), may hold values from -1 to 1
- contact_angles: float32 [2, 8192], P(None, ('wide', 'narrow')), may hold values from -3.140625 to 3.140625
Outputs:
- node_velocity: float32 [64, 16, 3, 256], P('wide', 'narrow')
- contact_force: float32 [8192], P(('wide', 'narrow'))
- moved_centers: float32 [64, 16, 3], P('wide', 'narrow')
The draws below stay inside these ranges and needn't reach their ends.
Inputs may be any that keep to these rules, and one draw needn't show every extreme that they name: `occupied`: in every device's 2 x 2 block of slots the live slots come first in row-major order, and each device holds at least one; some device has all 4 slots live. `anchors`: for a slot of the device with indices w along wide and n along narrow, the first entry lies in [w * 8, (w + 1) * 8) and the second in [n * 32, (n + 1) * 32). `centers`: each component of a centre is its slot's anchor entry plus 16/2 plus at most 0.5 either way. `near_list`: entries of live slots name live spheres other than the slot's own, held by the same device or by one whose wide and narrow indices each differ by at most one, cyclically; entries may repeat. `contact_pairs`: the first sphere of a contact is live and held by the device that holds the contact; the second is an entry of the first's near list.
All inputs are finite; a program needn't handle non-finite values.
Results may differ from the reference program's by a relative error of at most 0.0003.
Values sent between devices are 32-bit elements; how exact they have to be, the bound alone decides.
A program may use at most 128 MiB of HBM per device.

```python
import jax
import jax.numpy as jnp
from jax import lax

NODES = 256
GRID = 256
BLOCK = 16
NEAR = 2
SWEEPS = 6
S_SIDE = 2
CONT_DEV = 32
ROWS = 64
COLS = 16
SLOTS = 1024
CONTACTS = 8192
N_WIDE = 32
N_NARROW = 8


def to_grid(array):
    trailing = array.shape[2:]
    shaped = array.reshape((N_WIDE, N_NARROW, S_SIDE, S_SIDE) + trailing)
    return jnp.swapaxes(shaped, 1, 2).reshape((S_SIDE * N_WIDE, S_SIDE * N_NARROW) + trailing)


def geometry(key):
    folded = jax.random.fold_in(key, 31)
    streams = jax.random.split(folded, 12)
    devices_all = N_WIDE * N_NARROW
    per_device = S_SIDE * S_SIDE
    device_ids = jnp.arange(devices_all, dtype=jnp.int32)
    counts = jax.random.randint(streams[0], (devices_all,), 1, per_device + 1, dtype=jnp.int32)
    busiest = jax.random.randint(streams[1], (), 0, devices_all, dtype=jnp.int32)
    counts = jnp.where(device_ids == busiest, per_device, counts)
    slot_ids = jnp.arange(per_device, dtype=jnp.int32)
    occupied = (slot_ids[None, :] < counts[:, None]).astype(jnp.int32)
    wide_ids = device_ids // N_NARROW
    narrow_ids = device_ids % N_NARROW
    side_x = slot_ids % 2
    side_y = slot_ids // 2 % 2
    corner_ids = jnp.arange(4, dtype=jnp.int32)
    corner_x = corner_ids % 2
    corner_y = corner_ids // 2
    partner_w = (wide_ids[:, None, None] + side_x[None, :, None] - corner_x[None, None, :]) % N_WIDE
    partner_n = (narrow_ids[:, None, None] + side_y[None, :, None] - corner_y[None, None, :]) % N_NARROW
    partners = (partner_w * N_NARROW + partner_n).astype(jnp.int32)
    live_cand = slot_ids[None, None, None, :] < counts[partners][..., None]
    type_cand = (side_x[None, None, None, :] == corner_x[None, None, :, None]) & (side_y[None, None, None, :] == corner_y[None, None, :, None])
    self_cand = (partners[..., None] == device_ids[:, None, None, None]) & (slot_ids[None, None, None, :] == slot_ids[None, :, None, None])
    same_corner = live_cand & type_cand & ~self_cand
    any_valid = live_cand & ~self_cand
    priority = same_corner.astype(jnp.int32) * 2 ** 26 + any_valid.astype(jnp.int32) * 2 ** 25
    priority = priority.reshape(devices_all, per_device, 1, 4 * per_device)
    near_shape = (devices_all, per_device, NEAR, 4 * per_device)
    noise = jax.random.randint(streams[2], near_shape, 0, 2 ** 16, dtype=jnp.int32) * (4 * per_device) + jnp.arange(4 * per_device, dtype=jnp.int32)
    scores = noise + priority
    best = lax.top_k(scores, 1)[1][..., 0].astype(jnp.int32)
    corner_pick = best // per_device
    slot_pick = best % per_device
    chosen = jnp.sum(jnp.where(corner_pick[..., None] == corner_ids, partners[:, :, None, :], 0), axis=-1).astype(jnp.int32)
    near_ids = (chosen * per_device + slot_pick).astype(jnp.int32)
    contact_shape = (devices_all, CONT_DEV)
    first_local = jax.random.randint(streams[6], contact_shape, 0, counts[:, None], dtype=jnp.int32)
    which_entry = jax.random.randint(streams[7], contact_shape, 0, NEAR, dtype=jnp.int32)
    second_ids = near_ids[device_ids[:, None], first_local, which_entry]
    first_ids = device_ids[:, None] * per_device + first_local
    pairs = jnp.stack([first_ids.reshape(-1), second_ids.reshape(-1)]).astype(jnp.int32)
    anchor_shape = (devices_all, per_device)
    pencil_x = GRID // N_WIDE
    pencil_y = GRID // N_NARROW
    step_x = jnp.minimum(jax.random.randint(streams[8], anchor_shape, 0, 2, dtype=jnp.int32), pencil_x - 1)
    step_y = jnp.minimum(jax.random.randint(streams[9], anchor_shape, 0, 2, dtype=jnp.int32), pencil_y - 1)
    anchor_x = wide_ids[:, None] * pencil_x + jnp.where(side_x[None, :] == 1, pencil_x - 1 - step_x, step_x)
    anchor_y = narrow_ids[:, None] * pencil_y + jnp.where(side_y[None, :] == 1, pencil_y - 1 - step_y, step_y)
    corner_w = (wide_ids[:, None] + side_x[None, :]) % N_WIDE
    corner_n = (narrow_ids[:, None] + side_y[None, :]) % N_NARROW
    base_z = jax.random.randint(streams[10], (devices_all,), 0, GRID, dtype=jnp.int32)
    step_z = jax.random.randint(streams[11], anchor_shape, 0, 3, dtype=jnp.int32)
    anchor_z = (base_z[corner_w * N_NARROW + corner_n] + step_z) % GRID
    anchors = jnp.stack([anchor_x, anchor_y, anchor_z], axis=-1).astype(jnp.int32)
    return (to_grid(occupied), to_grid(anchors), to_grid(near_ids), pairs)


def draw_occupied(key, part):
    return geometry(key)[0]


def draw_anchors(key, part):
    return geometry(key)[1]


def draw_near_list(key, part):
    return geometry(key)[2]


def draw_contact_pairs(key, part):
    return geometry(key)[3]


def draw_centers(key, part):
    anchors = geometry(key)[1].astype(jnp.float32)
    jitter = jax.random.uniform(jax.random.fold_in(key, 57), anchors.shape, jnp.float32, -0.5, 0.5)
    return anchors + BLOCK // 2 + jitter


def block_scale(rng, extent, pieces, smallest, largest):
    def one(axis_at, shards_of):
        steps = jax.random.uniform(jax.random.fold_in(jax.random.fold_in(rng, 6), axis_at), (shards_of,), jnp.float32, smallest / len(pieces), largest / len(pieces))
        return jnp.repeat(jnp.exp(steps), extent[axis_at] // shards_of).reshape((-1,) + (1,) * (len(extent) - axis_at - 1))

    gain = one(*pieces[0])
    for cut in pieces[1:]:
        gain = gain * one(*cut)
    return gain


def normal_values(rng, extent, scale, reach, cuts=(), kind=jnp.bfloat16):
    entries = scale * jax.random.normal(rng, extent, jnp.float32)
    if cuts:
        entries = entries * block_scale(rng, extent, cuts, -0.22, 0.18)
    return jnp.clip(entries, -reach, reach).astype(kind)


def setup_inputs(seed: int = 0) -> dict:
    keys = jax.random.split(jax.random.key(seed), 10)
    return {
        "tractions": normal_values(keys[0], (ROWS, COLS, 3, NODES), 1.0, 6.0, ((0, 32), (1, 8)), jnp.float32),
        "centers": draw_centers(jax.random.fold_in(keys[9], 71), 0),
        "node_offsets": jnp.clip(jax.random.uniform(keys[2], (3, NODES), jnp.float32, -3.0, 3.0), -3.0, 3.0),
        "occupied": draw_occupied(jax.random.fold_in(keys[9], 71), 0),
        "anchors": draw_anchors(jax.random.fold_in(keys[9], 71), 0),
        "near_list": draw_near_list(jax.random.fold_in(keys[9], 71), 0),
        "contact_pairs": draw_contact_pairs(jax.random.fold_in(keys[9], 71), 0),
        "contact_gap": jnp.clip(jax.random.uniform(keys[7], (CONTACTS,), jnp.float32, -1.0, 1.0) * block_scale(keys[7], (CONTACTS,), ((0, 256),), -0.4, 0.0), -1.0, 1.0),
        "contact_angles": jnp.clip(jax.random.uniform(keys[8], (2, CONTACTS), jnp.float32, -3.140625, 3.140625), -3.140625, 3.140625),
    }


soften = 1.0
screen = 0.0625
near_scale = 0.05
spread_norm = 0.17958712212516656
mobility = 0.2
time_step = 0.5
relaxation = 0.35
ewald_split = 0.5

def block_weights(coordinate, anchor_cell):
    cell_centres = anchor_cell.astype(jnp.float32) + jnp.arange(BLOCK).astype(jnp.float32)
    distance = coordinate[:, None] - cell_centres[None, :]
    return jnp.exp(-distance * distance)

def spread_block(forces, position, anchor):
    weight_x = block_weights(position[0], anchor[0])
    weight_y = block_weights(position[1], anchor[1])
    weight_z = block_weights(position[2], anchor[2])
    planar = weight_x[:, :, None] * weight_y[:, None, :]
    loaded = forces[:, :, None, None] * planar[None]
    return spread_norm * jnp.einsum('cnab,ne->cabe', loaded, weight_z, precision=lax.Precision.HIGHEST)

def interp_block(mesh_block, position, anchor):
    weight_x = block_weights(position[0], anchor[0])
    weight_y = block_weights(position[1], anchor[1])
    weight_z = block_weights(position[2], anchor[2])
    along_z = jnp.einsum('cabe,ne->cabn', mesh_block, weight_z, precision=lax.Precision.HIGHEST)
    along_y = jnp.einsum('cabn,nb->can', along_z, weight_y, precision=lax.Precision.HIGHEST)
    return spread_norm * jnp.einsum('can,na->cn', along_y, weight_x, precision=lax.Precision.HIGHEST)

def stokes_tile(displacement, offsets, forces):
    separation = [displacement[component] + offsets[component][:, None] - offsets[component][None, :] for component in range(3)]
    radius_sq = separation[0] * separation[0] + separation[1] * separation[1] + separation[2] * separation[2]
    softened = radius_sq + soften
    weight = jnp.exp(-radius_sq * screen) / (softened * jnp.sqrt(softened))
    projected = separation[0] * forces[0][None, :] + separation[1] * forces[1][None, :] + separation[2] * forces[2][None, :]
    diagonal = (radius_sq + 2.0 * soften) * weight
    velocity = [lax.optimization_barrier(jnp.sum(diagonal * forces[component][None, :] + separation[component] * projected * weight, axis=1)) for component in range(3)]
    return near_scale * jnp.stack(velocity)

def nearest_image(difference):
    return difference - GRID * jnp.floor(difference / GRID + 0.5)

def far_kernel(wave_x, wave_y, wave_z, real_part, imag_part):
    wave_sq = wave_x * wave_x + wave_y * wave_y + wave_z * wave_z
    safe_sq = jnp.maximum(wave_sq, 1.0)
    damping = (ewald_split * jnp.pi / GRID) ** 2
    factor = jnp.where(wave_sq > 0.5, jnp.exp(-damping * wave_sq) / safe_sq, 0.0) * (GRID * GRID / (4.0 * jnp.pi * jnp.pi))
    waves = (wave_x, wave_y, wave_z)
    results = []
    for values in (real_part, imag_part):
        inner = waves[0] * values[0] + waves[1] * values[1] + waves[2] * values[2]
        results.append(jnp.stack([factor * (values[component] - waves[component] * inner / safe_sq) for component in range(3)]))
    return (results[0], results[1])

def flatten_slots(array):
    trailing = array.shape[2:]
    shaped = array.reshape((N_WIDE, S_SIDE, N_NARROW, S_SIDE) + trailing)
    return jnp.swapaxes(shaped, 1, 2).reshape((SLOTS,) + trailing)

def unflatten_slots(array):
    trailing = array.shape[1:]
    shaped = array.reshape((N_WIDE, N_NARROW, S_SIDE, S_SIDE) + trailing)
    return jnp.swapaxes(shaped, 1, 2).reshape((ROWS, COLS) + trailing)

def fold_wrap(mesh, dimension):
    head = lax.slice_in_dim(mesh, 0, GRID, axis=dimension)
    tail = lax.slice_in_dim(mesh, GRID, GRID + BLOCK, axis=dimension)
    return lax.dynamic_update_slice_in_dim(head, lax.slice_in_dim(head, 0, BLOCK, axis=dimension) + tail, 0, dimension)

def reference(tractions, centers, node_offsets, occupied, anchors, near_list, contact_pairs, contact_gap, contact_angles):
    forces = flatten_slots(tractions)
    centres = flatten_slots(centers)
    live = flatten_slots(occupied).astype(jnp.float32)
    starts = flatten_slots(anchors).astype(jnp.int32)
    neighbours = flatten_slots(near_list).astype(jnp.int32)
    zero_index = jnp.zeros((), jnp.int32)
    padded = jnp.zeros((3, GRID + BLOCK, GRID + BLOCK, GRID + BLOCK), jnp.float32)

    def deposit(slot_index, buffer):
        corner = starts[slot_index]
        location = (zero_index, corner[0], corner[1], corner[2])
        sphere_block = spread_block(forces[slot_index] * live[slot_index], centres[slot_index][:, None] + node_offsets, corner)
        current = lax.dynamic_slice(buffer, location, (3, BLOCK, BLOCK, BLOCK))
        return lax.dynamic_update_slice(buffer, current + sphere_block, location)
    mesh = lax.fori_loop(0, SLOTS, deposit, padded)
    for dimension in (1, 2, 3):
        mesh = fold_wrap(mesh, dimension)
    spectrum = jnp.fft.fftn(mesh, axes=(1, 2, 3))
    waves = (jnp.fft.fftfreq(GRID) * GRID).astype(jnp.float32)
    out_real, out_imag = far_kernel(waves[:, None, None], waves[None, :, None], waves[None, None, :], jnp.real(spectrum), jnp.imag(spectrum))
    velocity_mesh = jnp.real(jnp.fft.ifftn(lax.complex(out_real, out_imag), axes=(1, 2, 3))).astype(jnp.float32)
    wrapped = jnp.concatenate([velocity_mesh, velocity_mesh[:, :BLOCK]], axis=1)
    wrapped = jnp.concatenate([wrapped, wrapped[:, :, :BLOCK]], axis=2)
    wrapped = jnp.concatenate([wrapped, wrapped[:, :, :, :BLOCK]], axis=3)

    def sample(slot_index):
        corner = starts[slot_index]
        mesh_block = lax.dynamic_slice(wrapped, (zero_index, corner[0], corner[1], corner[2]), (3, BLOCK, BLOCK, BLOCK))
        return interp_block(mesh_block, centres[slot_index][:, None] + node_offsets, corner)
    far = lax.map(sample, jnp.arange(SLOTS, dtype=jnp.int32))

    def near_one(slot_index):
        centre = centres[slot_index]
        summed = stokes_tile(jnp.zeros((3,), jnp.float32), node_offsets, forces[slot_index])
        for neighbour_rank in range(NEAR):
            neighbour = neighbours[slot_index, neighbour_rank]
            summed = summed + stokes_tile(nearest_image(centre - centres[neighbour]), node_offsets, forces[neighbour])
        return summed

    def near_group(group_index):
        return jax.vmap(near_one)(group_index * 8 + jnp.arange(8, dtype=jnp.int32))
    near = lax.map(near_group, jnp.arange(SLOTS // 8, dtype=jnp.int32)).reshape(SLOTS, 3, NODES)
    node_velocity = (near + far) * live[:, None, None]
    hydro = lax.optimization_barrier(jnp.mean(node_velocity, axis=2))
    first_ids = contact_pairs[0]
    second_ids = contact_pairs[1]
    polar = contact_angles[0]
    azimuth = contact_angles[1]
    normal = jnp.stack([jnp.sin(polar) * jnp.cos(azimuth), jnp.sin(polar) * jnp.sin(azimuth), jnp.cos(polar)], axis=1)

    def totals(magnitude):
        loading = magnitude[:, None] * normal
        return jax.ops.segment_sum(loading, first_ids, num_segments=SLOTS) - jax.ops.segment_sum(loading, second_ids, num_segments=SLOTS)
    magnitude = jnp.zeros_like(contact_gap)
    for sweep_index in range(SWEEPS):
        velocity = hydro + mobility * totals(magnitude)
        relative = lax.optimization_barrier(jnp.sum(normal * (velocity[first_ids] - velocity[second_ids]), axis=1))
        magnitude = jnp.maximum(magnitude - relaxation * (contact_gap + time_step * relative) / (2.0 * time_step * mobility), 0.0)
    moved = centres + time_step * (hydro + mobility * totals(magnitude))
    return (unflatten_slots(node_velocity), magnitude, unflatten_slots(moved))
```

```python
import functools

import jax
import jax.numpy as jnp
import ml_dtypes
import numpy as np
from jax import lax
from jax.experimental import pallas as pl
from jax.experimental.pallas import tpu as pltpu
from jax.sharding import PartitionSpec as P

NODES = 256
GRID = 256
BLOCK = 16
NEAR = 2
SWEEPS = 6
SLOTS_DEV = 4

soften = 1.0
screen = 0.0625
near_scale = 0.05
spread_norm = 0.17958712212516656
mobility = 0.2
time_step = 0.5
relaxation = 0.35
ewald_split = 0.5

MESH = pl.DeviceIdType.MESH
F32 = jnp.float32
BF16 = jnp.bfloat16
VMEM_SPEC = pl.BlockSpec(memory_space=pltpu.VMEM)
SMEM_SPEC = pl.BlockSpec(memory_space=pltpu.SMEM)


def params(collective_id=None, limit=40):
    if collective_id is None:
        return pltpu.CompilerParams(vmem_limit_bytes=limit * 2**20)
    return pltpu.CompilerParams(
        vmem_limit_bytes=limit * 2**20, collective_id=collective_id, has_side_effects=True
    )


def trig_table(group):
    cell = np.arange(GRID)
    rows = []
    for first in range(0, GRID // 2, group):
        for half in (0, 1):
            for k in range(first, first + group):
                angle = 2.0 * np.pi / GRID * (k * cell % GRID)
                if half == 0:
                    rows.append(np.cos(angle))
                elif k == 0:
                    rows.append(np.cos(np.pi * cell))
                else:
                    rows.append(np.sin(angle))
    return np.stack(rows)


def halves(table):
    high = table.astype(np.float32).astype(ml_dtypes.bfloat16)
    low = (table - high.astype(np.float64)).astype(np.float32).astype(ml_dtypes.bfloat16)
    return high, low


def split(values):
    high = values.astype(BF16)
    return high, (values - high.astype(F32)).astype(BF16)


def dot(a, b, contract=((1,), (0,))):
    return lax.dot_general(a, b, (contract, ((), ())), preferred_element_type=F32)


def dot3(a, b):
    return dot(a[0], b[0]) + (dot(a[0], b[1]) + dot(a[1], b[0]))


def lanes_of(shape):
    return lax.broadcasted_iota(jnp.int32, shape, len(shape) - 1)


def roll(values, shift):
    return pltpu.roll(values, shift, len(values.shape) - 1)


def pack_lanes(u0, u1, u2, u3):
    lane = lanes_of(u0.shape)
    r1, r2, r3 = roll(u1, 96), roll(u2, 64), roll(u3, 32)
    return (
        jnp.where(lane < 96, u0, r1),
        jnp.where(lane < 64, r1, r2),
        jnp.where(lane < 32, r2, r3),
    )


def unpack_lanes(p0, p1, p2):
    lane = lanes_of(p0.shape)
    return (
        p0,
        roll(jnp.where(lane < 64, p1, p0), 32),
        roll(jnp.where(lane < 32, p2, p1), 64),
        roll(p2, 96),
    )


def greet(wide_count, narrow_count, offsets):
    w, n = lax.axis_index("wide"), lax.axis_index("narrow")
    barrier = pltpu.get_barrier_semaphore()
    for dw, dn in offsets:
        pl.semaphore_signal(
            barrier,
            inc=1,
            device_id=(
                lax.rem(w + dw + wide_count, wide_count),
                lax.rem(n + dn + narrow_count, narrow_count),
            ),
            device_id_type=MESH,
        )
    pl.semaphore_wait(barrier, len(offsets))


GATHER = [(dw, dn) for dw in (-2, -1, 0, 1) for dn in (-1, 0, 1)]


def gather_kernel(wide_count, narrow_count, own_ref, out_ref, held, send_sem, recv_sem):
    w, n = lax.axis_index("wide"), lax.axis_index("narrow")
    reach = [(dw, dn) for dw in (-2, -1, 0, 1, 2) for dn in (-1, 0, 1) if (dw, dn) != (0, 0)]
    greet(wide_count, narrow_count, reach)
    copies = []
    for place, (dw, dn) in enumerate(GATHER):
        if (dw, dn) == (0, 0):
            continue
        copy = pltpu.make_async_remote_copy(
            src_ref=own_ref,
            dst_ref=held.at[place],
            send_sem=send_sem.at[place],
            recv_sem=recv_sem.at[place],
            device_id=(
                lax.rem(w - dw + wide_count, wide_count),
                lax.rem(n - dn + narrow_count, narrow_count),
            ),
            device_id_type=MESH,
        )
        copy.start()
        copies.append((place, copy))
    out_ref[GATHER.index((0, 0))] = own_ref[...]
    for place, copy in copies:
        copy.wait_recv()
        out_ref[place] = held[place]
    for place, copy in copies:
        copy.wait_send()


def near_kernel(wide_count, narrow_count, list_ref, meta_ref, held_ref, off_ref, out_ref, offcol, source, columns):
    w, n = lax.axis_index("wide"), lax.axis_index("narrow")
    own = GATHER.index((0, 0))
    out_ref[...] = jnp.zeros_like(out_ref)
    columns[...] = jnp.zeros_like(columns)
    padded = jnp.concatenate([off_ref[...], jnp.zeros((5, NODES), F32)], axis=0)
    turned = jnp.transpose(padded)
    for c in range(3):
        offcol[c] = jnp.broadcast_to(turned[:, c : c + 1], (NODES, 128))

    for s in range(SLOTS_DEV):

        @pl.when(meta_ref[own, 24 + s] > 0.5)
        def _():
            for j in range(1 + NEAR):
                if j == 0:
                    place, within = own, s
                else:
                    entry = list_ref[s, j - 1]
                    holder = entry // SLOTS_DEV
                    within = entry % SLOTS_DEV
                    row = lax.rem(holder // narrow_count - w + 1 + wide_count, wide_count)
                    column = lax.rem(lax.rem(holder, narrow_count) - n + 1 + narrow_count, narrow_count)
                    place = (row + 1) * 3 + column
                for c in range(3):
                    if j == 0:
                        shift = 0.0
                    else:
                        e = meta_ref[own, 3 * s + c] - meta_ref[place, 3 * within + c]
                        shift = e - jnp.where(e >= 128.0, 256.0, jnp.where(e < -128.0, -256.0, 0.0))
                    source[j, c : c + 1, :] = shift - off_ref[c : c + 1, :]
                    source[j, 3 + c : 4 + c, :] = held_ref[place, pl.ds(within * 3 + c, 1), :]

            def chunk(i, carry):
                rows = pl.ds(pl.multiple_of(i * 8, 8), 8)
                sums = [jnp.zeros((8, 128), F32) for _ in range(3)]
                at = [offcol[c, rows, :] for c in range(3)]
                for j in range(1 + NEAR):
                    for half in (0, 1):
                        lanes = slice(half * 128, half * 128 + 128)
                        d = [at[c] + source[j, c : c + 1, lanes] for c in range(3)]
                        f = [source[j, 3 + c : 4 + c, lanes] for c in range(3)]
                        r2 = d[0] * d[0] + d[1] * d[1] + d[2] * d[2]
                        inverse = lax.rsqrt(r2 + soften)
                        weight = jnp.exp(r2 * (-screen)) * (inverse * inverse * inverse)
                        along = (d[0] * f[0] + d[1] * f[1] + d[2] * f[2]) * weight
                        diagonal = (r2 + 2.0 * soften) * weight
                        for c in range(3):
                            sums[c] = sums[c] + (diagonal * f[c] + d[c] * along)
                for c in range(3):
                    columns[rows, c : c + 1] = jnp.sum(sums[c], axis=1, keepdims=True)
                return carry

            lax.fori_loop(0, NODES // 8, chunk, 0)
            result = jnp.transpose(columns[...])
            out_ref[3 * s : 3 * s + 3, :] = near_scale * result[0:3, :]


def sphere_weights(wide_count, narrow_count, index, meta_ref, off_ref):
    w, n = lax.axis_index("wide"), lax.axis_index("narrow")
    size_x, size_y = GRID // wide_count, GRID // narrow_count
    dw = index // 8 - 2
    dn = (index // 4) % 2 - 1
    s = index % 4
    place = (dw + 2) * 3 + dn + 1
    anchor = [meta_ref[place, 12 + 3 * s + c].astype(jnp.int32) for c in range(3)]
    centre = [meta_ref[place, 3 * s + c] for c in range(3)]
    low_x = anchor[0] - size_x * lax.rem(w + dw + wide_count, wide_count) + size_x * dw
    low_y = anchor[1] - size_y * lax.rem(n + dn + narrow_count, narrow_count) + size_y * dn
    active = (meta_ref[place, 24 + s] > 0.5) & (low_x + BLOCK > 0) & (low_y + BLOCK > 0)

    def weights(c, low, count):
        cell = lax.broadcasted_iota(jnp.int32, (count, NODES), 0)
        position = centre[c] + off_ref[c : c + 1, :]
        distance = position - ((anchor[c] - low) + cell).astype(F32)
        inside = (cell >= low) & (cell < low + BLOCK)
        return jnp.where(inside, jnp.exp(-distance * distance), 0.0)

    return (
        place,
        s,
        active,
        anchor[2],
        lambda: (weights(0, low_x, size_x), weights(1, low_y, size_y), weights(2, anchor[2] % 8, 32)),
    )


def stacked(values, second):
    high, low = split(values)
    return jnp.concatenate([high, low, high] if second else [high, high, low], axis=0)


def spread_kernel(wide_count, narrow_count, meta_ref, held_ref, off_ref, tz_ref, out_ref, a_high, a_low, total, turned):
    total[...] = jnp.zeros_like(total)

    def sphere(index, carry):
        place, s, active, low_z, weights = sphere_weights(wide_count, narrow_count, index, meta_ref, off_ref)

        @pl.when(active)
        def _():
            wx, wy, wz = weights()
            table = tz_ref[pl.ds(pl.multiple_of(low_z // 8 * 8, 8), 32), :]
            along_z = split(
                dot(jnp.transpose(stacked(wz, False).astype(F32)).astype(BF16), stacked(table, True))
            )
            planar = jnp.concatenate(
                [
                    wy * (spread_norm * held_ref[place, pl.ds(s * 3 + c, 1), :])
                    for c in range(3)
                ],
                axis=0,
            )
            for x in range(8):
                high, low = split(planar * wx[x : x + 1, :])
                a_high[x * 96 : x * 96 + 96, :] = high
                a_low[x * 96 : x * 96 + 96, :] = low
            total[...] += dot3((a_high[...], a_low[...]), along_z)

        return carry

    lax.fori_loop(0, 24, sphere, 0)
    for x in range(8):
        block = jnp.concatenate([total[x * 96 : x * 96 + 96, :], jnp.zeros((32, GRID), F32)], axis=0)
        turned[pl.ds(x, GRID, stride=8), :] = jnp.transpose(block)
    values = turned[...].reshape(64, 4, 8, 128)
    packed = pack_lanes(*[values[:, j] for j in range(4)])
    for g in range(3):
        out_ref[:, :, :, g * 128 : g * 128 + 128] = packed[g].reshape(32, 2, 8, 128)


def interp_kernel(wide_count, narrow_count, meta_ref, off_ref, tz_ref, mesh_ref, out_ref, m_high, m_low, turned):
    out_ref[...] = jnp.zeros_like(out_ref)
    groups = [mesh_ref[:, :, :, g * 128 : g * 128 + 128].reshape(64, 8, 128) for g in range(3)]
    unpacked = unpack_lanes(*groups)
    turned[...] = jnp.stack(unpacked, axis=1).reshape(GRID * 8, 128)
    for x in range(8):
        block = jnp.transpose(turned[pl.ds(x, GRID, stride=8), :])
        high, low = split(block[:96])
        m_high[x * 96 : x * 96 + 96, :] = high
        m_low[x * 96 : x * 96 + 96, :] = low

    def sphere(index, carry):
        place, s, active, low_z, weights = sphere_weights(wide_count, narrow_count, index, meta_ref, off_ref)

        @pl.when(active)
        def _():
            wx, wy, wz = weights()
            table = tz_ref[pl.ds(pl.multiple_of(low_z // 8 * 8, 8), 32), :]
            along_z = split(
                dot(jnp.transpose(stacked(table, True).astype(F32)).astype(BF16), stacked(wz, False))
            )
            found = dot3((m_high[...], m_low[...]), along_z)
            summed = found[0:96] * wx[0:1, :]
            for x in range(1, 8):
                summed = summed + found[x * 96 : x * 96 + 96] * wx[x : x + 1, :]
            rows = [
                jnp.sum(summed[c * 32 : c * 32 + 32] * wy, axis=0, keepdims=True) * spread_norm
                for c in range(3)
            ]
            owner = index // 4
            for c in range(3):
                out_ref[owner, pl.ds(s * 3 + c, 1), :] = rows[c]

        return carry

    lax.fori_loop(0, 24, sphere, 0)


def exchange(axis, count, source, target, send_sem, recv_sem, me, other):
    def copy_to(step):
        to = lax.rem(me + step, count)
        device = (to, other) if axis == "wide" else (other, to)
        return pltpu.make_async_remote_copy(
            src_ref=source.at[to],
            dst_ref=target.at[me],
            send_sem=send_sem.at[step],
            recv_sem=recv_sem.at[step],
            device_id=device,
            device_id_type=MESH,
        )

    def begin(step, carry):
        copy_to(step).start()
        return carry

    def end(step, carry):
        copy_to(step).wait()
        return carry

    lax.fori_loop(1, count, begin, 0)
    target[me] = source[me]
    lax.fori_loop(1, count, end, 0)


def transform_kernel(
    wide_count,
    narrow_count,
    mesh_ref,
    tx_high,
    tx_low,
    ix_high,
    ix_low,
    ty_high,
    ty_low,
    iy_high,
    iy_low,
    out_ref,
    wide_in,
    narrow_out,
    narrow_in,
    narrow_back,
    narrow_home,
    wide_back,
    wide_home,
    lines,
    spectrum,
    wide_send,
    wide_recv,
    narrow_send,
    narrow_recv,
):
    w, n = lax.axis_index("wide"), lax.axis_index("narrow")
    greet(
        wide_count,
        narrow_count,
        [(step, 0) for step in range(1, wide_count)] + [(0, step) for step in range(1, narrow_count)],
    )
    exchange("wide", wide_count, mesh_ref, wide_in, wide_send.at[0], wide_recv.at[0], w, n)
    for half in (0, 1):
        block = split(wide_in[:, half].reshape(GRID, 384))
        along = dot3((tx_high[...], tx_low[...]), block)
        narrow_out[:, half] = along.reshape(narrow_count, 32, 384)
    exchange("narrow", narrow_count, narrow_out, narrow_in, narrow_send.at[0], narrow_recv.at[0], n, w)
    for half in (0, 1):
        for source in range(8):
            groups = [narrow_in[source, half, :, g * 128 : g * 128 + 128] for g in range(3)]
            unpacked = unpack_lanes(*groups)
            for j in range(4):
                lines[half * 128 + j * 32 : half * 128 + j * 32 + 32, source * 128 : source * 128 + 128] = unpacked[j]
    for half in (0, 1):
        rows = slice(half * 128, half * 128 + 128)
        spectrum[rows, :] = dot3(split(lines[rows, :]), (ty_high[...], ty_low[...]))

    row = lax.broadcasted_iota(jnp.int32, (32, 1), 0)
    k_x = (n * 16 + row % 16).astype(F32)
    nyquist_x = jnp.where((row >= 16) & (k_x < 0.5), 128.0, 0.0)
    lane = lax.broadcasted_iota(jnp.int32, (1, GRID), 1)
    k_y = (lane % 128).astype(F32)
    nyquist_y = jnp.where((lane >= 128) & (k_y < 0.5), 128.0, 0.0)
    square_xy = k_x * k_x + nyquist_x * nyquist_x + (k_y * k_y + nyquist_y * nyquist_y)
    scale_x = jnp.where(k_x < 0.5, 1.0, 2.0)
    scale_y = jnp.where(k_y < 0.5, 1.0, 2.0)
    scale_xy = scale_x * scale_y
    damping = (ewald_split * np.pi / GRID) ** 2
    constant = GRID * GRID / (4.0 * np.pi * np.pi) / float(GRID) ** 3
    turn_x = jnp.where(row < 16, k_x, -k_x)
    turn_y = jnp.where(lane < 128, k_y, -k_y)

    def derive_x(values):
        return turn_x * jnp.concatenate([values[16:], values[:16]], axis=0)

    def derive_y(values):
        return turn_y * jnp.concatenate([values[:, 128:], values[:, :128]], axis=1)

    def filtered(j, carry):
        k_z = (w * 4 + j).astype(F32)
        bases = [pl.multiple_of(half * 128 + j * 32, 32) for half in (0, 1)]
        fields = [
            [spectrum[pl.ds(bases[half], 32), c * 256 : c * 256 + 256] for c in range(3)]
            for half in (0, 1)
        ]
        flows = []
        nyquists_z = [jnp.zeros_like(k_z), jnp.where(k_z < 0.5, 128.0, 0.0)]
        scale_z = jnp.where(k_z < 0.5, 1.0, 2.0)
        turn_z = (k_z, -k_z)
        for half in (0, 1):
            values = fields[half]
            flows.append(derive_x(values[0]) + derive_y(values[1]) + turn_z[half] * fields[1 - half][2])
        for half in (0, 1):
            values = fields[half]
            nyquist_z = nyquists_z[half]
            square = square_xy + (k_z * k_z + nyquist_z * nyquist_z)
            safe = jnp.maximum(square, 1.0)
            inverse = 1.0 / safe
            factor = jnp.where(square > 0.5, jnp.exp(-damping * square) * inverse, 0.0)
            factor = factor * (scale_xy * (scale_z * constant))
            edge = (nyquist_x * values[0] + nyquist_y * values[1] + nyquist_z * values[2]) * inverse
            flow = [flows[half] * inverse, flows[1 - half] * inverse]
            gradient = [derive_x(flow[0]), derive_y(flow[0]), None]
            other_square = square_xy + (k_z * k_z + nyquists_z[1 - half] * nyquists_z[1 - half])
            gradient[2] = turn_z[half] * (flows[1 - half] * inverse)
            nyquist = (nyquist_x, nyquist_y, nyquist_z)
            for c in range(3):
                spectrum[pl.ds(bases[half], 32), c * 256 : c * 256 + 256] = factor * (
                    values[c] + gradient[c] - nyquist[c] * edge
                )
        return carry

    lax.fori_loop(0, 4, filtered, 0)
    for half in (0, 1):
        rows = slice(half * 128, half * 128 + 128)
        lines[rows, :] = dot3(split(spectrum[rows, :]), (iy_high[...], iy_low[...]))
    for half in (0, 1):
        for target in range(8):
            groups = [
                lines[half * 128 + j * 32 : half * 128 + j * 32 + 32, target * 128 : target * 128 + 128]
                for j in range(4)
            ]
            packed = pack_lanes(*groups)
            for g in range(3):
                narrow_back[target, half, :, g * 128 : g * 128 + 128] = packed[g]
    exchange("narrow", narrow_count, narrow_back, narrow_home, narrow_send.at[1], narrow_recv.at[1], n, w)
    for half in (0, 1):
        block = split(narrow_home[:, half].reshape(GRID, 384))
        along = dot3((ix_high[...], ix_low[...]), block)
        wide_back[:, half] = along.reshape(wide_count, 8, 384)
    exchange("wide", wide_count, wide_back, wide_home, wide_send.at[1], wide_recv.at[1], w, n)
    out_ref[...] = wide_home[...]


AROUND = [(dw, dn) for dw in (-1, 0, 1) for dn in (-1, 0, 1)]
PARTIAL = [(dw, dn) for dw in (-2, -1, 0) for dn in (-1, 0)]


def contact_kernel(
    wide_count,
    narrow_count,
    part_ref,
    near_ref,
    centre_ref,
    edge_ref,
    gap_ref,
    velocity_ref,
    force_ref,
    moved_ref,
    part_in,
    load_out,
    load_in,
    flow_out,
    flow_in,
    part_send,
    part_recv,
    load_send,
    load_recv,
    flow_send,
    flow_recv,
):
    w, n = lax.axis_index("wide"), lax.axis_index("narrow")

    def device(dw, dn):
        return (
            lax.rem(w + dw + wide_count, wide_count),
            lax.rem(n + dn + narrow_count, narrow_count),
        )

    greet(
        wide_count,
        narrow_count,
        [d for d in AROUND if d != (0, 0)] + [(-2, -1), (-2, 0), (2, 1), (2, 0)],
    )
    copies = []
    for place, (dw, dn) in enumerate(PARTIAL):
        if (dw, dn) == (0, 0):
            continue
        copy = pltpu.make_async_remote_copy(
            src_ref=part_ref.at[place],
            dst_ref=part_in.at[place],
            send_sem=part_send.at[place],
            recv_sem=part_recv.at[place],
            device_id=device(dw, dn),
            device_id_type=MESH,
        )
        copy.start()
        copies.append((place, copy))
    velocity = near_ref[...] + part_ref[PARTIAL.index((0, 0))]
    for place, copy in copies:
        copy.wait_recv()
        velocity = velocity + part_in[place]
    velocity_ref[...] = velocity
    hydro = jnp.broadcast_to(
        jnp.sum(velocity, axis=1, keepdims=True) * (1.0 / NODES), (16, 128)
    )

    def flow_copy(turn, place):
        dw, dn = AROUND[place]
        return pltpu.make_async_remote_copy(
            src_ref=flow_out.at[turn],
            dst_ref=flow_in.at[turn, 8 - place],
            send_sem=flow_send.at[turn, place],
            recv_sem=flow_recv.at[turn, 8 - place],
            device_id=device(dw, dn),
            device_id_type=MESH,
        )

    def load_copy(turn, place):
        dw, dn = AROUND[place]
        return pltpu.make_async_remote_copy(
            src_ref=load_out.at[turn, place],
            dst_ref=load_in.at[turn, 8 - place],
            send_sem=load_send.at[turn, place],
            recv_sem=load_recv.at[turn, 8 - place],
            device_id=device(dw, dn),
            device_id_type=MESH,
        )

    others = [place for place in range(9) if place != 4]

    def sweep(turn, carry):
        force, moving = carry
        flow_out[turn] = moving
        for place in others:
            flow_copy(turn, place).start()
        flow_in[turn, 4] = moving
        for place in others:
            flow_copy(turn, place).wait_recv()
        around = flow_in[turn].reshape(144, 128)
        relative = jnp.sum(edge_ref[...] * around, axis=0, keepdims=True)
        force = jnp.maximum(
            force
            - relaxation * (gap_ref[0:1, :] + time_step * relative) / (2.0 * time_step * mobility),
            0.0,
        )
        load = jnp.sum(edge_ref[...] * force, axis=1, keepdims=True)
        load_out[turn] = jnp.broadcast_to(load, (144, 128)).reshape(9, 16, 128)
        for place in others:
            load_copy(turn, place).start()
        summed = load_out[turn, 4]
        for place in others:
            load_copy(turn, place).wait_recv()
            summed = summed + load_in[turn, 8 - place]
        for place in others:
            load_copy(turn, place).wait_send()
            flow_copy(turn, place).wait_send()
        return force, hydro + mobility * summed

    force, moving = lax.fori_loop(0, SWEEPS, sweep, (jnp.zeros((1, 128), F32), hydro))
    force_ref[...] = jnp.broadcast_to(force, (8, 128))
    moved_ref[...] = centre_ref[...] + time_step * moving
    for place, copy in copies:
        copy.wait_send()


def local(
    wide_count,
    narrow_count,
    tractions,
    centers,
    node_offsets,
    occupied,
    anchors,
    near_list,
    contact_pairs,
    contact_gap,
    contact_angles,
):
    w, n = lax.axis_index("wide"), lax.axis_index("narrow")
    sizes = (wide_count, narrow_count)
    shape = jax.ShapeDtypeStruct
    dma = pltpu.SemaphoreType.DMA

    meta = jnp.concatenate(
        [
            centers.reshape(12),
            anchors.reshape(12).astype(F32),
            occupied.reshape(4).astype(F32),
            jnp.zeros((228,), F32),
        ]
    )
    own = jnp.concatenate([tractions.reshape(12, NODES), meta[None], jnp.zeros((3, NODES), F32)])
    held = pl.pallas_call(
        functools.partial(gather_kernel, *sizes),
        out_shape=shape((12, 16, NODES), F32),
        in_specs=[VMEM_SPEC],
        out_specs=VMEM_SPEC,
        scratch_shapes=[pltpu.VMEM((12, 16, NODES), F32), dma((12,)), dma((12,))],
        compiler_params=params(0),
        name="gather",
    )(own)
    metas = held[:, 12, :128]

    table_z = trig_table(4)
    wrapped_z = np.concatenate([table_z, table_z[:, :32]], axis=1).T.astype(np.float32)
    mesh = pl.pallas_call(
        functools.partial(spread_kernel, *sizes),
        out_shape=shape((32, 2, 8, 384), F32),
        in_specs=[SMEM_SPEC, VMEM_SPEC, VMEM_SPEC, VMEM_SPEC],
        out_specs=VMEM_SPEC,
        scratch_shapes=[
            pltpu.VMEM((768, NODES), BF16),
            pltpu.VMEM((768, NODES), BF16),
            pltpu.VMEM((768, GRID), F32),
            pltpu.VMEM((GRID * 8, 128), F32),
        ],
        compiler_params=params(),
        name="spread",
    )(metas, held, node_offsets, wrapped_z)

    table_x = trig_table(16)
    table_y = trig_table(128)
    wide_y = np.zeros((8, 128, 3, GRID))
    for c in range(3):
        wide_y[:, c * 32 : c * 32 + 32, c, :] = table_y.T.reshape(8, 32, GRID)
    wide_y = wide_y.reshape(1024, 768)
    mesh = pl.pallas_call(
        functools.partial(transform_kernel, *sizes),
        out_shape=shape((32, 2, 8, 384), F32),
        in_specs=[VMEM_SPEC] * 9,
        out_specs=VMEM_SPEC,
        scratch_shapes=[
            pltpu.VMEM((32, 2, 8, 384), F32),
            pltpu.VMEM((8, 2, 32, 384), F32),
            pltpu.VMEM((8, 2, 32, 384), F32),
            pltpu.VMEM((8, 2, 32, 384), F32),
            pltpu.VMEM((8, 2, 32, 384), F32),
            pltpu.VMEM((32, 2, 8, 384), F32),
            pltpu.VMEM((32, 2, 8, 384), F32),
            pltpu.VMEM((256, 1024), F32),
            pltpu.VMEM((256, 768), F32),
            dma((2, 32)),
            dma((2, 32)),
            dma((2, 8)),
            dma((2, 8)),
        ],
        compiler_params=params(1),
        name="transform",
    )(
        mesh,
        *halves(table_x),
        *halves(np.ascontiguousarray(table_x.T)),
        *halves(wide_y),
        *halves(np.ascontiguousarray(wide_y.T)),
    )

    part = pl.pallas_call(
        functools.partial(interp_kernel, *sizes),
        out_shape=shape((6, 16, NODES), F32),
        in_specs=[SMEM_SPEC, VMEM_SPEC, VMEM_SPEC, VMEM_SPEC],
        out_specs=VMEM_SPEC,
        scratch_shapes=[
            pltpu.VMEM((768, GRID), BF16),
            pltpu.VMEM((768, GRID), BF16),
            pltpu.VMEM((GRID * 8, 128), F32),
        ],
        compiler_params=params(),
        name="interpolate",
    )(metas, node_offsets, wrapped_z, mesh)

    near = pl.pallas_call(
        functools.partial(near_kernel, *sizes),
        out_shape=shape((16, NODES), F32),
        in_specs=[SMEM_SPEC, SMEM_SPEC, VMEM_SPEC, VMEM_SPEC],
        out_specs=VMEM_SPEC,
        scratch_shapes=[
            pltpu.VMEM((3, NODES, 128), F32),
            pltpu.VMEM((3, 8, NODES), F32),
            pltpu.VMEM((NODES, 8), F32),
        ],
        compiler_params=params(),
        name="near",
    )(near_list.reshape(4, NEAR), metas, held, node_offsets)

    polar, azimuth = contact_angles[0], contact_angles[1]
    normal = jnp.stack(
        [jnp.sin(polar) * jnp.cos(azimuth), jnp.sin(polar) * jnp.sin(azimuth), jnp.cos(polar)]
    )
    holder, within = contact_pairs // 4, contact_pairs % 4
    row_w = (holder // narrow_count - w + 1 + wide_count) % wide_count
    row_n = (holder % narrow_count - n + 1 + narrow_count) % narrow_count
    first_row = (row_w * 3 + row_n) * 16 + within * 3
    index = jnp.arange(144, dtype=jnp.int32)
    component = index % 16 % 3
    base = (index - component)[:, None]
    used = (index % 16 < 12)[:, None]
    sign = jnp.where(base == first_row[0][None, :], 1.0, 0.0) - jnp.where(
        base == first_row[1][None, :], 1.0, 0.0
    )
    spread_normal = jnp.where(
        (component == 0)[:, None],
        normal[0][None],
        jnp.where((component == 1)[:, None], normal[1][None], normal[2][None]),
    )
    edge = jnp.pad(jnp.where(used, sign * spread_normal, 0.0), ((0, 0), (0, 96)))
    gap = jnp.pad(jnp.broadcast_to(contact_gap[None], (8, 32)), ((0, 0), (0, 96)))
    centre_rows = jnp.broadcast_to(jnp.pad(centers.reshape(12, 1), ((0, 4), (0, 0))), (16, 128))
    velocity, force, moved = pl.pallas_call(
        functools.partial(contact_kernel, *sizes),
        out_shape=(shape((16, NODES), F32), shape((8, 128), F32), shape((16, 128), F32)),
        in_specs=[VMEM_SPEC] * 5,
        out_specs=(VMEM_SPEC,) * 3,
        scratch_shapes=[
            pltpu.VMEM((6, 16, NODES), F32),
            pltpu.VMEM((SWEEPS, 9, 16, 128), F32),
            pltpu.VMEM((SWEEPS, 9, 16, 128), F32),
            pltpu.VMEM((SWEEPS, 16, 128), F32),
            pltpu.VMEM((SWEEPS, 9, 16, 128), F32),
            dma((6,)),
            dma((6,)),
            dma((SWEEPS, 9)),
            dma((SWEEPS, 9)),
            dma((SWEEPS, 9)),
            dma((SWEEPS, 9)),
        ],
        compiler_params=params(2),
        name="contacts",
    )(part, near, centre_rows, edge, gap)
    return (
        velocity[:12].reshape(2, 2, 3, NODES),
        force[0, :32],
        moved[:12, 0].reshape(2, 2, 3),
    )


def solution(mesh):
    placed = (
        P("wide", "narrow", None, None),
        P("wide", "narrow", None),
        P(),
        P("wide", "narrow"),
        P("wide", "narrow", None),
        P("wide", "narrow", None),
        P(None, ("wide", "narrow")),
        P(("wide", "narrow")),
        P(None, ("wide", "narrow")),
    )
    return jax.shard_map(
        functools.partial(local, mesh.shape["wide"], mesh.shape["narrow"]),
        mesh=mesh,
        in_specs=placed,
        out_specs=(
            P("wide", "narrow", None, None),
            P(("wide", "narrow")),
            P("wide", "narrow", None),
        ),
        check_vma=False,
    )
```

```python
import functools

import jax
import jax.numpy as jnp
import ml_dtypes
import numpy as np
from jax import lax
from jax.experimental import pallas as pl
from jax.experimental.pallas import tpu as pltpu
from jax.sharding import PartitionSpec as P

NODES = 256
GRID = 256
BLOCK = 16
NEAR = 2
SWEEPS = 6
SLOTS_DEV = 4
ROWS_DEV = 3 * SLOTS_DEV
CONT_DEV = 32

soften = 1.0
screen = 0.0625
near_scale = 0.05
spread_norm = 0.17958712212516656
mobility = 0.2
time_step = 0.5
relaxation = 0.35
ewald_split = 0.5

MESH = pl.DeviceIdType.MESH
F32 = jnp.float32
BF16 = jnp.bfloat16
VMEM_SPEC = pl.BlockSpec(memory_space=pltpu.VMEM)
HBM_SPEC = pl.BlockSpec(memory_space=pltpu.HBM)
SMEM_SPEC = pl.BlockSpec(memory_space=pltpu.SMEM)


def params(collective_id=None, limit=40):
    if collective_id is None:
        return pltpu.CompilerParams(vmem_limit_bytes=limit * 2**20)
    return pltpu.CompilerParams(
        vmem_limit_bytes=limit * 2**20, collective_id=collective_id, has_side_effects=True
    )


def trig_table(group):
    cell = np.arange(GRID)
    rows = []
    for first in range(0, GRID // 2, group):
        for half in (0, 1):
            for k in range(first, first + group):
                angle = 2.0 * np.pi / GRID * (k * cell % GRID)
                if half == 0:
                    rows.append(np.cos(angle))
                elif k == 0:
                    rows.append(np.cos(np.pi * cell))
                else:
                    rows.append(np.sin(angle))
    return np.stack(rows)


def halves(table):
    high = table.astype(np.float32).astype(ml_dtypes.bfloat16)
    low = (table - high.astype(np.float64)).astype(np.float32).astype(ml_dtypes.bfloat16)
    return high, low


def split(values):
    high = values.astype(BF16)
    return high, (values - high.astype(F32)).astype(BF16)


def dot(a, b, contract=((1,), (0,))):
    return lax.dot_general(a, b, (contract, ((), ())), preferred_element_type=F32)


def dot3(a, b):
    return dot(a[0], b[0]) + (dot(a[0], b[1]) + dot(a[1], b[0]))


def lanes_of(shape):
    return lax.broadcasted_iota(jnp.int32, shape, len(shape) - 1)


def roll(values, shift):
    return pltpu.roll(values, shift, len(values.shape) - 1)


def pack_lanes(u0, u1, u2, u3):
    lane = lanes_of(u0.shape)
    r1, r2, r3 = roll(u1, 96), roll(u2, 64), roll(u3, 32)
    return (
        jnp.where(lane < 96, u0, r1),
        jnp.where(lane < 64, r1, r2),
        jnp.where(lane < 32, r2, r3),
    )


def unpack_lanes(p0, p1, p2):
    lane = lanes_of(p0.shape)
    return (
        p0,
        roll(jnp.where(lane < 64, p1, p0), 32),
        roll(jnp.where(lane < 32, p2, p1), 64),
        roll(p2, 96),
    )


def greet(wide_count, narrow_count, offsets):
    w, n = lax.axis_index("wide"), lax.axis_index("narrow")
    barrier = pltpu.get_barrier_semaphore()
    for dw, dn in offsets:
        pl.semaphore_signal(
            barrier,
            inc=1,
            device_id=(
                lax.rem(w + dw + wide_count, wide_count),
                lax.rem(n + dn + narrow_count, narrow_count),
            ),
            device_id_type=MESH,
        )
    pl.semaphore_wait(barrier, len(offsets))


GATHER = [(dw, dn) for dw in (-2, -1, 0, 1) for dn in (-1, 0, 1)]


def gather_kernel(
    wide_count,
    narrow_count,
    tractions_ref,
    centres_ref,
    anchors_ref,
    occupied_ref,
    out_ref,
    meta_ref,
    own_ref,
    held,
    send_sem,
    recv_sem,
):
    w, n = lax.axis_index("wide"), lax.axis_index("narrow")
    reach = [(dw, dn) for dw in (-2, -1, 0, 1, 2) for dn in (-1, 0, 1) if (dw, dn) != (0, 0)]
    slots = [(a, b) for a in (0, 1) for b in (0, 1)]
    numbers = [centres_ref[a, b, c] for a, b in slots for c in range(3)]
    numbers += [anchors_ref[a, b, c].astype(F32) for a, b in slots for c in range(3)]
    numbers += [occupied_ref[a, b].astype(F32) for a, b in slots]
    lane = lanes_of((1, NODES))
    line = jnp.zeros((1, NODES), F32)
    for place, number in enumerate(numbers):
        line = jnp.where(lane == place, number, line)
    for s, (a, b) in enumerate(slots):
        own_ref[3 * s : 3 * s + 3, :] = tractions_ref[a, b]
    own_ref[12:16, :] = jnp.broadcast_to(line, (4, NODES))
    greet(wide_count, narrow_count, reach)
    copies = []
    for place, (dw, dn) in enumerate(GATHER):
        if (dw, dn) == (0, 0):
            continue
        copy = pltpu.make_async_remote_copy(
            src_ref=own_ref,
            dst_ref=held.at[place],
            send_sem=send_sem.at[place],
            recv_sem=recv_sem.at[place],
            device_id=(
                lax.rem(w - dw + wide_count, wide_count),
                lax.rem(n - dn + narrow_count, narrow_count),
            ),
            device_id_type=MESH,
        )
        copy.start()
        copies.append((place, copy))
    own = GATHER.index((0, 0))
    out_ref[own] = own_ref[...]
    meta_ref[own : own + 1, :] = own_ref[12:13, 0:128]
    for place, copy in copies:
        copy.wait_recv()
        out_ref[place] = held[place]
        meta_ref[place : place + 1, :] = held[place, 12:13, 0:128]
    for place, copy in copies:
        copy.wait_send()


def near_field(sizes, list_ref, meta_ref, held_ref, off_ref, out_ref, offcol, source, columns):
    wide_count, narrow_count = sizes
    w, n = lax.axis_index("wide"), lax.axis_index("narrow")
    own = GATHER.index((0, 0))
    out_ref[...] = jnp.zeros_like(out_ref)
    columns[...] = jnp.zeros_like(columns)
    padded = jnp.concatenate([off_ref[...], jnp.zeros((5, NODES), F32)], axis=0)
    turned = jnp.transpose(padded)
    for c in range(3):
        offcol[c] = jnp.broadcast_to(turned[:, c : c + 1], (NODES, 128))

    for s in range(SLOTS_DEV):
        for j in range(1 + NEAR):
            if j == 0:
                place, within = own, s
            else:
                entry = list_ref[s, j - 1]
                holder = entry // SLOTS_DEV
                within = entry % SLOTS_DEV
                row = lax.rem(holder // narrow_count - w + 1 + wide_count, wide_count)
                column = lax.rem(lax.rem(holder, narrow_count) - n + 1 + narrow_count, narrow_count)
                place = (jnp.minimum(row, 2) + 1) * 3 + jnp.minimum(column, 2)
            for c in range(3):
                if j == 0:
                    shift = 0.0
                else:
                    e = meta_ref[own, 3 * s + c] - meta_ref[place, 3 * within + c]
                    shift = e - jnp.where(e >= 128.0, 256.0, jnp.where(e < -128.0, -256.0, 0.0))
                source[j, c : c + 1, :] = shift - off_ref[c : c + 1, :]
                source[j, 3 + c : 4 + c, :] = held_ref[place, pl.ds(within * 3 + c, 1), :]

        def chunk(i, carry):
            for part in (0, 1):
                rows = pl.ds(pl.multiple_of(i * 16 + part * 8, 8), 8)
                sums = [jnp.zeros((8, 128), F32) for _ in range(3)]
                at = [offcol[c, rows, :] for c in range(3)]
                for j in range(1 + NEAR):
                    for half in (0, 1):
                        lanes = slice(half * 128, half * 128 + 128)
                        d = [at[c] + source[j, c : c + 1, lanes] for c in range(3)]
                        f = [source[j, 3 + c : 4 + c, lanes] for c in range(3)]
                        r2 = d[0] * d[0] + d[1] * d[1] + d[2] * d[2]
                        inverse = lax.rsqrt(r2 + soften)
                        weight = jnp.exp(r2 * (-screen)) * (inverse * inverse * inverse)
                        along = (d[0] * f[0] + d[1] * f[1] + d[2] * f[2]) * weight
                        diagonal = (r2 + 2.0 * soften) * weight
                        for c in range(3):
                            sums[c] = sums[c] + (diagonal * f[c] + d[c] * along)
                for c in range(3):
                    columns[rows, c : c + 1] = jnp.sum(sums[c], axis=1, keepdims=True)
            return carry

        lax.fori_loop(0, NODES // 16, chunk, 0)
        result = jnp.transpose(columns[...])
        alive = jnp.where(meta_ref[own, 24 + s] > 0.5, near_scale, 0.0)
        out_ref[3 * s : 3 * s + 3, :] = alive * result[0:3, :]


def sphere_weights(wide_count, narrow_count, index, meta_ref, off_ref):
    w, n = lax.axis_index("wide"), lax.axis_index("narrow")
    size_x, size_y = GRID // wide_count, GRID // narrow_count
    dw = index // 8 - 2
    dn = (index // 4) % 2 - 1
    s = index % 4
    place = (dw + 2) * 3 + dn + 1
    anchor = [meta_ref[place, 12 + 3 * s + c].astype(jnp.int32) for c in range(3)]
    centre = [meta_ref[place, 3 * s + c] for c in range(3)]
    low_x = anchor[0] - size_x * lax.rem(w + dw + wide_count, wide_count) + size_x * dw
    low_y = anchor[1] - size_y * lax.rem(n + dn + narrow_count, narrow_count) + size_y * dn
    active = (meta_ref[place, 24 + s] > 0.5) & (low_x + BLOCK > 0) & (low_y + BLOCK > 0)

    def weights(c, low, count):
        cell = lax.broadcasted_iota(jnp.int32, (count, NODES), 0)
        position = centre[c] + off_ref[c : c + 1, :]
        distance = position - ((anchor[c] - low) + cell).astype(F32)
        inside = (cell >= low) & (cell < low + BLOCK)
        return jnp.where(inside, jnp.exp(-distance * distance), 0.0)

    return (
        place,
        s,
        active,
        anchor[2],
        lambda: (weights(0, low_x, size_x), weights(1, low_y, size_y), weights(2, anchor[2] % 8, 32)),
    )


def stacked(values, second):
    high, low = split(values)
    return jnp.concatenate([high, low, high] if second else [high, high, low], axis=0)


def spread_kernel(wide_count, narrow_count, meta_ref, held_ref, off_ref, tz_ref, out_ref, a_high, a_low, total, turned):
    total[...] = jnp.zeros_like(total)

    def sphere(index, carry):
        place, s, active, low_z, weights = sphere_weights(wide_count, narrow_count, index, meta_ref, off_ref)

        @pl.when(active)
        def _():
            wx, wy, wz = weights()
            table = tz_ref[pl.ds(pl.multiple_of(low_z // 8 * 8, 8), 32), :]
            along_z = split(
                dot(jnp.transpose(stacked(wz, False).astype(F32)).astype(BF16), stacked(table, True))
            )
            planar = jnp.concatenate(
                [
                    wy * (spread_norm * held_ref[place, pl.ds(s * 3 + c, 1), :])
                    for c in range(3)
                ],
                axis=0,
            )
            for x in range(8):
                high, low = split(planar * wx[x : x + 1, :])
                a_high[x * 96 : x * 96 + 96, :] = high
                a_low[x * 96 : x * 96 + 96, :] = low
            total[...] += dot3((a_high[...], a_low[...]), along_z)

        return carry

    lax.fori_loop(0, 24, sphere, 0)
    for x in range(8):
        block = jnp.concatenate([total[x * 96 : x * 96 + 96, :], jnp.zeros((32, GRID), F32)], axis=0)
        turned[pl.ds(x, GRID, stride=8), :] = jnp.transpose(block)
    values = turned[...].reshape(64, 4, 8, 128)
    packed = pack_lanes(*[values[:, j] for j in range(4)])
    for g in range(3):
        out_ref[:, :, :, g * 128 : g * 128 + 128] = packed[g].reshape(32, 2, 8, 128)


def interp_kernel(wide_count, narrow_count, meta_ref, off_ref, tz_ref, mesh_ref, out_ref, m_high, m_low, turned):
    out_ref[...] = jnp.zeros_like(out_ref)
    groups = [mesh_ref[:, :, :, g * 128 : g * 128 + 128].reshape(64, 8, 128) for g in range(3)]
    unpacked = unpack_lanes(*groups)
    turned[...] = jnp.stack(unpacked, axis=1).reshape(GRID * 8, 128)
    for x in range(8):
        block = jnp.transpose(turned[pl.ds(x, GRID, stride=8), :])
        high, low = split(block[:96])
        m_high[x * 96 : x * 96 + 96, :] = high
        m_low[x * 96 : x * 96 + 96, :] = low

    def sphere(index, carry):
        place, s, active, low_z, weights = sphere_weights(wide_count, narrow_count, index, meta_ref, off_ref)

        @pl.when(active)
        def _():
            wx, wy, wz = weights()
            table = tz_ref[pl.ds(pl.multiple_of(low_z // 8 * 8, 8), 32), :]
            along_z = split(
                dot(jnp.transpose(stacked(table, True).astype(F32)).astype(BF16), stacked(wz, False))
            )
            found = dot3((m_high[...], m_low[...]), along_z)
            summed = found[0:96] * wx[0:1, :]
            for x in range(1, 8):
                summed = summed + found[x * 96 : x * 96 + 96] * wx[x : x + 1, :]
            rows = [
                jnp.sum(summed[c * 32 : c * 32 + 32] * wy, axis=0, keepdims=True) * spread_norm
                for c in range(3)
            ]
            owner = index // 4
            for c in range(3):
                out_ref[owner, pl.ds(s * 3 + c, 1), :] = rows[c]

        return carry

    lax.fori_loop(0, 24, sphere, 0)


class Exchange:
    def __init__(self, axis, count, source, target, half, send_sem, recv_sem, me, other):
        self.__dict__.update(locals())

    def copy_to(self, step):
        to = lax.rem(self.me + step, self.count)
        return pltpu.make_async_remote_copy(
            src_ref=self.source.at[to, self.half],
            dst_ref=self.target.at[self.me, self.half],
            send_sem=self.send_sem.at[step],
            recv_sem=self.recv_sem.at[step],
            device_id=(to, self.other) if self.axis == "wide" else (self.other, to),
            device_id_type=MESH,
        )

    def begin(self):
        def step(index, carry):
            self.copy_to(index).start()
            return carry

        lax.fori_loop(1, self.count, step, 0)
        self.target[self.me, self.half] = self.source[self.me, self.half]

    def arrive(self):
        def step(index, carry):
            self.copy_to(index).wait_recv()
            return carry

        lax.fori_loop(1, self.count, step, 0)

    def sent(self):
        def step(index, carry):
            self.copy_to(index).wait_send()
            return carry

        lax.fori_loop(1, self.count, step, 0)


def transform_kernel(
    wide_count,
    narrow_count,
    mesh_ref,
    list_ref,
    meta_ref,
    held_ref,
    off_ref,
    pairs_ref,
    gap_ref,
    angles_ref,
    tables,
    out_ref,
    near_ref,
    contacts_ref,
    wide_in,
    narrow_out,
    narrow_in,
    narrow_back,
    narrow_home,
    wide_back,
    wide_home,
    lines,
    spectrum,
    t_x,
    t_yf,
    t_yi,
    offcol,
    source,
    columns,
    own_line,
    lines_in,
    column_out,
    column_in,
    wide_send,
    wide_recv,
    narrow_send,
    narrow_recv,
    table_sem,
    line_send,
    line_recv,
    column_send,
    column_recv,
):
    w, n = lax.axis_index("wide"), lax.axis_index("narrow")
    load = pltpu.make_async_copy(tables, t_x, table_sem)
    load.start()
    greet(
        wide_count,
        narrow_count,
        [(step, 0) for step in range(1, wide_count)] + [(0, step) for step in range(1, narrow_count)],
    )

    def exchanges(axis, source, target, way):
        if axis == "wide":
            fixed = (wide_count, w, n, wide_send, wide_recv)
        else:
            fixed = (narrow_count, n, w, narrow_send, narrow_recv)
        count, me, other, send_sem, recv_sem = fixed
        return [
            Exchange(
                axis, count, source, target, half, send_sem.at[way, half], recv_sem.at[way, half], me, other
            )
            for half in (0, 1)
        ]

    wide_go = exchanges("wide", mesh_ref, wide_in, 0)
    narrow_go = exchanges("narrow", narrow_out, narrow_in, 0)
    narrow_return = exchanges("narrow", narrow_back, narrow_home, 1)
    wide_return = exchanges("wide", wide_back, wide_home, 1)
    for half in (0, 1):
        wide_go[half].begin()

    ids = pairs_ref[...]
    within = (ids % SLOTS_DEV).astype(F32)
    holder = ids // SLOTS_DEV
    row_w = lax.rem(holder // narrow_count - w + 1 + wide_count, wide_count)
    row_n = lax.rem(lax.rem(holder, narrow_count) - n + 1 + narrow_count, narrow_count)
    seconds = ((row_w * 3 + row_n) * SLOTS_DEV).astype(F32) + within
    polar, azimuth = angles_ref[0:1, :], angles_ref[1:2, :]
    across = jnp.sin(polar)
    fields = [
        within[0:1],
        seconds[1:2],
        across * jnp.cos(azimuth),
        across * jnp.sin(azimuth),
        jnp.cos(polar),
        gap_ref[...].reshape(1, CONT_DEV),
    ]
    line = jnp.concatenate(fields + [jnp.zeros((1, 64), F32)], axis=1)
    own_line[...] = jnp.where(lax.broadcasted_iota(jnp.int32, (8, NODES), 0) == n, line, 0.0)

    def line_copy(step):
        return pltpu.make_async_remote_copy(
            src_ref=own_line,
            dst_ref=lines_in.at[step],
            send_sem=line_send.at[step],
            recv_sem=line_recv.at[step],
            device_id=(w, lax.rem(n + step, narrow_count)),
            device_id_type=MESH,
        )

    def column_copy(step):
        return pltpu.make_async_remote_copy(
            src_ref=column_out,
            dst_ref=column_in.at[w],
            send_sem=column_send.at[step],
            recv_sem=column_recv.at[step],
            device_id=(lax.rem(w + step, wide_count), n),
            device_id_type=MESH,
        )

    for step in range(1, narrow_count):
        line_copy(step).start()
    near_field(
        (wide_count, narrow_count), list_ref, meta_ref, held_ref, off_ref, near_ref, offcol, source, columns
    )
    load.wait()
    t_yf[...] = jnp.zeros_like(t_yf)
    for part in (0, 1):
        for piece in range(8):
            for c in range(3):
                t_yf[part, piece * 128 + c * 32 : piece * 128 + c * 32 + 32, c * 256 : c * 256 + 256] = t_x[
                    4 + part, piece * 32 : piece * 32 + 32, :
                ]
        for piece in range(8):
            for c in range(3):
                block = t_yf[part, piece * 128 : piece * 128 + 128, c * 256 : c * 256 + 256]
                t_yi[part, c * 256 : c * 256 + 256, piece * 128 : piece * 128 + 128] = jnp.transpose(
                    block.astype(F32)
                ).astype(BF16)
    for half in (0, 1):
        wide_go[half].arrive()
        block = split(wide_in[:, half].reshape(GRID, 384))
        along = dot3((t_x[0], t_x[1]), block)
        narrow_out[:, half] = along.reshape(narrow_count, 32, 384)
        narrow_go[half].begin()
    column = own_line[...]
    for step in range(1, narrow_count):
        line_copy(step).wait_recv()
        column = column + lines_in[step]
    column_out[...] = column
    column_in[w] = column

    def begin_column(step, carry):
        column_copy(step).start()
        return carry

    lax.fori_loop(1, wide_count, begin_column, 0)
    for half in (0, 1):
        narrow_go[half].arrive()
        for piece in range(8):
            groups = [narrow_in[piece, half, :, g * 128 : g * 128 + 128] for g in range(3)]
            unpacked = unpack_lanes(*groups)
            for j in range(4):
                lines[half * 128 + j * 32 : half * 128 + j * 32 + 32, piece * 128 : piece * 128 + 128] = unpacked[j]
        rows = slice(half * 128, half * 128 + 128)
        spectrum[rows, :] = dot3(split(lines[rows, :]), (t_yf[0], t_yf[1]))

    row = lax.broadcasted_iota(jnp.int32, (32, 1), 0)
    k_x = (n * 16 + row % 16).astype(F32)
    nyquist_x = jnp.where((row >= 16) & (k_x < 0.5), 128.0, 0.0)
    lane = lax.broadcasted_iota(jnp.int32, (1, GRID), 1)
    k_y = (lane % 128).astype(F32)
    nyquist_y = jnp.where((lane >= 128) & (k_y < 0.5), 128.0, 0.0)
    square_xy = k_x * k_x + nyquist_x * nyquist_x + (k_y * k_y + nyquist_y * nyquist_y)
    scale_x = jnp.where(k_x < 0.5, 1.0, 2.0)
    scale_y = jnp.where(k_y < 0.5, 1.0, 2.0)
    scale_xy = scale_x * scale_y
    damping = (ewald_split * np.pi / GRID) ** 2
    constant = GRID * GRID / (4.0 * np.pi * np.pi) / float(GRID) ** 3
    turn_x = jnp.where(row < 16, k_x, -k_x)
    turn_y = jnp.where(lane < 128, k_y, -k_y)

    def derive_x(values):
        return turn_x * jnp.concatenate([values[16:], values[:16]], axis=0)

    def derive_y(values):
        return turn_y * jnp.concatenate([values[:, 128:], values[:, :128]], axis=1)

    def filtered(j, carry):
        k_z = (w * 4 + j).astype(F32)
        bases = [pl.multiple_of(half * 128 + j * 32, 32) for half in (0, 1)]
        fields = [
            [spectrum[pl.ds(bases[half], 32), c * 256 : c * 256 + 256] for c in range(3)]
            for half in (0, 1)
        ]
        flows = []
        nyquists_z = [jnp.zeros_like(k_z), jnp.where(k_z < 0.5, 128.0, 0.0)]
        scale_z = jnp.where(k_z < 0.5, 1.0, 2.0)
        turn_z = (k_z, -k_z)
        for half in (0, 1):
            values = fields[half]
            flows.append(derive_x(values[0]) + derive_y(values[1]) + turn_z[half] * fields[1 - half][2])
        for half in (0, 1):
            values = fields[half]
            nyquist_z = nyquists_z[half]
            square = square_xy + (k_z * k_z + nyquist_z * nyquist_z)
            safe = jnp.maximum(square, 1.0)
            inverse = 1.0 / safe
            factor = jnp.where(square > 0.5, jnp.exp(-damping * square) * inverse, 0.0)
            factor = factor * (scale_xy * (scale_z * constant))
            edge = (nyquist_x * values[0] + nyquist_y * values[1] + nyquist_z * values[2]) * inverse
            flow = [flows[half] * inverse, flows[1 - half] * inverse]
            gradient = [derive_x(flow[0]), derive_y(flow[0]), None]
            gradient[2] = turn_z[half] * (flows[1 - half] * inverse)
            nyquist = (nyquist_x, nyquist_y, nyquist_z)
            for c in range(3):
                spectrum[pl.ds(bases[half], 32), c * 256 : c * 256 + 256] = factor * (
                    values[c] + gradient[c] - nyquist[c] * edge
                )
        return carry

    lax.fori_loop(0, 4, filtered, 0)
    for half in (0, 1):
        rows = slice(half * 128, half * 128 + 128)
        lines[rows, :] = dot3(split(spectrum[rows, :]), (t_yi[0], t_yi[1]))
        for target in range(8):
            groups = [
                lines[half * 128 + j * 32 : half * 128 + j * 32 + 32, target * 128 : target * 128 + 128]
                for j in range(4)
            ]
            packed = pack_lanes(*groups)
            for g in range(3):
                narrow_back[target, half, :, g * 128 : g * 128 + 128] = packed[g]
        narrow_return[half].begin()
    for half in (0, 1):
        narrow_return[half].arrive()
        block = split(narrow_home[:, half].reshape(GRID, 384))
        along = dot3((t_x[2], t_x[3]), block)
        wide_back[:, half] = along.reshape(wide_count, 8, 384)
        wide_return[half].begin()
    def end_column(step, carry):
        column_copy(step).wait()
        return carry

    lax.fori_loop(1, wide_count, end_column, 0)
    for step in range(1, narrow_count):
        line_copy(step).wait_send()
    contacts_ref[...] = column_in[...].reshape(wide_count * narrow_count, NODES)
    for group in (wide_go, narrow_go, narrow_return):
        for half in (0, 1):
            group[half].sent()
    for half in (0, 1):
        wide_return[half].arrive()
        out_ref[:, half] = wide_home[:, half]
    for half in (0, 1):
        wide_return[half].sent()


AROUND = [(dw, dn) for dw in (-1, 0, 1) for dn in (-1, 0, 1)]
PARTIAL = [(dw, dn) for dw in (-2, -1, 0) for dn in (-1, 0)]


def shift_narrow(values, dn, narrow_count):
    if dn == 0:
        return values
    place = lanes_of(values.shape) % narrow_count
    edge = 0 if dn == 1 else narrow_count - 1
    total = values.shape[-1]
    return jnp.where(
        place == edge,
        roll(values, (dn - dn * narrow_count) % total),
        roll(values, dn % total),
    )


def shift_wide(values, dw, narrow_count):
    if dw == 0:
        return values
    return roll(values, (dw * narrow_count) % values.shape[-1])


def contact_kernel(
    wide_count,
    narrow_count,
    part_ref,
    near_ref,
    static_ref,
    centre_ref,
    velocity_ref,
    force_ref,
    moved_ref,
    part_in,
    tile_out,
    tile_in,
    table_out,
    table_in,
    edges,
    around,
    loads,
    part_send,
    part_recv,
    narrow_send,
    narrow_recv,
    wide_send,
    wide_recv,
):
    w, n = lax.axis_index("wide"), lax.axis_index("narrow")
    devices = wide_count * narrow_count

    def device(dw, dn):
        return (
            lax.rem(w + dw + wide_count, wide_count),
            lax.rem(n + dn + narrow_count, narrow_count),
        )

    greet(
        wide_count,
        narrow_count,
        [(step, 0) for step in range(1, wide_count)]
        + [(0, step) for step in range(1, narrow_count)]
        + [(-2, -1), (-1, -1), (2, 1), (1, 1)],
    )
    own = PARTIAL.index((0, 0))
    pieces = [part_ref[p] + near_ref[...] if p == own else part_ref[p] for p in range(6)]
    means = [jnp.sum(piece, axis=1, keepdims=True) * (1.0 / NODES) for piece in pieces]
    column = jnp.concatenate(means + [jnp.zeros((32, 1), F32)], axis=0)
    line = jnp.transpose(jnp.broadcast_to(column, (128, 128)))[:8]
    tile_out[...] = jnp.where(lax.broadcasted_iota(jnp.int32, (8, 128), 0) == n, line, 0.0)

    def narrow_copy(step):
        to = lax.rem(n + step, narrow_count)
        return pltpu.make_async_remote_copy(
            src_ref=tile_out,
            dst_ref=tile_in.at[step],
            send_sem=narrow_send.at[step],
            recv_sem=narrow_recv.at[step],
            device_id=(w, to),
            device_id_type=MESH,
        )

    def wide_copy(step):
        to = lax.rem(w + step, wide_count)
        return pltpu.make_async_remote_copy(
            src_ref=table_out,
            dst_ref=table_in.at[w],
            send_sem=wide_send.at[step],
            recv_sem=wide_recv.at[step],
            device_id=(to, n),
            device_id_type=MESH,
        )

    for step in range(1, narrow_count):
        narrow_copy(step).start()
    copies = []
    for place, (dw, dn) in enumerate(PARTIAL):
        if (dw, dn) == (0, 0):
            continue
        copy = pltpu.make_async_remote_copy(
            src_ref=part_ref.at[place],
            dst_ref=part_in.at[place],
            send_sem=part_send.at[place],
            recv_sem=part_recv.at[place],
            device_id=device(dw, dn),
            device_id_type=MESH,
        )
        copy.start()
        copies.append((place, copy))
    tile = tile_out[...]
    for step in range(1, narrow_count):
        narrow_copy(step).wait_recv()
        tile = tile + tile_in[step]
    table_out[...] = tile
    table_in[w] = tile

    def begin(step, carry):
        wide_copy(step).start()
        return carry

    lax.fori_loop(1, wide_count, begin, 0)

    fields = jnp.transpose(static_ref[...])
    first, second, gap = fields[0:32], fields[32:64], fields[160:192]
    normal = [fields[64 + 32 * c : 96 + 32 * c] for c in range(3)]
    for place in range(9):
        for s in range(SLOTS_DEV):
            mark = jnp.where(second == float(place * SLOTS_DEV + s), -1.0, 0.0)
            if place == 4:
                mark = mark + jnp.where(first == float(s), 1.0, 0.0)
            for c in range(3):
                edges[place, 3 * s + c] = mark * normal[c]

    velocity = pieces[own]
    for place, copy in copies:
        copy.wait_recv()
        velocity = velocity + part_in[place]
    velocity_ref[...] = velocity

    def end(step, carry):
        wide_copy(step).wait_recv()
        return carry

    lax.fori_loop(1, wide_count, end, 0)
    spread_means = jnp.transpose(table_in[...].reshape(devices, 128))
    hydro = jnp.zeros((16, devices), F32)
    for p, (dw, dn) in enumerate(PARTIAL):
        moved_means = shift_wide(spread_means[p * 16 : p * 16 + 16], dw, narrow_count)
        hydro = hydro + shift_narrow(moved_means, dn, narrow_count)

    def totals(force):
        def one_place(place, carry):
            for k in range(ROWS_DEV):
                loads[place, k : k + 1, :] = jnp.sum(edges[place, k] * force, axis=0, keepdims=True)
            return carry

        lax.fori_loop(0, 9, one_place, 0)
        result = jnp.zeros((16, devices), F32)
        for dn in (-1, 0, 1):
            inner = jnp.zeros((16, devices), F32)
            for dw in (-1, 0, 1):
                inner = inner + shift_wide(loads[AROUND.index((dw, dn))], dw, narrow_count)
            result = result + shift_narrow(inner, dn, narrow_count)
        return result

    def sweep(turn, carry):
        force, moving = carry
        for dn in (-1, 0, 1):
            beside = shift_narrow(moving, -dn, narrow_count)
            for dw in (-1, 0, 1):
                around[AROUND.index((dw, dn))] = shift_wide(beside, -dw, narrow_count)

        def one_place(place, relative):
            for k in range(ROWS_DEV):
                relative = relative + edges[place, k] * around[place, k : k + 1, :]
            return relative

        relative = lax.fori_loop(0, 9, one_place, jnp.zeros((CONT_DEV, devices), F32))
        force = jnp.maximum(
            force - relaxation * (gap + time_step * relative) / (2.0 * time_step * mobility), 0.0
        )
        return force, hydro + mobility * totals(force)

    loads[...] = jnp.zeros_like(loads)
    force, moving = lax.fori_loop(
        0, SWEEPS, sweep, (jnp.zeros((CONT_DEV, devices), F32), hydro)
    )
    mine = lanes_of((1, devices)) == w * narrow_count + n
    own_force = jnp.sum(jnp.where(mine, force, 0.0), axis=1, keepdims=True)
    force_ref[...] = jnp.broadcast_to(own_force, (CONT_DEV, 128))
    own_moving = jnp.sum(jnp.where(mine, moving, 0.0), axis=1, keepdims=True)
    moved_ref[...] = centre_ref[...] + time_step * own_moving
    for place, copy in copies:
        copy.wait_send()
    for step in range(1, narrow_count):
        narrow_copy(step).wait_send()

    def finish(step, carry):
        wide_copy(step).wait_send()
        return carry

    lax.fori_loop(1, wide_count, finish, 0)


def local(
    wide_count,
    narrow_count,
    tractions,
    centers,
    node_offsets,
    occupied,
    anchors,
    near_list,
    contact_pairs,
    contact_gap,
    contact_angles,
):
    w, n = lax.axis_index("wide"), lax.axis_index("narrow")
    sizes = (wide_count, narrow_count)
    shape = jax.ShapeDtypeStruct
    dma = pltpu.SemaphoreType.DMA

    held, metas = pl.pallas_call(
        functools.partial(gather_kernel, *sizes),
        out_shape=(shape((12, 16, NODES), F32), shape((12, 128), F32)),
        in_specs=[VMEM_SPEC, SMEM_SPEC, SMEM_SPEC, SMEM_SPEC],
        out_specs=(VMEM_SPEC, VMEM_SPEC),
        scratch_shapes=[
            pltpu.VMEM((16, NODES), F32),
            pltpu.VMEM((12, 16, NODES), F32),
            dma((12,)),
            dma((12,)),
        ],
        compiler_params=params(0),
        name="gather",
    )(tractions, centers, anchors, occupied)

    table_z = trig_table(4)
    wrapped_z = np.concatenate([table_z, table_z[:, :32]], axis=1).T.astype(np.float32)
    mesh = pl.pallas_call(
        functools.partial(spread_kernel, *sizes),
        out_shape=shape((32, 2, 8, 384), F32),
        in_specs=[SMEM_SPEC, VMEM_SPEC, VMEM_SPEC, VMEM_SPEC],
        out_specs=VMEM_SPEC,
        scratch_shapes=[
            pltpu.VMEM((768, NODES), BF16),
            pltpu.VMEM((768, NODES), BF16),
            pltpu.VMEM((768, GRID), F32),
            pltpu.VMEM((GRID * 8, 128), F32),
        ],
        compiler_params=params(),
        name="spread",
    )(metas, held, node_offsets, wrapped_z)

    table_x = trig_table(16)
    table_y = trig_table(128)
    turned_x = np.ascontiguousarray(table_x.T)
    turned_y = np.ascontiguousarray(table_y.T)
    tables = np.stack([*halves(table_x), *halves(turned_x), *halves(turned_y)])
    mesh, near, contacts = pl.pallas_call(
        functools.partial(transform_kernel, *sizes),
        out_shape=(
            shape((32, 2, 8, 384), F32),
            shape((16, NODES), F32),
            shape((wide_count * narrow_count, NODES), F32),
        ),
        in_specs=[VMEM_SPEC, SMEM_SPEC, SMEM_SPEC] + [VMEM_SPEC] * 5 + [HBM_SPEC],
        out_specs=(VMEM_SPEC,) * 3,
        scratch_shapes=[
            pltpu.VMEM((32, 2, 8, 384), F32),
            pltpu.VMEM((8, 2, 32, 384), F32),
            pltpu.VMEM((8, 2, 32, 384), F32),
            pltpu.VMEM((8, 2, 32, 384), F32),
            pltpu.VMEM((8, 2, 32, 384), F32),
            pltpu.VMEM((32, 2, 8, 384), F32),
            pltpu.VMEM((32, 2, 8, 384), F32),
            pltpu.VMEM((256, 1024), F32),
            pltpu.VMEM((256, 768), F32),
            pltpu.VMEM((6, 256, 256), BF16),
            pltpu.VMEM((2, 1024, 768), BF16),
            pltpu.VMEM((2, 768, 1024), BF16),
            pltpu.VMEM((3, NODES, 128), F32),
            pltpu.VMEM((3, 8, NODES), F32),
            pltpu.VMEM((NODES, 8), F32),
            pltpu.VMEM((8, NODES), F32),
            pltpu.VMEM((8, 8, NODES), F32),
            pltpu.VMEM((8, NODES), F32),
            pltpu.VMEM((32, 8, NODES), F32),
            dma((2, 2, 32)),
            dma((2, 2, 32)),
            dma((2, 2, 8)),
            dma((2, 2, 8)),
            dma,
            dma((8,)),
            dma((8,)),
            dma((32,)),
            dma((32,)),
        ],
        compiler_params=params(1),
        name="transform",
    )(
        mesh,
        near_list.reshape(4, NEAR),
        metas,
        held,
        node_offsets,
        contact_pairs,
        contact_gap,
        contact_angles,
        tables,
    )

    part = pl.pallas_call(
        functools.partial(interp_kernel, *sizes),
        out_shape=shape((6, 16, NODES), F32),
        in_specs=[SMEM_SPEC, VMEM_SPEC, VMEM_SPEC, VMEM_SPEC],
        out_specs=VMEM_SPEC,
        scratch_shapes=[
            pltpu.VMEM((768, GRID), BF16),
            pltpu.VMEM((768, GRID), BF16),
            pltpu.VMEM((GRID * 8, 128), F32),
        ],
        compiler_params=params(),
        name="interpolate",
    )(metas, node_offsets, wrapped_z, mesh)

    centre_rows = jnp.broadcast_to(jnp.pad(centers.reshape(12, 1), ((0, 4), (0, 0))), (16, 128))
    devices = wide_count * narrow_count
    velocity, force, moved = pl.pallas_call(
        functools.partial(contact_kernel, *sizes),
        out_shape=(shape((16, NODES), F32), shape((CONT_DEV, 128), F32), shape((16, 128), F32)),
        in_specs=[VMEM_SPEC] * 4,
        out_specs=(VMEM_SPEC,) * 3,
        scratch_shapes=[
            pltpu.VMEM((6, 16, NODES), F32),
            pltpu.VMEM((8, 128), F32),
            pltpu.VMEM((8, 8, 128), F32),
            pltpu.VMEM((8, 128), F32),
            pltpu.VMEM((32, 8, 128), F32),
            pltpu.VMEM((9, ROWS_DEV, CONT_DEV, devices), F32),
            pltpu.VMEM((9, 16, devices), F32),
            pltpu.VMEM((9, 16, devices), F32),
            dma((6,)),
            dma((6,)),
            dma((8,)),
            dma((8,)),
            dma((32,)),
            dma((32,)),
        ],
        compiler_params=params(2),
        name="contacts",
    )(part, near, contacts, centre_rows)
    return (
        velocity[:12].reshape(2, 2, 3, NODES),
        force[:, 0],
        moved[:12, 0].reshape(2, 2, 3),
    )


def solution(mesh):
    placed = (
        P("wide", "narrow", None, None),
        P("wide", "narrow", None),
        P(),
        P("wide", "narrow"),
        P("wide", "narrow", None),
        P("wide", "narrow", None),
        P(None, ("wide", "narrow")),
        P(("wide", "narrow")),
        P(None, ("wide", "narrow")),
    )
    return jax.shard_map(
        functools.partial(local, mesh.shape["wide"], mesh.shape["narrow"]),
        mesh=mesh,
        in_specs=placed,
        out_specs=(
            P("wide", "narrow", None, None),
            P(("wide", "narrow")),
            P("wide", "narrow", None),
        ),
        check_vma=False,
    )
```

```python
import functools

import jax
import jax.numpy as jnp
import ml_dtypes
import numpy as np
from jax import lax
from jax.experimental import pallas as pl
from jax.experimental.pallas import tpu as pltpu
from jax.sharding import PartitionSpec as P

NODES = 256
GRID = 256
BLOCK = 16
NEAR = 2
SWEEPS = 6
SLOTS_DEV = 4
ROWS_DEV = 3 * SLOTS_DEV
CONT_DEV = 32

soften = 1.0
screen = 0.0625
near_scale = 0.05
spread_norm = 0.17958712212516656
mobility = 0.2
time_step = 0.5
relaxation = 0.35
ewald_split = 0.5

MESH = pl.DeviceIdType.MESH
F32 = jnp.float32
BF16 = jnp.bfloat16
VMEM_SPEC = pl.BlockSpec(memory_space=pltpu.VMEM)
HBM_SPEC = pl.BlockSpec(memory_space=pltpu.HBM)
SMEM_SPEC = pl.BlockSpec(memory_space=pltpu.SMEM)


def params(collective_id=None, limit=40):
    if collective_id is None:
        return pltpu.CompilerParams(vmem_limit_bytes=limit * 2**20)
    return pltpu.CompilerParams(
        vmem_limit_bytes=limit * 2**20, collective_id=collective_id, has_side_effects=True
    )


def trig_table(group):
    cell = np.arange(GRID)
    rows = []
    for first in range(0, GRID // 2, group):
        for half in (0, 1):
            for k in range(first, first + group):
                angle = 2.0 * np.pi / GRID * (k * cell % GRID)
                if half == 0:
                    rows.append(np.cos(angle))
                elif k == 0:
                    rows.append(np.cos(np.pi * cell))
                else:
                    rows.append(np.sin(angle))
    return np.stack(rows)


def halves(table):
    high = table.astype(np.float32).astype(ml_dtypes.bfloat16)
    low = (table - high.astype(np.float64)).astype(np.float32).astype(ml_dtypes.bfloat16)
    return high, low


def split(values):
    high = values.astype(BF16)
    return high, (values - high.astype(F32)).astype(BF16)


def dot(a, b, contract=((1,), (0,))):
    return lax.dot_general(a, b, (contract, ((), ())), preferred_element_type=F32)


def dot3(a, b):
    return dot(
        jnp.concatenate([a[0], a[0], a[1]], axis=1), jnp.concatenate([b[0], b[1], b[0]], axis=0)
    )


def lanes_of(shape):
    return lax.broadcasted_iota(jnp.int32, shape, len(shape) - 1)


def roll(values, shift):
    return pltpu.roll(values, shift, len(values.shape) - 1)


def pack_lanes(u0, u1, u2, u3):
    lane = lanes_of(u0.shape)
    r1, r2, r3 = roll(u1, 96), roll(u2, 64), roll(u3, 32)
    return (
        jnp.where(lane < 96, u0, r1),
        jnp.where(lane < 64, r1, r2),
        jnp.where(lane < 32, r2, r3),
    )


def unpack_lanes(p0, p1, p2):
    lane = lanes_of(p0.shape)
    return (
        p0,
        roll(jnp.where(lane < 64, p1, p0), 32),
        roll(jnp.where(lane < 32, p2, p1), 64),
        roll(p2, 96),
    )


def hail(wide_count, narrow_count, offsets):
    w, n = lax.axis_index("wide"), lax.axis_index("narrow")
    for dw, dn in offsets:
        pl.semaphore_signal(
            pltpu.get_barrier_semaphore(),
            inc=1,
            device_id=(
                lax.rem(w + dw + wide_count, wide_count),
                lax.rem(n + dn + narrow_count, narrow_count),
            ),
            device_id_type=MESH,
        )


def hear(offsets):
    pl.semaphore_wait(pltpu.get_barrier_semaphore(), len(offsets))


GATHER = [(dw, dn) for dw in (-2, -1, 0, 1) for dn in (-1, 0, 1)]


def gather_kernel(
    wide_count,
    narrow_count,
    tractions_ref,
    centres_ref,
    anchors_ref,
    occupied_ref,
    out_ref,
    meta_ref,
    cells_ref,
    own_ref,
    held,
    send_sem,
    recv_sem,
):
    w, n = lax.axis_index("wide"), lax.axis_index("narrow")
    reach = [(dw, dn) for dw in (-2, -1, 0, 1, 2) for dn in (-1, 0, 1) if (dw, dn) != (0, 0)]
    hail(wide_count, narrow_count, reach)
    slots = [(a, b) for a in (0, 1) for b in (0, 1)]
    numbers = [centres_ref[a, b, c] for a, b in slots for c in range(3)]
    numbers += [anchors_ref[a, b, c].astype(F32) for a, b in slots for c in range(3)]
    numbers += [occupied_ref[a, b].astype(F32) for a, b in slots]
    lane = lanes_of((1, NODES))
    line = jnp.zeros((1, NODES), F32)
    for place, number in enumerate(numbers):
        line = jnp.where(lane == place, number, line)
    for s, (a, b) in enumerate(slots):
        own_ref[3 * s : 3 * s + 3, :] = tractions_ref[a, b]
    own_ref[12:16, :] = jnp.broadcast_to(line, (4, NODES))
    hear(reach)
    copies = []
    for place, (dw, dn) in enumerate(GATHER):
        if (dw, dn) == (0, 0):
            continue
        copy = pltpu.make_async_remote_copy(
            src_ref=own_ref,
            dst_ref=held.at[place],
            send_sem=send_sem.at[place],
            recv_sem=recv_sem.at[place],
            device_id=(
                lax.rem(w - dw + wide_count, wide_count),
                lax.rem(n - dn + narrow_count, narrow_count),
            ),
            device_id_type=MESH,
        )
        copy.start()
        copies.append((place, copy))
    own = GATHER.index((0, 0))
    out_ref[own] = own_ref[...]
    meta_ref[own : own + 1, :] = own_ref[12:13, 0:128]
    cells_ref[own : own + 1, :] = own_ref[12:13, 0:128].astype(jnp.int32)
    for place, copy in copies:
        copy.wait_recv()
        out_ref[place] = held[place]
        meta_ref[place : place + 1, :] = held[place, 12:13, 0:128]
        cells_ref[place : place + 1, :] = held[place, 12:13, 0:128].astype(jnp.int32)
    for place, copy in copies:
        copy.wait_send()


def near_field(sizes, list_ref, meta_ref, held_ref, off_ref, out_ref, offcol, source, columns):
    wide_count, narrow_count = sizes
    w, n = lax.axis_index("wide"), lax.axis_index("narrow")
    own = GATHER.index((0, 0))
    out_ref[...] = jnp.zeros_like(out_ref)
    columns[...] = jnp.zeros_like(columns)
    for s in range(SLOTS_DEV):
        for j in range(1 + NEAR):
            if j == 0:
                place, within = own, s
            else:
                entry = list_ref[s, j - 1]
                holder = entry // SLOTS_DEV
                within = entry % SLOTS_DEV
                row = lax.rem(holder // narrow_count - w + 1 + wide_count, wide_count)
                column = lax.rem(lax.rem(holder, narrow_count) - n + 1 + narrow_count, narrow_count)
                place = (jnp.minimum(row, 2) + 1) * 3 + jnp.minimum(column, 2)
            for c in range(3):
                if j == 0:
                    shift = 0.0
                else:
                    e = meta_ref[own, 3 * s + c] - meta_ref[place, 3 * within + c]
                    shift = e - jnp.where(e >= 128.0, 256.0, jnp.where(e < -128.0, -256.0, 0.0))
                source[j, c : c + 1, :] = shift - off_ref[c : c + 1, :]
                source[j, 3 + c : 4 + c, :] = held_ref[place, pl.ds(within * 3 + c, 1), :]

        def chunk(i, carry):
            for part in (0, 1):
                rows = pl.ds(pl.multiple_of(i * 16 + part * 8, 8), 8)
                sums = [jnp.zeros((8, 128), F32) for _ in range(3)]
                at = [offcol[c, rows, :] for c in range(3)]
                for j in range(1 + NEAR):
                    for half in (0, 1):
                        lanes = slice(half * 128, half * 128 + 128)
                        d = [at[c] + source[j, c : c + 1, lanes] for c in range(3)]
                        f = [source[j, 3 + c : 4 + c, lanes] for c in range(3)]
                        r2 = d[0] * d[0] + d[1] * d[1] + d[2] * d[2]
                        inverse = lax.rsqrt(r2 + soften)
                        weight = jnp.exp(r2 * (-screen)) * (inverse * inverse * inverse)
                        along = (d[0] * f[0] + d[1] * f[1] + d[2] * f[2]) * weight
                        diagonal = (r2 + 2.0 * soften) * weight
                        for c in range(3):
                            sums[c] = sums[c] + (diagonal * f[c] + d[c] * along)
                for c in range(3):
                    columns[rows, c : c + 1] = jnp.sum(sums[c], axis=1, keepdims=True)
            return carry

        lax.fori_loop(0, NODES // 16, chunk, 0)
        result = jnp.transpose(columns[...])
        alive = jnp.where(meta_ref[own, 24 + s] > 0.5, near_scale, 0.0)
        out_ref[3 * s : 3 * s + 3, :] = alive * result[0:3, :]


def columns_of(off_ref, offcol):
    padded = jnp.concatenate([off_ref[...], jnp.zeros((5, NODES), F32)], axis=0)
    turned = jnp.transpose(padded)
    for c in range(3):
        offcol[c] = jnp.broadcast_to(turned[:, c : c + 1], (NODES, 128))


def sphere_weights(sizes, dw, dn, s, meta_ref, cells_ref, off_ref, offcol, tz_ref):
    wide_count, narrow_count = sizes
    w, n = lax.axis_index("wide"), lax.axis_index("narrow")
    size_x, size_y = GRID // wide_count, GRID // narrow_count
    place = (dw + 2) * 3 + dn + 1
    anchor = [cells_ref[place, 12 + 3 * s + c] for c in range(3)]
    centre = [meta_ref[place, 3 * s + c] for c in range(3)]
    alive = jnp.where(meta_ref[place, 24 + s] > 0.5, spread_norm, 0.0)
    low_x = anchor[0] - size_x * lax.rem(w + dw + wide_count, wide_count) + size_x * dw
    low_y = anchor[1] - size_y * lax.rem(n + dn + narrow_count, narrow_count) + size_y * dn
    low_z = anchor[2] % 8

    def weights(cell, position, base, low, factor):
        distance = position - (base + cell).astype(F32)
        inside = (cell >= low) & (cell < low + BLOCK)
        return jnp.where(inside, jnp.exp(-distance * distance) * factor, 0.0)

    def rows(c, low, count, factor):
        cell = lax.broadcasted_iota(jnp.int32, (count, NODES), 0)
        return weights(cell, centre[c] + off_ref[c : c + 1, :], anchor[c] - low, low, factor)

    lane = lanes_of((NODES, 128))
    wz = weights(lane % 32, centre[2] + offcol[2], anchor[2] - low_z, low_z, 1.0)
    high = wz.astype(BF16).astype(F32)
    left = jnp.where(lane < 64, high, jnp.where(lane < 96, wz - high, 0.0)).astype(BF16)
    tile = anchor[2] // 8
    t_high, t_low = split(jnp.concatenate([tz_ref[tile + t] for t in range(4)], axis=0))
    right = jnp.concatenate([t_high, t_low, t_high, jnp.zeros((32, GRID), BF16)], axis=0)
    along_z = split(dot(left, right))
    return place, rows(0, low_x, size_x, alive), rows(1, low_y, 16 if dn else size_y, 1.0), along_z


def pair_loop(body, unroll=1):
    for dn in (-1, 0):

        def step(index, carry):
            body(index // 2 - 2, dn, index % 2)
            return carry

        lax.fori_loop(0, 6, step, 0, unroll=unroll)


def spread(sizes, meta_ref, cells_ref, held_ref, off_ref, tz_ref, out_ref, offcol, a_high, a_low, total, turned):
    total[...] = jnp.zeros_like(total)

    def pair(dw, dn, which):
        span = 16 if dn else 32
        sums = []
        for member in (0, 1):
            s = 2 * which + member
            place, wx, wy, along_z = sphere_weights(sizes, dw, dn, s, meta_ref, cells_ref, off_ref, offcol, tz_ref)
            planar = jnp.concatenate(
                [wy * held_ref[place, pl.ds(s * 3 + c, 1), :] for c in range(3)], axis=0
            )
            size = 3 * span
            for x in range(8):
                high, low = split(planar * wx[x : x + 1, :])
                a_high[member, x * size : x * size + size, :] = high
                a_low[member, x * size : x * size + size, :] = low
            rows = slice(0, 8 * size)
            sums.append(dot3((a_high[member, rows, :], a_low[member, rows, :]), along_z))
        both = sums[0] + sums[1]
        if dn == 0:
            total[...] += both
        else:
            for block in range(24):
                total[block * 32 : block * 32 + 16, :] += both[block * 16 : block * 16 + 16]

    pair_loop(pair)
    for x in range(8):
        block = jnp.concatenate([total[x * 96 : x * 96 + 96, :], jnp.zeros((32, GRID), F32)], axis=0)
        turned[pl.ds(x, GRID, stride=8), :] = jnp.transpose(block)
    values = turned[...].reshape(64, 4, 8, 128)
    packed = pack_lanes(*[values[:, j] for j in range(4)])
    for g in range(3):
        out_ref[:, :, :, g * 128 : g * 128 + 128] = packed[g].reshape(32, 2, 8, 128)


def interpolate(sizes, meta_ref, cells_ref, off_ref, tz_ref, mesh_ref, out_ref, offcol, m_high, m_low, h_high, h_low, turned):
    out_ref[...] = jnp.zeros_like(out_ref)
    groups = [mesh_ref[:, :, :, g * 128 : g * 128 + 128].reshape(64, 8, 128) for g in range(3)]
    unpacked = unpack_lanes(*groups)
    turned[...] = jnp.stack(unpacked, axis=1).reshape(GRID * 8, 128)
    for x in range(8):
        block = jnp.transpose(turned[pl.ds(x, GRID, stride=8), :])
        high, low = split(block[:96])
        m_high[x * 96 : x * 96 + 96, :] = high
        m_low[x * 96 : x * 96 + 96, :] = low
        for c in range(3):
            target = slice(x * 48 + c * 16, x * 48 + c * 16 + 16)
            h_high[target, :] = high[c * 32 : c * 32 + 16]
            h_low[target, :] = low[c * 32 : c * 32 + 16]

    def pair(dw, dn, which):
        span = 16 if dn else 32
        size = 3 * span
        for member in (0, 1):
            s = 2 * which + member
            place, wx, wy, along_z = sphere_weights(sizes, dw, dn, s, meta_ref, cells_ref, off_ref, offcol, tz_ref)
            left = (h_high[...], h_low[...]) if dn else (m_high[...], m_low[...])
            turn = ((1,), (1,))
            found = dot(
                jnp.concatenate([left[0], left[0], left[1]], axis=1),
                jnp.concatenate([along_z[0], along_z[1], along_z[0]], axis=1),
                turn,
            )
            summed = found[0:size] * wx[0:1, :]
            for x in range(1, 8):
                summed = summed + found[x * size : x * size + size] * wx[x : x + 1, :]
            owner = (dw + 2) * 2 + dn + 1
            for c in range(3):
                out_ref[owner, pl.ds(s * 3 + c, 1), :] = jnp.sum(
                    summed[c * span : c * span + span] * wy, axis=0, keepdims=True
                )

    pair_loop(pair, 2)


class Exchange:
    def __init__(self, axis, count, source, target, half, send_sem, recv_sem, me, other):
        self.__dict__.update(locals())

    def copy_to(self, step):
        to = lax.rem(self.me + step, self.count)
        return pltpu.make_async_remote_copy(
            src_ref=self.source.at[to, self.half],
            dst_ref=self.target.at[self.me, self.half],
            send_sem=self.send_sem.at[step],
            recv_sem=self.recv_sem.at[step],
            device_id=(to, self.other) if self.axis == "wide" else (self.other, to),
            device_id_type=MESH,
        )

    def begin(self):
        def step(index, carry):
            self.copy_to(index).start()
            return carry

        lax.fori_loop(1, self.count, step, 0)
        self.target[self.me, self.half] = self.source[self.me, self.half]

    def arrive(self):
        def step(index, carry):
            self.copy_to(index).wait_recv()
            return carry

        lax.fori_loop(1, self.count, step, 0)

    def sent(self):
        def step(index, carry):
            self.copy_to(index).wait_send()
            return carry

        lax.fori_loop(1, self.count, step, 0)


def transform_kernel(
    wide_count,
    narrow_count,
    list_ref,
    meta_ref,
    cells_ref,
    held_ref,
    off_ref,
    tz_ref,
    pairs_ref,
    gap_ref,
    angles_ref,
    tables,
    out_ref,
    near_ref,
    contacts_ref,
    a_high,
    a_low,
    total,
    turned,
    mesh_ref,
    wide_in,
    narrow_out,
    narrow_in,
    narrow_back,
    narrow_home,
    wide_back,
    wide_home,
    lines,
    spectrum,
    t_x,
    t_yf,
    t_yi,
    offcol,
    source,
    columns,
    own_line,
    lines_in,
    column_out,
    column_in,
    wide_send,
    wide_recv,
    narrow_send,
    narrow_recv,
    table_sem,
    line_send,
    line_recv,
    column_send,
    column_recv,
):
    w, n = lax.axis_index("wide"), lax.axis_index("narrow")
    load = pltpu.make_async_copy(tables, t_x, table_sem)
    load.start()
    reach = [(step, 0) for step in range(1, wide_count)] + [(0, step) for step in range(1, narrow_count)]
    sizes = (wide_count, narrow_count)
    hail(*sizes, reach)
    columns_of(off_ref, offcol)
    spread(sizes, meta_ref, cells_ref, held_ref, off_ref, tz_ref, mesh_ref, offcol, a_high, a_low, total, turned)
    hear(reach)

    def exchanges(axis, source, target, way):
        if axis == "wide":
            fixed = (wide_count, w, n, wide_send, wide_recv)
        else:
            fixed = (narrow_count, n, w, narrow_send, narrow_recv)
        count, me, other, send_sem, recv_sem = fixed
        return [
            Exchange(
                axis, count, source, target, half, send_sem.at[way, half], recv_sem.at[way, half], me, other
            )
            for half in (0, 1)
        ]

    wide_go = exchanges("wide", mesh_ref, wide_in, 0)
    narrow_go = exchanges("narrow", narrow_out, narrow_in, 0)
    narrow_return = exchanges("narrow", narrow_back, narrow_home, 1)
    wide_return = exchanges("wide", wide_back, wide_home, 1)
    for half in (0, 1):
        wide_go[half].begin()

    ids = pairs_ref[...]
    within = (ids % SLOTS_DEV).astype(F32)
    holder = ids // SLOTS_DEV
    row_w = lax.rem(holder // narrow_count - w + 1 + wide_count, wide_count)
    row_n = lax.rem(lax.rem(holder, narrow_count) - n + 1 + narrow_count, narrow_count)
    seconds = ((row_w * 3 + row_n) * SLOTS_DEV).astype(F32) + within
    polar, azimuth = angles_ref[0:1, :], angles_ref[1:2, :]
    across = jnp.sin(polar)
    fields = [
        within[0:1],
        seconds[1:2],
        across * jnp.cos(azimuth),
        across * jnp.sin(azimuth),
        jnp.cos(polar),
        gap_ref[...].reshape(1, CONT_DEV),
    ]
    line = jnp.concatenate(fields + [jnp.zeros((1, 64), F32)], axis=1)
    own_line[...] = jnp.where(lax.broadcasted_iota(jnp.int32, (8, NODES), 0) == n, line, 0.0)

    def line_copy(step):
        return pltpu.make_async_remote_copy(
            src_ref=own_line,
            dst_ref=lines_in.at[step],
            send_sem=line_send.at[step],
            recv_sem=line_recv.at[step],
            device_id=(w, lax.rem(n + step, narrow_count)),
            device_id_type=MESH,
        )

    def column_copy(step):
        return pltpu.make_async_remote_copy(
            src_ref=column_out,
            dst_ref=column_in.at[w],
            send_sem=column_send.at[step],
            recv_sem=column_recv.at[step],
            device_id=(lax.rem(w + step, wide_count), n),
            device_id_type=MESH,
        )

    for step in range(1, narrow_count):
        line_copy(step).start()
    near_field(
        (wide_count, narrow_count), list_ref, meta_ref, held_ref, off_ref, near_ref, offcol, source, columns
    )
    load.wait()
    t_yf[...] = jnp.zeros_like(t_yf)
    for part in (0, 1):
        for piece in range(8):
            for c in range(3):
                t_yf[part, piece * 128 + c * 32 : piece * 128 + c * 32 + 32, c * 256 : c * 256 + 256] = t_x[
                    4 + part, piece * 32 : piece * 32 + 32, :
                ]
        for piece in range(8):
            for c in range(3):
                block = t_yf[part, piece * 128 : piece * 128 + 128, c * 256 : c * 256 + 256]
                t_yi[part, c * 256 : c * 256 + 256, piece * 128 : piece * 128 + 128] = jnp.transpose(
                    block.astype(F32)
                ).astype(BF16)
    for half in (0, 1):
        wide_go[half].arrive()
        block = split(wide_in[:, half].reshape(GRID, 384))
        along = dot3((t_x[0], t_x[1]), block)
        narrow_out[:, half] = along.reshape(narrow_count, 32, 384)
        narrow_go[half].begin()
    column = own_line[...]
    for step in range(1, narrow_count):
        line_copy(step).wait_recv()
        column = column + lines_in[step]
    column_out[...] = column
    column_in[w] = column

    def begin_column(step, carry):
        column_copy(step).start()
        return carry

    lax.fori_loop(1, wide_count, begin_column, 0)
    row = lax.broadcasted_iota(jnp.int32, (32, 1), 0)
    k_x = (n * 16 + row % 16).astype(F32)
    nyquist_x = jnp.where((row >= 16) & (k_x < 0.5), 128.0, 0.0)
    lane = lax.broadcasted_iota(jnp.int32, (1, GRID), 1)
    k_y = (lane % 128).astype(F32)
    nyquist_y = jnp.where((lane >= 128) & (k_y < 0.5), 128.0, 0.0)
    square_xy = k_x * k_x + nyquist_x * nyquist_x + (k_y * k_y + nyquist_y * nyquist_y)
    scale_x = jnp.where(k_x < 0.5, 1.0, 2.0)
    scale_y = jnp.where(k_y < 0.5, 1.0, 2.0)
    scale_xy = scale_x * scale_y
    damping = (ewald_split * np.pi / GRID) ** 2
    constant = GRID * GRID / (4.0 * np.pi * np.pi) / float(GRID) ** 3
    turn_x = jnp.where(row < 16, k_x, -k_x)
    turn_y = jnp.where(lane < 128, k_y, -k_y)

    def derive_x(values):
        return turn_x * jnp.concatenate([values[16:], values[:16]], axis=0)

    def derive_y(values):
        return turn_y * jnp.concatenate([values[:, 128:], values[:, :128]], axis=1)

    def filtered(index, group):
        k_z = (w * 4 + group * 2 + index).astype(F32)
        bases = [pl.multiple_of(group * 128 + half * 64 + index * 32, 32) for half in (0, 1)]
        fields = [
            [spectrum[pl.ds(bases[half], 32), c * 256 : c * 256 + 256] for c in range(3)]
            for half in (0, 1)
        ]
        flows = []
        nyquists_z = [jnp.zeros_like(k_z), jnp.where(k_z < 0.5, 128.0, 0.0)]
        scale_z = jnp.where(k_z < 0.5, 1.0, 2.0)
        turn_z = (k_z, -k_z)
        for half in (0, 1):
            values = fields[half]
            flows.append(derive_x(values[0]) + derive_y(values[1]) + turn_z[half] * fields[1 - half][2])
        for half in (0, 1):
            values = fields[half]
            nyquist_z = nyquists_z[half]
            square = square_xy + (k_z * k_z + nyquist_z * nyquist_z)
            safe = jnp.maximum(square, 1.0)
            inverse = 1.0 / safe
            factor = jnp.where(square > 0.5, jnp.exp(-damping * square) * inverse, 0.0)
            factor = factor * (scale_xy * (scale_z * constant))
            edge = (nyquist_x * values[0] + nyquist_y * values[1] + nyquist_z * values[2]) * inverse
            flow = [flows[half] * inverse, flows[1 - half] * inverse]
            gradient = [derive_x(flow[0]), derive_y(flow[0]), None]
            gradient[2] = turn_z[half] * (flows[1 - half] * inverse)
            nyquist = (nyquist_x, nyquist_y, nyquist_z)
            for c in range(3):
                spectrum[pl.ds(bases[half], 32), c * 256 : c * 256 + 256] = factor * (
                    values[c] + gradient[c] - nyquist[c] * edge
                )
        return group

    for half in (0, 1):
        narrow_go[half].arrive()
        for piece in range(8):
            groups = [narrow_in[piece, half, :, g * 128 : g * 128 + 128] for g in range(3)]
            unpacked = unpack_lanes(*groups)
            for j in range(4):
                lines[half * 128 + j * 32 : half * 128 + j * 32 + 32, piece * 128 : piece * 128 + 128] = unpacked[j]
        rows = slice(half * 128, half * 128 + 128)
        spectrum[rows, :] = dot3(split(lines[rows, :]), (t_yf[0], t_yf[1]))
        lax.fori_loop(0, 2, filtered, half)
        lines[rows, :] = dot3(split(spectrum[rows, :]), (t_yi[0], t_yi[1]))
        for target in range(8):
            groups = [
                lines[half * 128 + j * 32 : half * 128 + j * 32 + 32, target * 128 : target * 128 + 128]
                for j in range(4)
            ]
            packed = pack_lanes(*groups)
            for g in range(3):
                narrow_back[target, half, :, g * 128 : g * 128 + 128] = packed[g]
        narrow_return[half].begin()
    for half in (0, 1):
        narrow_return[half].arrive()
        block = split(narrow_home[:, half].reshape(GRID, 384))
        along = dot3((t_x[2], t_x[3]), block)
        wide_back[:, half] = along.reshape(wide_count, 8, 384)
        wide_return[half].begin()
    def end_column(step, carry):
        column_copy(step).wait()
        return carry

    lax.fori_loop(1, wide_count, end_column, 0)
    for step in range(1, narrow_count):
        line_copy(step).wait_send()
    contacts_ref[...] = column_in[...].reshape(wide_count * narrow_count, NODES)
    for group in (wide_go, narrow_go, narrow_return):
        for half in (0, 1):
            group[half].sent()
    for half in (0, 1):
        wide_return[half].arrive()
        out_ref[:, half] = wide_home[:, half]
    for half in (0, 1):
        wide_return[half].sent()


AROUND = [(dw, dn) for dw in (-1, 0, 1) for dn in (-1, 0, 1)]
PARTIAL = [(dw, dn) for dw in (-2, -1, 0) for dn in (-1, 0)]


def shift_narrow(values, dn, narrow_count):
    if dn == 0:
        return values
    place = lanes_of(values.shape) % narrow_count
    edge = 0 if dn == 1 else narrow_count - 1
    total = values.shape[-1]
    return jnp.where(
        place == edge,
        roll(values, (dn - dn * narrow_count) % total),
        roll(values, dn % total),
    )


def shift_wide(values, dw, narrow_count):
    if dw == 0:
        return values
    return roll(values, (dw * narrow_count) % values.shape[-1])


def contact_kernel(
    wide_count,
    narrow_count,
    meta_ref,
    cells_ref,
    off_ref,
    tz_ref,
    mesh_ref,
    near_ref,
    static_ref,
    centre_ref,
    velocity_ref,
    force_ref,
    moved_ref,
    offcol,
    m_high,
    m_low,
    h_high,
    h_low,
    turned,
    part_ref,
    part_in,
    tile_out,
    tile_in,
    table_out,
    table_in,
    edges,
    around,
    loads,
    part_send,
    part_recv,
    narrow_send,
    narrow_recv,
    wide_send,
    wide_recv,
):
    w, n = lax.axis_index("wide"), lax.axis_index("narrow")
    devices = wide_count * narrow_count

    def device(dw, dn):
        return (
            lax.rem(w + dw + wide_count, wide_count),
            lax.rem(n + dn + narrow_count, narrow_count),
        )

    reach = (
        [(step, 0) for step in range(1, wide_count)]
        + [(0, step) for step in range(1, narrow_count)]
        + [(-2, -1), (-1, -1), (2, 1), (1, 1)]
    )
    sizes = (wide_count, narrow_count)
    hail(*sizes, reach)
    columns_of(off_ref, offcol)
    interpolate(
        sizes, meta_ref, cells_ref, off_ref, tz_ref, mesh_ref, part_ref, offcol, m_high, m_low, h_high, h_low, turned
    )
    hear(reach)
    own = PARTIAL.index((0, 0))
    pieces = [part_ref[p] + near_ref[...] if p == own else part_ref[p] for p in range(6)]
    means = [jnp.sum(piece, axis=1, keepdims=True) * (1.0 / NODES) for piece in pieces]
    column = jnp.concatenate(means + [jnp.zeros((32, 1), F32)], axis=0)
    line = jnp.transpose(jnp.broadcast_to(column, (128, 128)))[:8]
    tile_out[...] = jnp.where(lax.broadcasted_iota(jnp.int32, (8, 128), 0) == n, line, 0.0)

    def narrow_copy(step):
        to = lax.rem(n + step, narrow_count)
        return pltpu.make_async_remote_copy(
            src_ref=tile_out,
            dst_ref=tile_in.at[step],
            send_sem=narrow_send.at[step],
            recv_sem=narrow_recv.at[step],
            device_id=(w, to),
            device_id_type=MESH,
        )

    def wide_copy(step):
        to = lax.rem(w + step, wide_count)
        return pltpu.make_async_remote_copy(
            src_ref=table_out,
            dst_ref=table_in.at[w],
            send_sem=wide_send.at[step],
            recv_sem=wide_recv.at[step],
            device_id=(to, n),
            device_id_type=MESH,
        )

    for step in range(1, narrow_count):
        narrow_copy(step).start()
    copies = []
    for place, (dw, dn) in enumerate(PARTIAL):
        if (dw, dn) == (0, 0):
            continue
        copy = pltpu.make_async_remote_copy(
            src_ref=part_ref.at[place],
            dst_ref=part_in.at[place],
            send_sem=part_send.at[place],
            recv_sem=part_recv.at[place],
            device_id=device(dw, dn),
            device_id_type=MESH,
        )
        copy.start()
        copies.append((place, copy))
    tile = tile_out[...]
    for step in range(1, narrow_count):
        narrow_copy(step).wait_recv()
        tile = tile + tile_in[step]
    table_out[...] = tile
    table_in[w] = tile

    def begin(step, carry):
        wide_copy(step).start()
        return carry

    lax.fori_loop(1, wide_count, begin, 0)

    fields = jnp.transpose(static_ref[...])
    first, second, gap = fields[0:32], fields[32:64], fields[160:192]
    normal = [fields[64 + 32 * c : 96 + 32 * c] for c in range(3)]
    for place in range(9):
        for s in range(SLOTS_DEV):
            mark = jnp.where(second == float(place * SLOTS_DEV + s), -1.0, 0.0)
            if place == 4:
                mark = mark + jnp.where(first == float(s), 1.0, 0.0)
            for c in range(3):
                edges[place, 3 * s + c] = mark * normal[c]

    velocity = pieces[own]
    for place, copy in copies:
        copy.wait_recv()
        velocity = velocity + part_in[place]
    velocity_ref[...] = velocity

    def end(step, carry):
        wide_copy(step).wait_recv()
        return carry

    lax.fori_loop(1, wide_count, end, 0)
    spread_means = jnp.transpose(table_in[...].reshape(devices, 128))
    hydro = jnp.zeros((16, devices), F32)
    for p, (dw, dn) in enumerate(PARTIAL):
        moved_means = shift_wide(spread_means[p * 16 : p * 16 + 16], dw, narrow_count)
        hydro = hydro + shift_narrow(moved_means, dn, narrow_count)

    def totals(force):
        def one_place(place, carry):
            for k in range(ROWS_DEV):
                loads[place, k : k + 1, :] = jnp.sum(edges[place, k] * force, axis=0, keepdims=True)
            return carry

        lax.fori_loop(0, 9, one_place, 0)
        result = jnp.zeros((16, devices), F32)
        for dn in (-1, 0, 1):
            inner = jnp.zeros((16, devices), F32)
            for dw in (-1, 0, 1):
                inner = inner + shift_wide(loads[AROUND.index((dw, dn))], dw, narrow_count)
            result = result + shift_narrow(inner, dn, narrow_count)
        return result

    def sweep(turn, carry):
        force, moving = carry
        for dn in (-1, 0, 1):
            beside = shift_narrow(moving, -dn, narrow_count)
            for dw in (-1, 0, 1):
                around[AROUND.index((dw, dn))] = shift_wide(beside, -dw, narrow_count)

        def one_place(place, relative):
            for k in range(ROWS_DEV):
                relative = relative + edges[place, k] * around[place, k : k + 1, :]
            return relative

        relative = lax.fori_loop(0, 9, one_place, jnp.zeros((CONT_DEV, devices), F32))
        force = jnp.maximum(
            force - relaxation * (gap + time_step * relative) / (2.0 * time_step * mobility), 0.0
        )
        return force, hydro + mobility * totals(force)

    loads[...] = jnp.zeros_like(loads)
    force, moving = lax.fori_loop(
        0, SWEEPS, sweep, (jnp.zeros((CONT_DEV, devices), F32), hydro)
    )
    mine = lanes_of((1, devices)) == w * narrow_count + n
    own_force = jnp.sum(jnp.where(mine, force, 0.0), axis=1, keepdims=True)
    force_ref[...] = jnp.broadcast_to(own_force, (CONT_DEV, 128))
    own_moving = jnp.sum(jnp.where(mine, moving, 0.0), axis=1, keepdims=True)
    moved_ref[...] = centre_ref[...] + time_step * own_moving
    for place, copy in copies:
        copy.wait_send()
    for step in range(1, narrow_count):
        narrow_copy(step).wait_send()

    def finish(step, carry):
        wide_copy(step).wait_send()
        return carry

    lax.fori_loop(1, wide_count, finish, 0)


def local(
    wide_count,
    narrow_count,
    tractions,
    centers,
    node_offsets,
    occupied,
    anchors,
    near_list,
    contact_pairs,
    contact_gap,
    contact_angles,
):
    w, n = lax.axis_index("wide"), lax.axis_index("narrow")
    sizes = (wide_count, narrow_count)
    shape = jax.ShapeDtypeStruct
    dma = pltpu.SemaphoreType.DMA

    held, metas, cells = pl.pallas_call(
        functools.partial(gather_kernel, *sizes),
        out_shape=(shape((12, 16, NODES), F32), shape((12, 128), F32), shape((12, 128), jnp.int32)),
        in_specs=[VMEM_SPEC, SMEM_SPEC, SMEM_SPEC, SMEM_SPEC],
        out_specs=(VMEM_SPEC,) * 3,
        scratch_shapes=[
            pltpu.VMEM((16, NODES), F32),
            pltpu.VMEM((12, 16, NODES), F32),
            dma((12,)),
            dma((12,)),
        ],
        compiler_params=params(0),
        name="gather",
    )(tractions, centers, anchors, occupied)

    table_z = trig_table(2)
    wrapped_z = np.concatenate([table_z, table_z[:, :32]], axis=1).T.astype(np.float32).reshape(36, 8, GRID)
    table_x = trig_table(16)
    table_y = trig_table(128)
    turned_x = np.ascontiguousarray(table_x.T)
    turned_y = np.ascontiguousarray(table_y.T)
    tables = np.stack([*halves(table_x), *halves(turned_x), *halves(turned_y)])
    mesh, near, contacts = pl.pallas_call(
        functools.partial(transform_kernel, *sizes),
        out_shape=(
            shape((32, 2, 8, 384), F32),
            shape((16, NODES), F32),
            shape((wide_count * narrow_count, NODES), F32),
        ),
        in_specs=[SMEM_SPEC] * 3 + [VMEM_SPEC] * 6 + [HBM_SPEC],
        out_specs=(VMEM_SPEC,) * 3,
        scratch_shapes=[
            pltpu.VMEM((2, 768, NODES), BF16),
            pltpu.VMEM((2, 768, NODES), BF16),
            pltpu.VMEM((768, GRID), F32),
            pltpu.VMEM((GRID * 8, 128), F32),
            pltpu.VMEM((32, 2, 8, 384), F32),
            pltpu.VMEM((32, 2, 8, 384), F32),
            pltpu.VMEM((8, 2, 32, 384), F32),
            pltpu.VMEM((8, 2, 32, 384), F32),
            pltpu.VMEM((8, 2, 32, 384), F32),
            pltpu.VMEM((8, 2, 32, 384), F32),
            pltpu.VMEM((32, 2, 8, 384), F32),
            pltpu.VMEM((32, 2, 8, 384), F32),
            pltpu.VMEM((256, 1024), F32),
            pltpu.VMEM((256, 768), F32),
            pltpu.VMEM((6, 256, 256), BF16),
            pltpu.VMEM((2, 1024, 768), BF16),
            pltpu.VMEM((2, 768, 1024), BF16),
            pltpu.VMEM((3, NODES, 128), F32),
            pltpu.VMEM((3, 8, NODES), F32),
            pltpu.VMEM((NODES, 8), F32),
            pltpu.VMEM((8, NODES), F32),
            pltpu.VMEM((8, 8, NODES), F32),
            pltpu.VMEM((8, NODES), F32),
            pltpu.VMEM((32, 8, NODES), F32),
            dma((2, 2, 32)),
            dma((2, 2, 32)),
            dma((2, 2, 8)),
            dma((2, 2, 8)),
            dma,
            dma((8,)),
            dma((8,)),
            dma((32,)),
            dma((32,)),
        ],
        compiler_params=params(1),
        name="transform",
    )(
        near_list.reshape(4, NEAR),
        metas,
        cells,
        held,
        node_offsets,
        wrapped_z,
        contact_pairs,
        contact_gap,
        contact_angles,
        tables,
    )

    centre_rows = jnp.broadcast_to(jnp.pad(centers.reshape(12, 1), ((0, 4), (0, 0))), (16, 128))
    devices = wide_count * narrow_count
    velocity, force, moved = pl.pallas_call(
        functools.partial(contact_kernel, *sizes),
        out_shape=(shape((16, NODES), F32), shape((CONT_DEV, 128), F32), shape((16, 128), F32)),
        in_specs=[SMEM_SPEC] * 2 + [VMEM_SPEC] * 6,
        out_specs=(VMEM_SPEC,) * 3,
        scratch_shapes=[
            pltpu.VMEM((3, NODES, 128), F32),
            pltpu.VMEM((768, GRID), BF16),
            pltpu.VMEM((768, GRID), BF16),
            pltpu.VMEM((384, GRID), BF16),
            pltpu.VMEM((384, GRID), BF16),
            pltpu.VMEM((GRID * 8, 128), F32),
            pltpu.VMEM((6, 16, NODES), F32),
            pltpu.VMEM((6, 16, NODES), F32),
            pltpu.VMEM((8, 128), F32),
            pltpu.VMEM((8, 8, 128), F32),
            pltpu.VMEM((8, 128), F32),
            pltpu.VMEM((32, 8, 128), F32),
            pltpu.VMEM((9, ROWS_DEV, CONT_DEV, devices), F32),
            pltpu.VMEM((9, 16, devices), F32),
            pltpu.VMEM((9, 16, devices), F32),
            dma((6,)),
            dma((6,)),
            dma((8,)),
            dma((8,)),
            dma((32,)),
            dma((32,)),
        ],
        compiler_params=params(2),
        name="contacts",
    )(metas, cells, node_offsets, wrapped_z, mesh, near, contacts, centre_rows)
    return (
        velocity[:12].reshape(2, 2, 3, NODES),
        force[:, 0],
        moved[:12, 0].reshape(2, 2, 3),
    )


def solution(mesh):
    placed = (
        P("wide", "narrow", None, None),
        P("wide", "narrow", None),
        P(),
        P("wide", "narrow"),
        P("wide", "narrow", None),
        P("wide", "narrow", None),
        P(None, ("wide", "narrow")),
        P(("wide", "narrow")),
        P(None, ("wide", "narrow")),
    )
    return jax.shard_map(
        functools.partial(local, mesh.shape["wide"], mesh.shape["narrow"]),
        mesh=mesh,
        in_specs=placed,
        out_specs=(
            P("wide", "narrow", None, None),
            P(("wide", "narrow")),
            P("wide", "narrow", None),
        ),
        check_vma=False,
    )
```

```python
import functools

import jax
import jax.numpy as jnp
import ml_dtypes
import numpy as np
from jax import lax
from jax.experimental import pallas as pl
from jax.experimental.pallas import tpu as pltpu
from jax.sharding import PartitionSpec as P

NODES = 256
GRID = 256
BLOCK = 16
NEAR = 2
SWEEPS = 6
SLOTS_DEV = 4
ROWS_DEV = 3 * SLOTS_DEV
CONT_DEV = 32

soften = 1.0
screen = 0.0625
near_scale = 0.05
spread_norm = 0.17958712212516656
mobility = 0.2
time_step = 0.5
relaxation = 0.35
ewald_split = 0.5

MESH = pl.DeviceIdType.MESH
F32 = jnp.float32
BF16 = jnp.bfloat16
VMEM_SPEC = pl.BlockSpec(memory_space=pltpu.VMEM)
HBM_SPEC = pl.BlockSpec(memory_space=pltpu.HBM)
SMEM_SPEC = pl.BlockSpec(memory_space=pltpu.SMEM)


def params(collective_id=None, limit=40):
    if collective_id is None:
        return pltpu.CompilerParams(vmem_limit_bytes=limit * 2**20)
    return pltpu.CompilerParams(
        vmem_limit_bytes=limit * 2**20, collective_id=collective_id, has_side_effects=True
    )


def trig_table(group):
    cell = np.arange(GRID)
    rows = []
    for first in range(0, GRID // 2, group):
        for half in (0, 1):
            for k in range(first, first + group):
                angle = 2.0 * np.pi / GRID * (k * cell % GRID)
                if half == 0:
                    rows.append(np.cos(angle))
                elif k == 0:
                    rows.append(np.cos(np.pi * cell))
                else:
                    rows.append(np.sin(angle))
    return np.stack(rows)


def halves(table):
    high = table.astype(np.float32).astype(ml_dtypes.bfloat16)
    low = (table - high.astype(np.float64)).astype(np.float32).astype(ml_dtypes.bfloat16)
    return high, low


def split(values):
    high = values.astype(BF16)
    return high, (values - high.astype(F32)).astype(BF16)


def dot(a, b, contract=((1,), (0,))):
    return lax.dot_general(a, b, (contract, ((), ())), preferred_element_type=F32)


def dot3(a, b):
    return dot(
        jnp.concatenate([a[0], a[0], a[1]], axis=1), jnp.concatenate([b[0], b[1], b[0]], axis=0)
    )


def lanes_of(shape):
    return lax.broadcasted_iota(jnp.int32, shape, len(shape) - 1)


def roll(values, shift):
    return pltpu.roll(values, shift, len(values.shape) - 1)


def pack_lanes(u0, u1, u2, u3):
    lane = lanes_of(u0.shape)
    r1, r2, r3 = roll(u1, 96), roll(u2, 64), roll(u3, 32)
    return (
        jnp.where(lane < 96, u0, r1),
        jnp.where(lane < 64, r1, r2),
        jnp.where(lane < 32, r2, r3),
    )


def unpack_lanes(p0, p1, p2):
    lane = lanes_of(p0.shape)
    return (
        p0,
        roll(jnp.where(lane < 64, p1, p0), 32),
        roll(jnp.where(lane < 32, p2, p1), 64),
        roll(p2, 96),
    )


def hail(wide_count, narrow_count, offsets):
    w, n = lax.axis_index("wide"), lax.axis_index("narrow")
    for dw, dn in offsets:
        pl.semaphore_signal(
            pltpu.get_barrier_semaphore(),
            inc=1,
            device_id=(
                lax.rem(w + dw + wide_count, wide_count),
                lax.rem(n + dn + narrow_count, narrow_count),
            ),
            device_id_type=MESH,
        )


def hear(offsets):
    pl.semaphore_wait(pltpu.get_barrier_semaphore(), len(offsets))


GATHER = [(dw, dn) for dw in (-2, -1, 0, 1) for dn in (-1, 0, 1)]


def gather_kernel(
    wide_count,
    narrow_count,
    tractions_ref,
    centres_ref,
    anchors_ref,
    occupied_ref,
    out_ref,
    meta_ref,
    cells_ref,
    own_ref,
    held,
    send_sem,
    recv_sem,
):
    w, n = lax.axis_index("wide"), lax.axis_index("narrow")
    reach = [(dw, dn) for dw in (-2, -1, 0, 1, 2) for dn in (-1, 0, 1) if (dw, dn) != (0, 0)]
    hail(wide_count, narrow_count, reach)
    slots = [(a, b) for a in (0, 1) for b in (0, 1)]
    numbers = [centres_ref[a, b, c] for a, b in slots for c in range(3)]
    numbers += [anchors_ref[a, b, c].astype(F32) for a, b in slots for c in range(3)]
    numbers += [occupied_ref[a, b].astype(F32) for a, b in slots]
    lane = lanes_of((1, NODES))
    line = jnp.zeros((1, NODES), F32)
    for place, number in enumerate(numbers):
        line = jnp.where(lane == place, number, line)
    for s, (a, b) in enumerate(slots):
        own_ref[3 * s : 3 * s + 3, :] = tractions_ref[a, b]
    own_ref[12:16, :] = jnp.broadcast_to(line, (4, NODES))
    hear(reach)
    copies = []
    for place, (dw, dn) in enumerate(GATHER):
        if (dw, dn) == (0, 0):
            continue
        copy = pltpu.make_async_remote_copy(
            src_ref=own_ref,
            dst_ref=held.at[place],
            send_sem=send_sem.at[place],
            recv_sem=recv_sem.at[place],
            device_id=(
                lax.rem(w - dw + wide_count, wide_count),
                lax.rem(n - dn + narrow_count, narrow_count),
            ),
            device_id_type=MESH,
        )
        copy.start()
        copies.append((place, copy))
    own = GATHER.index((0, 0))
    out_ref[own] = own_ref[...]
    meta_ref[own : own + 1, :] = own_ref[12:13, 0:128]
    cells_ref[own : own + 1, :] = own_ref[12:13, 0:128].astype(jnp.int32)
    for place, copy in copies:
        copy.wait_recv()
        out_ref[place] = held[place]
        meta_ref[place : place + 1, :] = held[place, 12:13, 0:128]
        cells_ref[place : place + 1, :] = held[place, 12:13, 0:128].astype(jnp.int32)
    for place, copy in copies:
        copy.wait_send()


def near_field(sizes, list_ref, meta_ref, held_ref, off_ref, out_ref, offcol, source, columns):
    wide_count, narrow_count = sizes
    w, n = lax.axis_index("wide"), lax.axis_index("narrow")
    own = GATHER.index((0, 0))
    out_ref[...] = jnp.zeros_like(out_ref)
    columns[...] = jnp.zeros_like(columns)
    for s in range(SLOTS_DEV):
        for j in range(1 + NEAR):
            if j == 0:
                place, within = own, s
            else:
                entry = list_ref[s, j - 1]
                holder = entry // SLOTS_DEV
                within = entry % SLOTS_DEV
                row = lax.rem(holder // narrow_count - w + 1 + wide_count, wide_count)
                column = lax.rem(lax.rem(holder, narrow_count) - n + 1 + narrow_count, narrow_count)
                place = (jnp.minimum(row, 2) + 1) * 3 + jnp.minimum(column, 2)
            for c in range(3):
                if j == 0:
                    shift = 0.0
                else:
                    e = meta_ref[own, 3 * s + c] - meta_ref[place, 3 * within + c]
                    shift = e - jnp.where(e >= 128.0, 256.0, jnp.where(e < -128.0, -256.0, 0.0))
                source[j, c : c + 1, :] = shift - off_ref[c : c + 1, :]
                source[j, 3 + c : 4 + c, :] = held_ref[place, pl.ds(within * 3 + c, 1), :]

        def chunk(i, carry):
            for part in (0, 1):
                rows = pl.ds(pl.multiple_of(i * 16 + part * 8, 8), 8)
                sums = [jnp.zeros((8, 128), F32) for _ in range(3)]
                at = [offcol[c, rows, :] for c in range(3)]
                for j in range(1 + NEAR):
                    for half in (0, 1):
                        lanes = slice(half * 128, half * 128 + 128)
                        d = [at[c] + source[j, c : c + 1, lanes] for c in range(3)]
                        f = [source[j, 3 + c : 4 + c, lanes] for c in range(3)]
                        r2 = d[0] * d[0] + d[1] * d[1] + d[2] * d[2]
                        inverse = lax.rsqrt(r2 + soften)
                        weight = jnp.exp(r2 * (-screen)) * (inverse * inverse * inverse)
                        along = (d[0] * f[0] + d[1] * f[1] + d[2] * f[2]) * weight
                        diagonal = (r2 + 2.0 * soften) * weight
                        for c in range(3):
                            sums[c] = sums[c] + (diagonal * f[c] + d[c] * along)
                for c in range(3):
                    columns[rows, c : c + 1] = jnp.sum(sums[c], axis=1, keepdims=True)
            return carry

        lax.fori_loop(0, NODES // 16, chunk, 0)
        result = jnp.transpose(columns[...])
        alive = jnp.where(meta_ref[own, 24 + s] > 0.5, near_scale, 0.0)
        out_ref[3 * s : 3 * s + 3, :] = alive * result[0:3, :]


def columns_of(off_ref, offcol):
    padded = jnp.concatenate([off_ref[...], jnp.zeros((5, NODES), F32)], axis=0)
    turned = jnp.transpose(padded)
    for c in range(3):
        offcol[c] = jnp.broadcast_to(turned[:, c : c + 1], (NODES, 128))


def sphere_weights(sizes, dw, dn, s, meta_ref, cells_ref, off_ref, offcol, tz_ref):
    wide_count, narrow_count = sizes
    w, n = lax.axis_index("wide"), lax.axis_index("narrow")
    size_x, size_y = GRID // wide_count, GRID // narrow_count
    place = (dw + 2) * 3 + dn + 1
    anchor = [cells_ref[place, 12 + 3 * s + c] for c in range(3)]
    centre = [meta_ref[place, 3 * s + c] for c in range(3)]
    alive = jnp.where(meta_ref[place, 24 + s] > 0.5, spread_norm, 0.0)
    low_x = anchor[0] - size_x * lax.rem(w + dw + wide_count, wide_count) + size_x * dw
    low_y = anchor[1] - size_y * lax.rem(n + dn + narrow_count, narrow_count) + size_y * dn
    low_z = anchor[2] % 8

    def weights(cell, position, base, low, factor):
        distance = position - (base + cell).astype(F32)
        inside = (cell >= low) & (cell < low + BLOCK)
        return jnp.where(inside, jnp.exp(-distance * distance) * factor, 0.0)

    def rows(c, low, count, factor):
        cell = lax.broadcasted_iota(jnp.int32, (count, NODES), 0)
        return weights(cell, centre[c] + off_ref[c : c + 1, :], anchor[c] - low, low, factor)

    lane = lanes_of((NODES, 128))
    wz = weights(lane % 32, centre[2] + offcol[2], anchor[2] - low_z, low_z, 1.0)
    high = wz.astype(BF16).astype(F32)
    left = jnp.where(lane < 64, high, jnp.where(lane < 96, wz - high, 0.0)).astype(BF16)
    tile = anchor[2] // 8
    t_high, t_low = split(jnp.concatenate([tz_ref[tile + t] for t in range(4)], axis=0))
    right = jnp.concatenate([t_high, t_low, t_high, jnp.zeros((32, GRID), BF16)], axis=0)
    along_z = split(dot(left, right))
    return place, rows(0, low_x, size_x, alive), rows(1, low_y, 16 if dn else size_y, 1.0), along_z


def pair_loop(body, dn, unroll=1):
    def step(index, carry):
        body(index // 2 - 2, dn, index % 2)
        return carry

    lax.fori_loop(0, 6, step, 0, unroll=unroll)


def spread(sizes, meta_ref, cells_ref, held_ref, off_ref, tz_ref, out_ref, offcol, a_high, a_low, total, turned):
    total[...] = jnp.zeros_like(total)

    def pair(dw, dn, which):
        span = 16 if dn else 32
        sums = []
        for member in (0, 1):
            s = 2 * which + member
            place, wx, wy, along_z = sphere_weights(sizes, dw, dn, s, meta_ref, cells_ref, off_ref, offcol, tz_ref)
            planar = jnp.concatenate(
                [wy * held_ref[place, pl.ds(s * 3 + c, 1), :] for c in range(3)], axis=0
            )
            size = 3 * span
            for x in range(8):
                high, low = split(planar * wx[x : x + 1, :])
                a_high[member, x * size : x * size + size, :] = high
                a_low[member, x * size : x * size + size, :] = low
            rows = slice(0, 8 * size)
            sums.append(dot3((a_high[member, rows, :], a_low[member, rows, :]), along_z))
        both = sums[0] + sums[1]
        if dn == 0:
            total[...] += both
        else:
            for block in range(24):
                total[block * 32 : block * 32 + 16, :] += both[block * 16 : block * 16 + 16]

    pair_loop(pair, -1)
    pair_loop(pair, 0)
    for x in range(8):
        block = jnp.concatenate([total[x * 96 : x * 96 + 96, :], jnp.zeros((32, GRID), F32)], axis=0)
        turned[pl.ds(x, GRID, stride=8), :] = jnp.transpose(block)
    values = turned[...].reshape(64, 4, 8, 128)
    packed = pack_lanes(*[values[:, j] for j in range(4)])
    for g in range(3):
        out_ref[:, :, :, g * 128 : g * 128 + 128] = packed[g].reshape(32, 2, 8, 128)


def mean_weights(sizes, meta_ref, cells_ref, off_ref, tz_ref, offcol, full, half):
    def pair(dw, dn, which):
        span = 16 if dn else 32
        for member in (0, 1):
            s = 2 * which + member
            place, wx, wy, along_z = sphere_weights(
                sizes, dw, dn, s, meta_ref, cells_ref, off_ref, offcol, tz_ref
            )
            wy = wy * (1.0 / NODES)
            left = split(jnp.concatenate([wy * wx[x : x + 1, :] for x in range(8)], axis=0))
            target = half if dn else full
            target[(dw + 2) * 4 + s] = dot3(left, along_z)

    pair_loop(pair, -1)
    pair_loop(pair, 0)


def mean_velocities(values, full, half, rows_ref):
    rows_ref[...] = jnp.zeros_like(rows_ref)
    for dn in (-1, 0):
        span = 16 if dn else 32

        def sphere(index, carry):
            source = half if dn else full
            tiles = [jnp.zeros((8, GRID), F32) for _ in range(3)]
            for x in range(8):
                for y in range(0, span, 8):
                    weight = source[index, x * span + y : x * span + y + 8, :]
                    for c in range(3):
                        at = x * 96 + c * 32 + y
                        tiles[c] = tiles[c] + values[at : at + 8, :] * weight
            piece = (index // 4) * 2 + dn + 1
            for c in range(3):
                rows_ref[piece, pl.ds((index % 4) * 3 + c, 1), :] = jnp.sum(tiles[c], axis=0, keepdims=True)
            return carry

        lax.fori_loop(0, 12, sphere, 0)


def unpack_mesh(mesh_ref, values, m_high, m_low, h_high, h_low, turned):
    groups = [mesh_ref[:, :, :, g * 128 : g * 128 + 128].reshape(64, 8, 128) for g in range(3)]
    unpacked = unpack_lanes(*groups)
    turned[...] = jnp.stack(unpacked, axis=1).reshape(GRID * 8, 128)
    for x in range(8):
        block = jnp.transpose(turned[pl.ds(x, GRID, stride=8), :])[:96]
        values[x * 96 : x * 96 + 96, :] = block
        high, low = split(block)
        m_high[x * 96 : x * 96 + 96, :] = high
        m_low[x * 96 : x * 96 + 96, :] = low
        for c in range(3):
            target = slice(x * 48 + c * 16, x * 48 + c * 16 + 16)
            h_high[target, :] = high[c * 32 : c * 32 + 16]
            h_low[target, :] = low[c * 32 : c * 32 + 16]


def interpolate(
    sizes, lower, meta_ref, cells_ref, off_ref, tz_ref, out_ref, offcol, m_high, m_low, h_high, h_low
):
    def pair(dw, dn, which):
        span = 16 if dn else 32
        size = 3 * span
        for member in (0, 1):
            s = 2 * which + member
            place, wx, wy, along_z = sphere_weights(sizes, dw, dn, s, meta_ref, cells_ref, off_ref, offcol, tz_ref)
            left = (h_high[...], h_low[...]) if dn else (m_high[...], m_low[...])
            turn = ((1,), (1,))
            found = dot(
                jnp.concatenate([left[0], left[0], left[1]], axis=1),
                jnp.concatenate([along_z[0], along_z[1], along_z[0]], axis=1),
                turn,
            )
            summed = found[0:size] * wx[0:1, :]
            for x in range(1, 8):
                summed = summed + found[x * size : x * size + size] * wx[x : x + 1, :]
            owner = (dw + 2) * 2 + dn + 1
            for c in range(3):
                out_ref[owner, pl.ds(s * 3 + c, 1), :] = jnp.sum(
                    summed[c * span : c * span + span] * wy, axis=0, keepdims=True
                )

    pair_loop(pair, lower, 2)


AROUND = [(dw, dn) for dw in (-1, 0, 1) for dn in (-1, 0, 1)]
PARTIAL = [(dw, dn) for dw in (-2, -1, 0) for dn in (-1, 0)]


def shift_narrow(values, dn, narrow_count):
    if dn == 0:
        return values
    place = lanes_of(values.shape) % narrow_count
    edge = 0 if dn == 1 else narrow_count - 1
    total = values.shape[-1]
    return jnp.where(
        place == edge,
        roll(values, (dn - dn * narrow_count) % total),
        roll(values, dn % total),
    )


def shift_wide(values, dw, narrow_count):
    if dw == 0:
        return values
    return roll(values, (dw * narrow_count) % values.shape[-1])


class Exchange:
    def __init__(self, axis, count, source, target, half, send_sem, recv_sem, me, other):
        self.__dict__.update(locals())

    def copy_to(self, step):
        to = lax.rem(self.me + step, self.count)
        return pltpu.make_async_remote_copy(
            src_ref=self.source.at[to, self.half],
            dst_ref=self.target.at[self.me, self.half],
            send_sem=self.send_sem.at[step],
            recv_sem=self.recv_sem.at[step],
            device_id=(to, self.other) if self.axis == "wide" else (self.other, to),
            device_id_type=MESH,
        )

    def begin(self):
        def step(index, carry):
            self.copy_to(index).start()
            return carry

        lax.fori_loop(1, self.count, step, 0)
        self.target[self.me, self.half] = self.source[self.me, self.half]

    def arrive(self):
        def step(index, carry):
            self.copy_to(index).wait_recv()
            return carry

        lax.fori_loop(1, self.count, step, 0)

    def sent(self):
        def step(index, carry):
            self.copy_to(index).wait_send()
            return carry

        lax.fori_loop(1, self.count, step, 0)


def flow_kernel(
    wide_count,
    narrow_count,
    list_ref,
    meta_ref,
    cells_ref,
    held_ref,
    off_ref,
    tz_ref,
    pairs_ref,
    gap_ref,
    angles_ref,
    tables,
    velocity_ref,
    force_ref,
    moved_ref,
    near_ref,
    m_high,
    m_low,
    h_high,
    h_low,
    full_means,
    half_means,
    mean_rows,
    part_ref,
    part_in,
    tile_out,
    tile_in,
    table_out,
    table_in,
    edges,
    around,
    loads,
    part_send,
    part_recv,
    tile_send,
    tile_recv,
    spread_send,
    spread_recv,
    a_high,
    a_low,
    total,
    turned,
    mesh_ref,
    wide_in,
    narrow_out,
    narrow_in,
    narrow_back,
    narrow_home,
    wide_back,
    wide_home,
    lines,
    spectrum,
    t_x,
    t_yf,
    t_yi,
    offcol,
    source,
    columns,
    own_line,
    lines_in,
    column_out,
    column_in,
    wide_send,
    wide_recv,
    narrow_send,
    narrow_recv,
    table_sem,
    line_send,
    line_recv,
    column_send,
    column_recv,
):
    w, n = lax.axis_index("wide"), lax.axis_index("narrow")
    load = pltpu.make_async_copy(tables, t_x, table_sem)
    load.start()
    reach = (
        [(step, 0) for step in range(1, wide_count)]
        + [(0, step) for step in range(1, narrow_count)]
        + [(-2, -1), (-1, -1), (2, 1), (1, 1)]
    )
    sizes = (wide_count, narrow_count)
    hail(*sizes, reach)
    columns_of(off_ref, offcol)
    spread(sizes, meta_ref, cells_ref, held_ref, off_ref, tz_ref, mesh_ref, offcol, a_high, a_low, total, turned)
    hear(reach)

    def exchanges(axis, source, target, way):
        if axis == "wide":
            fixed = (wide_count, w, n, wide_send, wide_recv)
        else:
            fixed = (narrow_count, n, w, narrow_send, narrow_recv)
        count, me, other, send_sem, recv_sem = fixed
        return [
            Exchange(
                axis, count, source, target, half, send_sem.at[way, half], recv_sem.at[way, half], me, other
            )
            for half in (0, 1)
        ]

    wide_go = exchanges("wide", mesh_ref, wide_in, 0)
    narrow_go = exchanges("narrow", narrow_out, narrow_in, 0)
    narrow_return = exchanges("narrow", narrow_back, narrow_home, 1)
    wide_return = exchanges("wide", wide_back, wide_home, 1)
    for half in (0, 1):
        wide_go[half].begin()

    ids = pairs_ref[...]
    within = (ids % SLOTS_DEV).astype(F32)
    holder = ids // SLOTS_DEV
    row_w = lax.rem(holder // narrow_count - w + 1 + wide_count, wide_count)
    row_n = lax.rem(lax.rem(holder, narrow_count) - n + 1 + narrow_count, narrow_count)
    seconds = ((row_w * 3 + row_n) * SLOTS_DEV).astype(F32) + within
    polar, azimuth = angles_ref[0:1, :], angles_ref[1:2, :]
    across = jnp.sin(polar)
    fields = [
        within[0:1],
        seconds[1:2],
        across * jnp.cos(azimuth),
        across * jnp.sin(azimuth),
        jnp.cos(polar),
        gap_ref[...].reshape(1, CONT_DEV),
    ]
    line = jnp.concatenate(fields + [jnp.zeros((1, 64), F32)], axis=1)
    own_line[...] = jnp.where(lax.broadcasted_iota(jnp.int32, (8, NODES), 0) == n, line, 0.0)

    def line_copy(step):
        return pltpu.make_async_remote_copy(
            src_ref=own_line,
            dst_ref=lines_in.at[step],
            send_sem=line_send.at[step],
            recv_sem=line_recv.at[step],
            device_id=(w, lax.rem(n + step, narrow_count)),
            device_id_type=MESH,
        )

    def column_copy(step):
        return pltpu.make_async_remote_copy(
            src_ref=column_out,
            dst_ref=column_in.at[w],
            send_sem=column_send.at[step],
            recv_sem=column_recv.at[step],
            device_id=(lax.rem(w + step, wide_count), n),
            device_id_type=MESH,
        )

    for step in range(1, narrow_count):
        line_copy(step).start()
    near_field(
        (wide_count, narrow_count), list_ref, meta_ref, held_ref, off_ref, near_ref, offcol, source, columns
    )
    mean_weights(sizes, meta_ref, cells_ref, off_ref, tz_ref, offcol, full_means, half_means)
    load.wait()
    t_yf[...] = jnp.zeros_like(t_yf)
    for part in (0, 1):
        for piece in range(8):
            for c in range(3):
                t_yf[part, piece * 128 + c * 32 : piece * 128 + c * 32 + 32, c * 256 : c * 256 + 256] = t_x[
                    4 + part, piece * 32 : piece * 32 + 32, :
                ]
        for piece in range(8):
            for c in range(3):
                block = t_yf[part, piece * 128 : piece * 128 + 128, c * 256 : c * 256 + 256]
                t_yi[part, c * 256 : c * 256 + 256, piece * 128 : piece * 128 + 128] = jnp.transpose(
                    block.astype(F32)
                ).astype(BF16)
    for half in (0, 1):
        wide_go[half].arrive()
        block = split(wide_in[:, half].reshape(GRID, 384))
        along = dot3((t_x[0], t_x[1]), block)
        narrow_out[:, half] = along.reshape(narrow_count, 32, 384)
        narrow_go[half].begin()
    column = own_line[...]
    for step in range(1, narrow_count):
        line_copy(step).wait_recv()
        column = column + lines_in[step]
    column_out[...] = column
    column_in[w] = column

    def begin_column(step, carry):
        column_copy(step).start()
        return carry

    lax.fori_loop(1, wide_count, begin_column, 0)
    row = lax.broadcasted_iota(jnp.int32, (32, 1), 0)
    k_x = (n * 16 + row % 16).astype(F32)
    nyquist_x = jnp.where((row >= 16) & (k_x < 0.5), 128.0, 0.0)
    lane = lax.broadcasted_iota(jnp.int32, (1, GRID), 1)
    k_y = (lane % 128).astype(F32)
    nyquist_y = jnp.where((lane >= 128) & (k_y < 0.5), 128.0, 0.0)
    square_xy = k_x * k_x + nyquist_x * nyquist_x + (k_y * k_y + nyquist_y * nyquist_y)
    scale_x = jnp.where(k_x < 0.5, 1.0, 2.0)
    scale_y = jnp.where(k_y < 0.5, 1.0, 2.0)
    scale_xy = scale_x * scale_y
    damping = (ewald_split * np.pi / GRID) ** 2
    constant = GRID * GRID / (4.0 * np.pi * np.pi) / float(GRID) ** 3
    turn_x = jnp.where(row < 16, k_x, -k_x)
    turn_y = jnp.where(lane < 128, k_y, -k_y)

    def derive_x(values):
        return turn_x * jnp.concatenate([values[16:], values[:16]], axis=0)

    def derive_y(values):
        return turn_y * jnp.concatenate([values[:, 128:], values[:, :128]], axis=1)

    def filtered(index, group):
        k_z = (w * 4 + group * 2 + index).astype(F32)
        bases = [pl.multiple_of(group * 128 + half * 64 + index * 32, 32) for half in (0, 1)]
        fields = [
            [spectrum[pl.ds(bases[half], 32), c * 256 : c * 256 + 256] for c in range(3)]
            for half in (0, 1)
        ]
        flows = []
        nyquists_z = [jnp.zeros_like(k_z), jnp.where(k_z < 0.5, 128.0, 0.0)]
        scale_z = jnp.where(k_z < 0.5, 1.0, 2.0)
        turn_z = (k_z, -k_z)
        for half in (0, 1):
            values = fields[half]
            flows.append(derive_x(values[0]) + derive_y(values[1]) + turn_z[half] * fields[1 - half][2])
        for half in (0, 1):
            values = fields[half]
            nyquist_z = nyquists_z[half]
            square = square_xy + (k_z * k_z + nyquist_z * nyquist_z)
            safe = jnp.maximum(square, 1.0)
            inverse = 1.0 / safe
            factor = jnp.where(square > 0.5, jnp.exp(-damping * square) * inverse, 0.0)
            factor = factor * (scale_xy * (scale_z * constant))
            edge = (nyquist_x * values[0] + nyquist_y * values[1] + nyquist_z * values[2]) * inverse
            flow = [flows[half] * inverse, flows[1 - half] * inverse]
            gradient = [derive_x(flow[0]), derive_y(flow[0]), None]
            gradient[2] = turn_z[half] * (flows[1 - half] * inverse)
            nyquist = (nyquist_x, nyquist_y, nyquist_z)
            for c in range(3):
                spectrum[pl.ds(bases[half], 32), c * 256 : c * 256 + 256] = factor * (
                    values[c] + gradient[c] - nyquist[c] * edge
                )
        return group

    for half in (0, 1):
        narrow_go[half].arrive()
        for piece in range(8):
            groups = [narrow_in[piece, half, :, g * 128 : g * 128 + 128] for g in range(3)]
            unpacked = unpack_lanes(*groups)
            for j in range(4):
                lines[half * 128 + j * 32 : half * 128 + j * 32 + 32, piece * 128 : piece * 128 + 128] = unpacked[j]
        rows = slice(half * 128, half * 128 + 128)
        spectrum[rows, :] = dot3(split(lines[rows, :]), (t_yf[0], t_yf[1]))
        lax.fori_loop(0, 2, filtered, half)
        lines[rows, :] = dot3(split(spectrum[rows, :]), (t_yi[0], t_yi[1]))
        for target in range(8):
            groups = [
                lines[half * 128 + j * 32 : half * 128 + j * 32 + 32, target * 128 : target * 128 + 128]
                for j in range(4)
            ]
            packed = pack_lanes(*groups)
            for g in range(3):
                narrow_back[target, half, :, g * 128 : g * 128 + 128] = packed[g]
        narrow_return[half].begin()
    for half in (0, 1):
        narrow_return[half].arrive()
        block = split(narrow_home[:, half].reshape(GRID, 384))
        along = dot3((t_x[2], t_x[3]), block)
        wide_back[:, half] = along.reshape(wide_count, 8, 384)
        wide_return[half].begin()
    def end_column(step, carry):
        column_copy(step).wait()
        return carry

    lax.fori_loop(1, wide_count, end_column, 0)
    for step in range(1, narrow_count):
        line_copy(step).wait_send()
    fields = jnp.transpose(column_in[...].reshape(wide_count * narrow_count, NODES))
    first, second, gap = fields[0:32], fields[32:64], fields[160:192]
    normal = [fields[64 + 32 * c : 96 + 32 * c] for c in range(3)]
    for place in range(9):
        for s in range(SLOTS_DEV):
            mark = jnp.where(second == float(place * SLOTS_DEV + s), -1.0, 0.0)
            if place == 4:
                mark = mark + jnp.where(first == float(s), 1.0, 0.0)
            for c in range(3):
                edges[place, 3 * s + c] = mark * normal[c]
    for group in (wide_go, narrow_go, narrow_return):
        for half in (0, 1):
            group[half].sent()
    for half in (0, 1):
        wide_return[half].arrive()
    unpack_mesh(wide_home, total, m_high, m_low, h_high, h_low, turned)
    mean_velocities(total, full_means, half_means, mean_rows)

    def device(dw, dn):
        return (
            lax.rem(w + dw + wide_count, wide_count),
            lax.rem(n + dn + narrow_count, narrow_count),
        )

    devices = wide_count * narrow_count
    own = PARTIAL.index((0, 0))
    means = [jnp.sum(mean_rows[p], axis=1, keepdims=True) for p in range(6)]
    means[own] = means[own] + jnp.sum(near_ref[...], axis=1, keepdims=True) * (1.0 / NODES)
    column = jnp.concatenate(means + [jnp.zeros((32, 1), F32)], axis=0)
    line = jnp.transpose(jnp.broadcast_to(column, (128, 128)))[:8]
    tile_out[...] = jnp.where(lax.broadcasted_iota(jnp.int32, (8, 128), 0) == n, line, 0.0)

    def narrow_copy(step):
        to = lax.rem(n + step, narrow_count)
        return pltpu.make_async_remote_copy(
            src_ref=tile_out,
            dst_ref=tile_in.at[step],
            send_sem=tile_send.at[step],
            recv_sem=tile_recv.at[step],
            device_id=(w, to),
            device_id_type=MESH,
        )

    def wide_copy(step):
        to = lax.rem(w + step, wide_count)
        return pltpu.make_async_remote_copy(
            src_ref=table_out,
            dst_ref=table_in.at[w],
            send_sem=spread_send.at[step],
            recv_sem=spread_recv.at[step],
            device_id=(to, n),
            device_id_type=MESH,
        )

    for step in range(1, narrow_count):
        narrow_copy(step).start()
    part_ref[...] = jnp.zeros_like(part_ref)
    fixed = (meta_ref, cells_ref, off_ref, tz_ref, part_ref, offcol, m_high, m_low, h_high, h_low)
    interpolate(sizes, -1, *fixed)
    tile = tile_out[...]
    for step in range(1, narrow_count):
        narrow_copy(step).wait_recv()
        tile = tile + tile_in[step]
    table_out[...] = tile
    table_in[w] = tile

    def begin(step, carry):
        wide_copy(step).start()
        return carry

    lax.fori_loop(1, wide_count, begin, 0)

    interpolate(sizes, 0, *fixed)
    copies = []
    for place, (dw, dn) in enumerate(PARTIAL):
        if (dw, dn) == (0, 0):
            continue
        copy = pltpu.make_async_remote_copy(
            src_ref=part_ref.at[place],
            dst_ref=part_in.at[place],
            send_sem=part_send.at[place],
            recv_sem=part_recv.at[place],
            device_id=device(dw, dn),
            device_id_type=MESH,
        )
        copy.start()
        copies.append((place, copy))
    def end(step, carry):
        wide_copy(step).wait_recv()
        return carry

    lax.fori_loop(1, wide_count, end, 0)
    spread_means = jnp.transpose(table_in[...].reshape(devices, 128))
    hydro = jnp.zeros((16, devices), F32)
    for p, (dw, dn) in enumerate(PARTIAL):
        moved_means = shift_wide(spread_means[p * 16 : p * 16 + 16], dw, narrow_count)
        hydro = hydro + shift_narrow(moved_means, dn, narrow_count)

    def totals(force):
        def one_place(place, carry):
            for k in range(ROWS_DEV):
                loads[place, k : k + 1, :] = jnp.sum(edges[place, k] * force, axis=0, keepdims=True)
            return carry

        lax.fori_loop(0, 9, one_place, 0)
        result = jnp.zeros((16, devices), F32)
        for dn in (-1, 0, 1):
            inner = jnp.zeros((16, devices), F32)
            for dw in (-1, 0, 1):
                inner = inner + shift_wide(loads[AROUND.index((dw, dn))], dw, narrow_count)
            result = result + shift_narrow(inner, dn, narrow_count)
        return result

    def sweep(turn, carry):
        force, moving = carry
        for dn in (-1, 0, 1):
            beside = shift_narrow(moving, -dn, narrow_count)
            for dw in (-1, 0, 1):
                around[AROUND.index((dw, dn))] = shift_wide(beside, -dw, narrow_count)

        def one_place(place, relative):
            for k in range(ROWS_DEV):
                relative = relative + edges[place, k] * around[place, k : k + 1, :]
            return relative

        relative = lax.fori_loop(0, 9, one_place, jnp.zeros((CONT_DEV, devices), F32))
        force = jnp.maximum(
            force - relaxation * (gap + time_step * relative) / (2.0 * time_step * mobility), 0.0
        )
        return force, hydro + mobility * totals(force)

    loads[...] = jnp.zeros_like(loads)
    force, moving = lax.fori_loop(
        0, SWEEPS, sweep, (jnp.zeros((CONT_DEV, devices), F32), hydro)
    )
    mine = lanes_of((1, devices)) == w * narrow_count + n
    own_force = jnp.sum(jnp.where(mine, force, 0.0), axis=1, keepdims=True)
    force_ref[...] = jnp.broadcast_to(own_force, (CONT_DEV, 128))
    own_moving = jnp.sum(jnp.where(mine, moving, 0.0), axis=1, keepdims=True)
    row = lax.broadcasted_iota(jnp.int32, (16, 128), 0)
    centre = jnp.zeros((16, 128), F32)
    for k in range(ROWS_DEV):
        centre = jnp.where(row == k, meta_ref[GATHER.index((0, 0)), k], centre)
    moved_ref[...] = centre + time_step * own_moving
    velocity = part_ref[own] + near_ref[...]
    for place, copy in copies:
        copy.wait_recv()
        velocity = velocity + part_in[place]
    velocity_ref[...] = velocity
    for place, copy in copies:
        copy.wait_send()
    for half in (0, 1):
        wide_return[half].sent()
    for step in range(1, narrow_count):
        narrow_copy(step).wait_send()

    def finish(step, carry):
        wide_copy(step).wait_send()
        return carry

    lax.fori_loop(1, wide_count, finish, 0)


def local(
    wide_count,
    narrow_count,
    tractions,
    centers,
    node_offsets,
    occupied,
    anchors,
    near_list,
    contact_pairs,
    contact_gap,
    contact_angles,
):
    w, n = lax.axis_index("wide"), lax.axis_index("narrow")
    sizes = (wide_count, narrow_count)
    shape = jax.ShapeDtypeStruct
    dma = pltpu.SemaphoreType.DMA

    held, metas, cells = pl.pallas_call(
        functools.partial(gather_kernel, *sizes),
        out_shape=(shape((12, 16, NODES), F32), shape((12, 128), F32), shape((12, 128), jnp.int32)),
        in_specs=[VMEM_SPEC, SMEM_SPEC, SMEM_SPEC, SMEM_SPEC],
        out_specs=(VMEM_SPEC,) * 3,
        scratch_shapes=[
            pltpu.VMEM((16, NODES), F32),
            pltpu.VMEM((12, 16, NODES), F32),
            dma((12,)),
            dma((12,)),
        ],
        compiler_params=params(0),
        name="gather",
    )(tractions, centers, anchors, occupied)

    table_z = trig_table(2)
    wrapped_z = np.concatenate([table_z, table_z[:, :32]], axis=1).T.astype(np.float32).reshape(36, 8, GRID)
    table_x = trig_table(16)
    table_y = trig_table(128)
    turned_x = np.ascontiguousarray(table_x.T)
    turned_y = np.ascontiguousarray(table_y.T)
    tables = np.stack([*halves(table_x), *halves(turned_x), *halves(turned_y)])
    devices = wide_count * narrow_count
    velocity, force, moved = pl.pallas_call(
        functools.partial(flow_kernel, *sizes),
        out_shape=(shape((16, NODES), F32), shape((CONT_DEV, 128), F32), shape((16, 128), F32)),
        in_specs=[SMEM_SPEC] * 3 + [VMEM_SPEC] * 6 + [HBM_SPEC],
        out_specs=(VMEM_SPEC,) * 3,
        scratch_shapes=[
            pltpu.VMEM((16, NODES), F32),
            pltpu.VMEM((768, GRID), BF16),
            pltpu.VMEM((768, GRID), BF16),
            pltpu.VMEM((384, GRID), BF16),
            pltpu.VMEM((384, GRID), BF16),
            pltpu.VMEM((12, 256, GRID), F32),
            pltpu.VMEM((12, 128, GRID), F32),
            pltpu.VMEM((6, 16, NODES), F32),
            pltpu.VMEM((6, 16, NODES), F32),
            pltpu.VMEM((6, 16, NODES), F32),
            pltpu.VMEM((8, 128), F32),
            pltpu.VMEM((8, 8, 128), F32),
            pltpu.VMEM((8, 128), F32),
            pltpu.VMEM((32, 8, 128), F32),
            pltpu.VMEM((9, ROWS_DEV, CONT_DEV, devices), F32),
            pltpu.VMEM((9, 16, devices), F32),
            pltpu.VMEM((9, 16, devices), F32),
            dma((6,)),
            dma((6,)),
            dma((8,)),
            dma((8,)),
            dma((32,)),
            dma((32,)),
            pltpu.VMEM((2, 768, NODES), BF16),
            pltpu.VMEM((2, 768, NODES), BF16),
            pltpu.VMEM((768, GRID), F32),
            pltpu.VMEM((GRID * 8, 128), F32),
            pltpu.VMEM((32, 2, 8, 384), F32),
            pltpu.VMEM((32, 2, 8, 384), F32),
            pltpu.VMEM((8, 2, 32, 384), F32),
            pltpu.VMEM((8, 2, 32, 384), F32),
            pltpu.VMEM((8, 2, 32, 384), F32),
            pltpu.VMEM((8, 2, 32, 384), F32),
            pltpu.VMEM((32, 2, 8, 384), F32),
            pltpu.VMEM((32, 2, 8, 384), F32),
            pltpu.VMEM((256, 1024), F32),
            pltpu.VMEM((256, 768), F32),
            pltpu.VMEM((6, 256, 256), BF16),
            pltpu.VMEM((2, 1024, 768), BF16),
            pltpu.VMEM((2, 768, 1024), BF16),
            pltpu.VMEM((3, NODES, 128), F32),
            pltpu.VMEM((3, 8, NODES), F32),
            pltpu.VMEM((NODES, 8), F32),
            pltpu.VMEM((8, NODES), F32),
            pltpu.VMEM((8, 8, NODES), F32),
            pltpu.VMEM((8, NODES), F32),
            pltpu.VMEM((32, 8, NODES), F32),
            dma((2, 2, 32)),
            dma((2, 2, 32)),
            dma((2, 2, 8)),
            dma((2, 2, 8)),
            dma,
            dma((8,)),
            dma((8,)),
            dma((32,)),
            dma((32,)),
        ],
        compiler_params=params(1, 56),
        name="flow",
    )(
        near_list.reshape(4, NEAR),
        metas,
        cells,
        held,
        node_offsets,
        wrapped_z,
        contact_pairs,
        contact_gap,
        contact_angles,
        tables,
    )
    return (
        velocity[:12].reshape(2, 2, 3, NODES),
        force[:, 0],
        moved[:12, 0].reshape(2, 2, 3),
    )


def solution(mesh):
    placed = (
        P("wide", "narrow", None, None),
        P("wide", "narrow", None),
        P(),
        P("wide", "narrow"),
        P("wide", "narrow", None),
        P("wide", "narrow", None),
        P(None, ("wide", "narrow")),
        P(("wide", "narrow")),
        P(None, ("wide", "narrow")),
    )
    return jax.shard_map(
        functools.partial(local, mesh.shape["wide"], mesh.shape["narrow"]),
        mesh=mesh,
        in_specs=placed,
        out_specs=(
            P("wide", "narrow", None, None),
            P(("wide", "narrow")),
            P("wide", "narrow", None),
        ),
        check_vma=False,
    )
```

```python
import functools

import jax
import jax.numpy as jnp
import ml_dtypes
import numpy as np
from jax import lax
from jax.experimental import pallas as pl
from jax.experimental.pallas import tpu as pltpu
from jax.sharding import PartitionSpec as P

NODES = 256
GRID = 256
BLOCK = 16
NEAR = 2
SWEEPS = 6
SLOTS_DEV = 4
ROWS_DEV = 3 * SLOTS_DEV
CONT_DEV = 32
EDGE_ROWS = 112

soften = 1.0
screen = 0.0625
near_scale = 0.05
spread_norm = 0.17958712212516656
mobility = 0.2
time_step = 0.5
relaxation = 0.35
ewald_split = 0.5

MESH = pl.DeviceIdType.MESH
F32 = jnp.float32
BF16 = jnp.bfloat16
VMEM_SPEC = pl.BlockSpec(memory_space=pltpu.VMEM)
HBM_SPEC = pl.BlockSpec(memory_space=pltpu.HBM)
SMEM_SPEC = pl.BlockSpec(memory_space=pltpu.SMEM)


def params(collective_id=None, limit=40):
    if collective_id is None:
        return pltpu.CompilerParams(vmem_limit_bytes=limit * 2**20)
    return pltpu.CompilerParams(
        vmem_limit_bytes=limit * 2**20, collective_id=collective_id, has_side_effects=True
    )


def trig_table(group):
    cell = np.arange(GRID)
    rows = []
    for first in range(0, GRID // 2, group):
        for half in (0, 1):
            for k in range(first, first + group):
                angle = 2.0 * np.pi / GRID * (k * cell % GRID)
                if half == 0:
                    rows.append(np.cos(angle))
                elif k == 0:
                    rows.append(np.cos(np.pi * cell))
                else:
                    rows.append(np.sin(angle))
    return np.stack(rows)


def halves(table):
    high = table.astype(np.float32).astype(ml_dtypes.bfloat16)
    low = (table - high.astype(np.float64)).astype(np.float32).astype(ml_dtypes.bfloat16)
    return high, low


def split(values):
    high = values.astype(BF16)
    return high, (values - high.astype(F32)).astype(BF16)


def dot(a, b, contract=((1,), (0,))):
    return lax.dot_general(a, b, (contract, ((), ())), preferred_element_type=F32)


def dot3(a, b):
    return dot(
        jnp.concatenate([a[0], a[0], a[1]], axis=1), jnp.concatenate([b[0], b[1], b[0]], axis=0)
    )


def lanes_of(shape):
    return lax.broadcasted_iota(jnp.int32, shape, len(shape) - 1)


def roll(values, shift):
    return pltpu.roll(values, shift, len(values.shape) - 1)


def pack_lanes(u0, u1, u2, u3):
    lane = lanes_of(u0.shape)
    r1, r2, r3 = roll(u1, 96), roll(u2, 64), roll(u3, 32)
    return (
        jnp.where(lane < 96, u0, r1),
        jnp.where(lane < 64, r1, r2),
        jnp.where(lane < 32, r2, r3),
    )


def unpack_lanes(p0, p1, p2):
    lane = lanes_of(p0.shape)
    return (
        p0,
        roll(jnp.where(lane < 64, p1, p0), 32),
        roll(jnp.where(lane < 32, p2, p1), 64),
        roll(p2, 96),
    )


def hail(wide_count, narrow_count, offsets):
    w, n = lax.axis_index("wide"), lax.axis_index("narrow")
    for dw, dn in offsets:
        pl.semaphore_signal(
            pltpu.get_barrier_semaphore(),
            inc=1,
            device_id=(
                lax.rem(w + dw + wide_count, wide_count),
                lax.rem(n + dn + narrow_count, narrow_count),
            ),
            device_id_type=MESH,
        )


def hear(offsets):
    pl.semaphore_wait(pltpu.get_barrier_semaphore(), len(offsets))


GATHER = [(dw, dn) for dw in (-2, -1, 0, 1) for dn in (-1, 0, 1)]


def gather_kernel(
    wide_count,
    narrow_count,
    tractions_ref,
    centres_ref,
    anchors_ref,
    occupied_ref,
    out_ref,
    meta_ref,
    cells_ref,
    own_ref,
    held,
    send_sem,
    recv_sem,
):
    w, n = lax.axis_index("wide"), lax.axis_index("narrow")
    reach = [(dw, dn) for dw in (-2, -1, 0, 1, 2) for dn in (-1, 0, 1) if (dw, dn) != (0, 0)]
    hail(wide_count, narrow_count, reach)
    slots = [(a, b) for a in (0, 1) for b in (0, 1)]
    numbers = [centres_ref[a, b, c] for a, b in slots for c in range(3)]
    numbers += [anchors_ref[a, b, c].astype(F32) for a, b in slots for c in range(3)]
    numbers += [occupied_ref[a, b].astype(F32) for a, b in slots]
    lane = lanes_of((1, NODES))
    line = jnp.zeros((1, NODES), F32)
    for place, number in enumerate(numbers):
        line = jnp.where(lane == place, number, line)
    for s, (a, b) in enumerate(slots):
        own_ref[3 * s : 3 * s + 3, :] = tractions_ref[a, b]
    own_ref[12:16, :] = jnp.broadcast_to(line, (4, NODES))
    hear(reach)
    copies = []
    for place, (dw, dn) in enumerate(GATHER):
        if (dw, dn) == (0, 0):
            continue
        copy = pltpu.make_async_remote_copy(
            src_ref=own_ref,
            dst_ref=held.at[place],
            send_sem=send_sem.at[place],
            recv_sem=recv_sem.at[place],
            device_id=(
                lax.rem(w - dw + wide_count, wide_count),
                lax.rem(n - dn + narrow_count, narrow_count),
            ),
            device_id_type=MESH,
        )
        copy.start()
        copies.append((place, copy))
    own = GATHER.index((0, 0))
    out_ref[own] = own_ref[...]
    meta_ref[own : own + 1, :] = own_ref[12:13, 0:128]
    cells_ref[own : own + 1, :] = own_ref[12:13, 0:128].astype(jnp.int32)
    for place, copy in copies:
        copy.wait_recv()
        out_ref[place] = held[place]
        meta_ref[place : place + 1, :] = held[place, 12:13, 0:128]
        cells_ref[place : place + 1, :] = held[place, 12:13, 0:128].astype(jnp.int32)
    for place, copy in copies:
        copy.wait_send()


def near_field(sizes, list_ref, meta_ref, held_ref, off_ref, out_ref, offcol, source, columns):
    wide_count, narrow_count = sizes
    w, n = lax.axis_index("wide"), lax.axis_index("narrow")
    own = GATHER.index((0, 0))
    out_ref[...] = jnp.zeros_like(out_ref)
    columns[...] = jnp.zeros_like(columns)
    for s in range(SLOTS_DEV):
        for j in range(1 + NEAR):
            if j == 0:
                place, within = own, s
            else:
                entry = list_ref[s // 2, s % 2, j - 1]
                holder = entry // SLOTS_DEV
                within = entry % SLOTS_DEV
                row = lax.rem(holder // narrow_count - w + 1 + wide_count, wide_count)
                column = lax.rem(lax.rem(holder, narrow_count) - n + 1 + narrow_count, narrow_count)
                place = (jnp.minimum(row, 2) + 1) * 3 + jnp.minimum(column, 2)
            for c in range(3):
                if j == 0:
                    shift = 0.0
                else:
                    e = meta_ref[own, 3 * s + c] - meta_ref[place, 3 * within + c]
                    shift = e - jnp.where(e >= 128.0, 256.0, jnp.where(e < -128.0, -256.0, 0.0))
                source[j, c : c + 1, :] = shift - off_ref[c : c + 1, :]
                source[j, 3 + c : 4 + c, :] = held_ref[place, pl.ds(within * 3 + c, 1), :]

        def chunk(i, carry):
            for part in (0, 1):
                rows = pl.ds(pl.multiple_of(i * 16 + part * 8, 8), 8)
                sums = [jnp.zeros((8, 128), F32) for _ in range(3)]
                at = [offcol[c, rows, :] for c in range(3)]
                for j in range(1 + NEAR):
                    for half in (0, 1):
                        lanes = slice(half * 128, half * 128 + 128)
                        d = [at[c] + source[j, c : c + 1, lanes] for c in range(3)]
                        f = [source[j, 3 + c : 4 + c, lanes] for c in range(3)]
                        r2 = d[0] * d[0] + d[1] * d[1] + d[2] * d[2]
                        inverse = lax.rsqrt(r2 + soften)
                        weight = jnp.exp(r2 * (-screen)) * (inverse * inverse * inverse)
                        along = (d[0] * f[0] + d[1] * f[1] + d[2] * f[2]) * weight
                        diagonal = (r2 + 2.0 * soften) * weight
                        for c in range(3):
                            sums[c] = sums[c] + (diagonal * f[c] + d[c] * along)
                for c in range(3):
                    columns[rows, c : c + 1] = jnp.sum(sums[c], axis=1, keepdims=True)
            return carry

        lax.fori_loop(0, NODES // 16, chunk, 0)
        result = jnp.transpose(columns[...])
        alive = jnp.where(meta_ref[own, 24 + s] > 0.5, near_scale, 0.0)
        out_ref[3 * s : 3 * s + 3, :] = alive * result[0:3, :]


def columns_of(off_ref, offcol):
    padded = jnp.concatenate([off_ref[...], jnp.zeros((5, NODES), F32)], axis=0)
    turned = jnp.transpose(padded)
    for c in range(3):
        offcol[c] = jnp.broadcast_to(turned[:, c : c + 1], (NODES, 128))


def sphere_weights(sizes, dw, dn, s, meta_ref, cells_ref, off_ref, offcol, tz_ref):
    wide_count, narrow_count = sizes
    w, n = lax.axis_index("wide"), lax.axis_index("narrow")
    size_x, size_y = GRID // wide_count, GRID // narrow_count
    place = (dw + 2) * 3 + dn + 1
    anchor = [cells_ref[place, 12 + 3 * s + c] for c in range(3)]
    centre = [meta_ref[place, 3 * s + c] for c in range(3)]
    alive = jnp.where(meta_ref[place, 24 + s] > 0.5, spread_norm, 0.0)
    low_x = anchor[0] - size_x * lax.rem(w + dw + wide_count, wide_count) + size_x * dw
    low_y = anchor[1] - size_y * lax.rem(n + dn + narrow_count, narrow_count) + size_y * dn
    low_z = anchor[2] % 8

    def weights(cell, position, base, low, factor):
        distance = position - (base + cell).astype(F32)
        inside = (cell >= low) & (cell < low + BLOCK)
        return jnp.where(inside, jnp.exp(-distance * distance) * factor, 0.0)

    def rows(c, low, count, factor):
        cell = lax.broadcasted_iota(jnp.int32, (count, NODES), 0)
        return weights(cell, centre[c] + off_ref[c : c + 1, :], anchor[c] - low, low, factor)

    lane = lanes_of((NODES, 128))
    wz = weights(lane % 32, centre[2] + offcol[2], anchor[2] - low_z, low_z, 1.0)
    high = wz.astype(BF16).astype(F32)
    left = jnp.where(lane < 64, high, jnp.where(lane < 96, wz - high, 0.0)).astype(BF16)
    tile = anchor[2] // 8
    t_high, t_low = split(jnp.concatenate([tz_ref[tile + t] for t in range(4)], axis=0))
    right = jnp.concatenate([t_high, t_low, t_high, jnp.zeros((32, GRID), BF16)], axis=0)
    along_z = split(dot(left, right))
    return place, rows(0, low_x, size_x, alive), rows(1, low_y, 16 if dn else size_y, 1.0), along_z


def pair_loop(body, dn, unroll=1):
    def step(index, carry):
        body(index // 2 - 2, dn, index % 2)
        return carry

    lax.fori_loop(0, 6, step, 0, unroll=unroll)


def spread(sizes, meta_ref, cells_ref, held_ref, off_ref, tz_ref, out_ref, offcol, a_high, a_low, total, turned):
    total[...] = jnp.zeros_like(total)

    def pair(dw, dn, which):
        span = 16 if dn else 32
        sums = []
        for member in (0, 1):
            s = 2 * which + member
            place, wx, wy, along_z = sphere_weights(sizes, dw, dn, s, meta_ref, cells_ref, off_ref, offcol, tz_ref)
            planar = jnp.concatenate(
                [wy * held_ref[place, pl.ds(s * 3 + c, 1), :] for c in range(3)], axis=0
            )
            size = 3 * span
            for x in range(8):
                high, low = split(planar * wx[x : x + 1, :])
                a_high[member, x * size : x * size + size, :] = high
                a_low[member, x * size : x * size + size, :] = low
            rows = slice(0, 8 * size)
            sums.append(dot3((a_high[member, rows, :], a_low[member, rows, :]), along_z))
        both = sums[0] + sums[1]
        if dn == 0:
            total[...] += both
        else:
            for block in range(24):
                total[block * 32 : block * 32 + 16, :] += both[block * 16 : block * 16 + 16]

    pair_loop(pair, -1)
    pair_loop(pair, 0)
    for x in range(8):
        block = jnp.concatenate([total[x * 96 : x * 96 + 96, :], jnp.zeros((32, GRID), F32)], axis=0)
        turned[pl.ds(x, GRID, stride=8), :] = jnp.transpose(block)
    values = turned[...].reshape(64, 4, 8, 128)
    packed = pack_lanes(*[values[:, j] for j in range(4)])
    for g in range(3):
        out_ref[:, :, :, g * 128 : g * 128 + 128] = packed[g].reshape(32, 2, 8, 128)


def mean_weights(sizes, meta_ref, cells_ref, off_ref, tz_ref, offcol, full, half):
    def pair(dw, dn, which):
        span = 16 if dn else 32
        for member in (0, 1):
            s = 2 * which + member
            place, wx, wy, along_z = sphere_weights(
                sizes, dw, dn, s, meta_ref, cells_ref, off_ref, offcol, tz_ref
            )
            wy = wy * (1.0 / NODES)
            left = split(jnp.concatenate([wy * wx[x : x + 1, :] for x in range(8)], axis=0))
            target = half if dn else full
            target[(dw + 2) * 4 + s] = dot3(left, along_z)

    pair_loop(pair, -1)
    pair_loop(pair, 0)


def mean_velocities(values, full, half, rows_ref):
    rows_ref[...] = jnp.zeros_like(rows_ref)
    for dn in (-1, 0):
        span = 16 if dn else 32

        def sphere(index, carry):
            source = half if dn else full
            tiles = [jnp.zeros((8, GRID), F32) for _ in range(3)]
            for x in range(8):
                for y in range(0, span, 8):
                    weight = source[index, x * span + y : x * span + y + 8, :]
                    for c in range(3):
                        at = x * 96 + c * 32 + y
                        tiles[c] = tiles[c] + values[at : at + 8, :] * weight
            piece = (index // 4) * 2 + dn + 1
            for c in range(3):
                rows_ref[piece, pl.ds((index % 4) * 3 + c, 1), :] = jnp.sum(tiles[c], axis=0, keepdims=True)
            return carry

        lax.fori_loop(0, 12, sphere, 0)


def unpack_mesh(mesh_ref, values, m_high, m_low, h_high, h_low, turned):
    groups = [mesh_ref[:, :, :, g * 128 : g * 128 + 128].reshape(64, 8, 128) for g in range(3)]
    unpacked = unpack_lanes(*groups)
    turned[...] = jnp.stack(unpacked, axis=1).reshape(GRID * 8, 128)
    for x in range(8):
        block = jnp.transpose(turned[pl.ds(x, GRID, stride=8), :])[:96]
        values[x * 96 : x * 96 + 96, :] = block
        high, low = split(block)
        m_high[x * 96 : x * 96 + 96, :] = high
        m_low[x * 96 : x * 96 + 96, :] = low
        for c in range(3):
            target = slice(x * 48 + c * 16, x * 48 + c * 16 + 16)
            h_high[target, :] = high[c * 32 : c * 32 + 16]
            h_low[target, :] = low[c * 32 : c * 32 + 16]


def interpolate(
    sizes, lower, meta_ref, cells_ref, off_ref, tz_ref, out_ref, offcol, m_high, m_low, h_high, h_low
):
    def pair(dw, dn, which):
        span = 16 if dn else 32
        size = 3 * span
        for member in (0, 1):
            s = 2 * which + member
            place, wx, wy, along_z = sphere_weights(sizes, dw, dn, s, meta_ref, cells_ref, off_ref, offcol, tz_ref)
            left = (h_high[...], h_low[...]) if dn else (m_high[...], m_low[...])
            turn = ((1,), (1,))
            found = dot(
                jnp.concatenate([left[0], left[0], left[1]], axis=1),
                jnp.concatenate([along_z[0], along_z[1], along_z[0]], axis=1),
                turn,
            )
            summed = found[0:size] * wx[0:1, :]
            for x in range(1, 8):
                summed = summed + found[x * size : x * size + size] * wx[x : x + 1, :]
            owner = (dw + 2) * 2 + dn + 1
            for c in range(3):
                out_ref[owner, pl.ds(s * 3 + c, 1), :] = jnp.sum(
                    summed[c * span : c * span + span] * wy, axis=0, keepdims=True
                )

    pair_loop(pair, lower, 2)


AROUND = [(dw, dn) for dw in (-1, 0, 1) for dn in (-1, 0, 1)]
PARTIAL = [(dw, dn) for dw in (-2, -1, 0) for dn in (-1, 0)]


def shift_narrow(values, dn, narrow_count):
    if dn == 0:
        return values
    place = lanes_of(values.shape) % narrow_count
    edge = 0 if dn == 1 else narrow_count - 1
    total = values.shape[-1]
    return jnp.where(
        place == edge,
        roll(values, (dn - dn * narrow_count) % total),
        roll(values, dn % total),
    )


def shift_wide(values, dw, narrow_count):
    if dw == 0:
        return values
    return roll(values, (dw * narrow_count) % values.shape[-1])


class Exchange:
    def __init__(self, axis, count, source, target, half, send_sem, recv_sem, me, other):
        self.__dict__.update(locals())

    def copy_to(self, step):
        to = lax.rem(self.me + step, self.count)
        return pltpu.make_async_remote_copy(
            src_ref=self.source.at[to, self.half],
            dst_ref=self.target.at[self.me, self.half],
            send_sem=self.send_sem.at[step],
            recv_sem=self.recv_sem.at[step],
            device_id=(to, self.other) if self.axis == "wide" else (self.other, to),
            device_id_type=MESH,
        )

    def begin(self):
        def step(index, carry):
            self.copy_to(index).start()
            return carry

        lax.fori_loop(1, self.count, step, 0)
        self.target[self.me, self.half] = self.source[self.me, self.half]

    def arrive(self):
        def step(index, carry):
            self.copy_to(index).wait_recv()
            return carry

        lax.fori_loop(1, self.count, step, 0)

    def sent(self):
        def step(index, carry):
            self.copy_to(index).wait_send()
            return carry

        lax.fori_loop(1, self.count, step, 0)


def flow_kernel(
    wide_count,
    narrow_count,
    list_ref,
    meta_ref,
    cells_ref,
    held_ref,
    off_ref,
    tz_ref,
    pairs_ref,
    gap_ref,
    angles_ref,
    tables,
    velocity_ref,
    force_ref,
    moved_ref,
    near_ref,
    m_high,
    m_low,
    h_high,
    h_low,
    full_means,
    half_means,
    mean_rows,
    part_ref,
    part_in,
    tile_out,
    tile_in,
    table_out,
    table_in,
    edges,
    fields,
    around,
    loads,
    relatives,
    forces,
    part_send,
    part_recv,
    tile_send,
    tile_recv,
    spread_send,
    spread_recv,
    a_high,
    a_low,
    total,
    turned,
    mesh_ref,
    wide_in,
    narrow_out,
    narrow_in,
    narrow_back,
    narrow_home,
    wide_back,
    wide_home,
    lines,
    spectrum,
    t_x,
    t_yf,
    t_yi,
    offcol,
    source,
    columns,
    own_line,
    lines_in,
    column_out,
    column_in,
    wide_send,
    wide_recv,
    narrow_send,
    narrow_recv,
    table_sem,
    line_send,
    line_recv,
    column_send,
    column_recv,
):
    w, n = lax.axis_index("wide"), lax.axis_index("narrow")
    load = pltpu.make_async_copy(tables, t_x, table_sem)
    load.start()
    reach = (
        [(step, 0) for step in range(1, wide_count)]
        + [(0, step) for step in range(1, narrow_count)]
        + [(-2, -1), (-1, -1), (2, 1), (1, 1)]
    )
    sizes = (wide_count, narrow_count)
    hail(*sizes, reach)
    columns_of(off_ref, offcol)
    spread(sizes, meta_ref, cells_ref, held_ref, off_ref, tz_ref, mesh_ref, offcol, a_high, a_low, total, turned)
    hear(reach)

    def exchanges(axis, source, target, way):
        if axis == "wide":
            fixed = (wide_count, w, n, wide_send, wide_recv)
        else:
            fixed = (narrow_count, n, w, narrow_send, narrow_recv)
        count, me, other, send_sem, recv_sem = fixed
        return [
            Exchange(
                axis, count, source, target, half, send_sem.at[way, half], recv_sem.at[way, half], me, other
            )
            for half in (0, 1)
        ]

    wide_go = exchanges("wide", mesh_ref, wide_in, 0)
    narrow_go = exchanges("narrow", narrow_out, narrow_in, 0)
    narrow_return = exchanges("narrow", narrow_back, narrow_home, 1)
    wide_return = exchanges("wide", wide_back, wide_home, 1)
    for half in (0, 1):
        wide_go[half].begin()

    ids = pairs_ref[...]
    within = (ids % SLOTS_DEV).astype(F32)
    holder = ids // SLOTS_DEV
    row_w = lax.rem(holder // narrow_count - w + 1 + wide_count, wide_count)
    row_n = lax.rem(lax.rem(holder, narrow_count) - n + 1 + narrow_count, narrow_count)
    seconds = ((row_w * 3 + row_n) * SLOTS_DEV).astype(F32) + within
    polar, azimuth = angles_ref[0:1, :], angles_ref[1:2, :]
    across = jnp.sin(polar)
    parts = [
        within[0:1],
        seconds[1:2],
        across * jnp.cos(azimuth),
        across * jnp.sin(azimuth),
        jnp.cos(polar),
        gap_ref[...].reshape(1, CONT_DEV),
    ]
    line = jnp.concatenate(parts + [jnp.zeros((1, 64), F32)], axis=1)
    own_line[...] = jnp.where(lax.broadcasted_iota(jnp.int32, (8, NODES), 0) == n, line, 0.0)

    def line_copy(step):
        return pltpu.make_async_remote_copy(
            src_ref=own_line,
            dst_ref=lines_in.at[step],
            send_sem=line_send.at[step],
            recv_sem=line_recv.at[step],
            device_id=(w, lax.rem(n + step, narrow_count)),
            device_id_type=MESH,
        )

    def column_copy(step):
        return pltpu.make_async_remote_copy(
            src_ref=column_out,
            dst_ref=column_in.at[w],
            send_sem=column_send.at[step],
            recv_sem=column_recv.at[step],
            device_id=(lax.rem(w + step, wide_count), n),
            device_id_type=MESH,
        )

    for step in range(1, narrow_count):
        line_copy(step).start()
    mean_weights(sizes, meta_ref, cells_ref, off_ref, tz_ref, offcol, full_means, half_means)
    load.wait()
    t_yf[...] = jnp.zeros_like(t_yf)
    for part in (0, 1):
        for piece in range(8):
            for c in range(3):
                t_yf[part, piece * 128 + c * 32 : piece * 128 + c * 32 + 32, c * 256 : c * 256 + 256] = t_x[
                    4 + part, piece * 32 : piece * 32 + 32, :
                ]
        for piece in range(8):
            for c in range(3):
                block = t_yf[part, piece * 128 : piece * 128 + 128, c * 256 : c * 256 + 256]
                t_yi[part, c * 256 : c * 256 + 256, piece * 128 : piece * 128 + 128] = jnp.transpose(
                    block.astype(F32)
                ).astype(BF16)
    for half in (0, 1):
        wide_go[half].arrive()
        block = split(wide_in[:, half].reshape(GRID, 384))
        along = dot3((t_x[0], t_x[1]), block)
        narrow_out[:, half] = along.reshape(narrow_count, 32, 384)
        narrow_go[half].begin()
    column = own_line[...]
    for step in range(1, narrow_count):
        line_copy(step).wait_recv()
        column = column + lines_in[step]
    column_out[...] = column
    column_in[w] = column

    def begin_column(step, carry):
        column_copy(step).start()
        return carry

    lax.fori_loop(1, wide_count, begin_column, 0)
    row = lax.broadcasted_iota(jnp.int32, (32, 1), 0)
    k_x = (n * 16 + row % 16).astype(F32)
    nyquist_x = jnp.where((row >= 16) & (k_x < 0.5), 128.0, 0.0)
    lane = lax.broadcasted_iota(jnp.int32, (1, GRID), 1)
    k_y = (lane % 128).astype(F32)
    nyquist_y = jnp.where((lane >= 128) & (k_y < 0.5), 128.0, 0.0)
    square_xy = k_x * k_x + nyquist_x * nyquist_x + (k_y * k_y + nyquist_y * nyquist_y)
    scale_x = jnp.where(k_x < 0.5, 1.0, 2.0)
    scale_y = jnp.where(k_y < 0.5, 1.0, 2.0)
    scale_xy = scale_x * scale_y
    damping = (ewald_split * np.pi / GRID) ** 2
    constant = GRID * GRID / (4.0 * np.pi * np.pi) / float(GRID) ** 3
    turn_x = jnp.where(row < 16, k_x, -k_x)
    turn_y = jnp.where(lane < 128, k_y, -k_y)

    def derive_x(values):
        return turn_x * jnp.concatenate([values[16:], values[:16]], axis=0)

    def derive_y(values):
        return turn_y * jnp.concatenate([values[:, 128:], values[:, :128]], axis=1)

    def filtered(index, group):
        k_z = (w * 4 + group * 2 + index).astype(F32)
        bases = [pl.multiple_of(group * 128 + half * 64 + index * 32, 32) for half in (0, 1)]
        fields = [
            [spectrum[pl.ds(bases[half], 32), c * 256 : c * 256 + 256] for c in range(3)]
            for half in (0, 1)
        ]
        flows = []
        nyquists_z = [jnp.zeros_like(k_z), jnp.where(k_z < 0.5, 128.0, 0.0)]
        scale_z = jnp.where(k_z < 0.5, 1.0, 2.0)
        turn_z = (k_z, -k_z)
        for half in (0, 1):
            values = fields[half]
            flows.append(derive_x(values[0]) + derive_y(values[1]) + turn_z[half] * fields[1 - half][2])
        for half in (0, 1):
            values = fields[half]
            nyquist_z = nyquists_z[half]
            square = square_xy + (k_z * k_z + nyquist_z * nyquist_z)
            safe = jnp.maximum(square, 1.0)
            inverse = 1.0 / safe
            factor = jnp.where(square > 0.5, jnp.exp(-damping * square) * inverse, 0.0)
            factor = factor * (scale_xy * (scale_z * constant))
            edge = (nyquist_x * values[0] + nyquist_y * values[1] + nyquist_z * values[2]) * inverse
            flow = [flows[half] * inverse, flows[1 - half] * inverse]
            gradient = [derive_x(flow[0]), derive_y(flow[0]), None]
            gradient[2] = turn_z[half] * (flows[1 - half] * inverse)
            nyquist = (nyquist_x, nyquist_y, nyquist_z)
            for c in range(3):
                spectrum[pl.ds(bases[half], 32), c * 256 : c * 256 + 256] = factor * (
                    values[c] + gradient[c] - nyquist[c] * edge
                )
        return group

    for half in (0, 1):
        narrow_go[half].arrive()
        for piece in range(8):
            groups = [narrow_in[piece, half, :, g * 128 : g * 128 + 128] for g in range(3)]
            unpacked = unpack_lanes(*groups)
            for j in range(4):
                lines[half * 128 + j * 32 : half * 128 + j * 32 + 32, piece * 128 : piece * 128 + 128] = unpacked[j]
        rows = slice(half * 128, half * 128 + 128)
        spectrum[rows, :] = dot3(split(lines[rows, :]), (t_yf[0], t_yf[1]))
        lax.fori_loop(0, 2, filtered, half)
        lines[rows, :] = dot3(split(spectrum[rows, :]), (t_yi[0], t_yi[1]))
        for target in range(8):
            groups = [
                lines[half * 128 + j * 32 : half * 128 + j * 32 + 32, target * 128 : target * 128 + 128]
                for j in range(4)
            ]
            packed = pack_lanes(*groups)
            for g in range(3):
                narrow_back[target, half, :, g * 128 : g * 128 + 128] = packed[g]
        narrow_return[half].begin()
    for half in (0, 1):
        narrow_return[half].arrive()
        block = split(narrow_home[:, half].reshape(GRID, 384))
        along = dot3((t_x[2], t_x[3]), block)
        wide_back[:, half] = along.reshape(wide_count, 8, 384)
        wide_return[half].begin()
    near_field(
        (wide_count, narrow_count), list_ref, meta_ref, held_ref, off_ref, near_ref, offcol, source, columns
    )
    def end_column(step, carry):
        column_copy(step).wait()
        return carry

    lax.fori_loop(1, wide_count, end_column, 0)
    for step in range(1, narrow_count):
        line_copy(step).wait_send()
    fields[...] = jnp.transpose(column_in[...].reshape(wide_count * narrow_count, NODES))
    sphere = lax.broadcasted_iota(jnp.int32, (EDGE_ROWS, 1), 0)
    component = sphere % 3
    sphere = (sphere // 3).astype(F32)

    def incidence(i, carry):
        first, second = fields[pl.ds(i, 1), :] + 4.0 * SLOTS_DEV, fields[pl.ds(32 + i, 1), :]
        normal = [fields[pl.ds(64 + 32 * c + i, 1), :] for c in range(3)]
        along = jnp.where(component == 0, normal[0], jnp.where(component == 1, normal[1], normal[2]))
        sign = jnp.where(sphere == first, 1.0, 0.0) - jnp.where(sphere == second, 1.0, 0.0)
        edges[i] = sign * along
        return carry

    lax.fori_loop(0, CONT_DEV, incidence, 0)
    for group in (wide_go, narrow_go, narrow_return):
        for half in (0, 1):
            group[half].sent()
    for half in (0, 1):
        wide_return[half].arrive()
    unpack_mesh(wide_home, total, m_high, m_low, h_high, h_low, turned)
    mean_velocities(total, full_means, half_means, mean_rows)

    def device(dw, dn):
        return (
            lax.rem(w + dw + wide_count, wide_count),
            lax.rem(n + dn + narrow_count, narrow_count),
        )

    devices = wide_count * narrow_count
    own = PARTIAL.index((0, 0))
    means = [jnp.sum(mean_rows[p], axis=1, keepdims=True) for p in range(6)]
    means[own] = means[own] + jnp.sum(near_ref[...], axis=1, keepdims=True) * (1.0 / NODES)
    column = jnp.concatenate(means + [jnp.zeros((32, 1), F32)], axis=0)
    line = jnp.transpose(jnp.broadcast_to(column, (128, 128)))[:8]
    tile_out[...] = jnp.where(lax.broadcasted_iota(jnp.int32, (8, 128), 0) == n, line, 0.0)

    def narrow_copy(step):
        to = lax.rem(n + step, narrow_count)
        return pltpu.make_async_remote_copy(
            src_ref=tile_out,
            dst_ref=tile_in.at[step],
            send_sem=tile_send.at[step],
            recv_sem=tile_recv.at[step],
            device_id=(w, to),
            device_id_type=MESH,
        )

    def wide_copy(step):
        to = lax.rem(w + step, wide_count)
        return pltpu.make_async_remote_copy(
            src_ref=table_out,
            dst_ref=table_in.at[w],
            send_sem=spread_send.at[step],
            recv_sem=spread_recv.at[step],
            device_id=(to, n),
            device_id_type=MESH,
        )

    for step in range(1, narrow_count):
        narrow_copy(step).start()
    part_ref[...] = jnp.zeros_like(part_ref)
    fixed = (meta_ref, cells_ref, off_ref, tz_ref, part_ref, offcol, m_high, m_low, h_high, h_low)
    interpolate(sizes, -1, *fixed)
    tile = tile_out[...]
    for step in range(1, narrow_count):
        narrow_copy(step).wait_recv()
        tile = tile + tile_in[step]
    table_out[...] = tile
    table_in[w] = tile

    def begin(step, carry):
        wide_copy(step).start()
        return carry

    lax.fori_loop(1, wide_count, begin, 0)

    interpolate(sizes, 0, *fixed)
    copies = []
    for place, (dw, dn) in enumerate(PARTIAL):
        if (dw, dn) == (0, 0):
            continue
        copy = pltpu.make_async_remote_copy(
            src_ref=part_ref.at[place],
            dst_ref=part_in.at[place],
            send_sem=part_send.at[place],
            recv_sem=part_recv.at[place],
            device_id=device(dw, dn),
            device_id_type=MESH,
        )
        copy.start()
        copies.append((place, copy))
    def end(step, carry):
        wide_copy(step).wait_recv()
        return carry

    lax.fori_loop(1, wide_count, end, 0)
    spread_means = jnp.transpose(table_in[...].reshape(devices, 128))
    hydro = jnp.zeros((16, devices), F32)
    for p, (dw, dn) in enumerate(PARTIAL):
        moved_means = shift_wide(spread_means[p * 16 : p * 16 + 16], dw, narrow_count)
        hydro = hydro + shift_narrow(moved_means, dn, narrow_count)

    gap = fields[160:192, :]

    def totals():
        def one_contact(i, sums):
            return sums + edges[i] * forces[pl.ds(i, 1), :]

        loads[...] = lax.fori_loop(
            0, CONT_DEV, one_contact, jnp.zeros((EDGE_ROWS, devices), F32), unroll=4
        )
        result = jnp.zeros((ROWS_DEV, devices), F32)
        for dn in (-1, 0, 1):
            inner = jnp.zeros((ROWS_DEV, devices), F32)
            for dw in (-1, 0, 1):
                start = AROUND.index((dw, dn)) * ROWS_DEV
                inner = inner + shift_wide(loads[start : start + ROWS_DEV, :], dw, narrow_count)
            result = result + shift_narrow(inner, dn, narrow_count)
        return jnp.concatenate([result, jnp.zeros((16 - ROWS_DEV, devices), F32)], axis=0)

    def sweep(turn, moving):
        for dn in (-1, 0, 1):
            beside = shift_narrow(moving, -dn, narrow_count)
            for dw in (-1, 0, 1):
                start = AROUND.index((dw, dn)) * ROWS_DEV
                around[start : start + ROWS_DEV, :] = shift_wide(beside, -dw, narrow_count)[:ROWS_DEV]

        def eight_contacts(block, carry):
            rows = [
                jnp.sum(edges[block * 8 + i] * around[...], axis=0, keepdims=True) for i in range(8)
            ]
            at = pl.ds(pl.multiple_of(block * 8, 8), 8)
            relatives[at, :] = jnp.concatenate(rows, axis=0)
            return carry

        lax.fori_loop(0, CONT_DEV // 8, eight_contacts, 0)
        forces[...] = jnp.maximum(
            forces[...]
            - relaxation * (gap + time_step * relatives[...]) / (2.0 * time_step * mobility),
            0.0,
        )
        return hydro + mobility * totals()

    around[...] = jnp.zeros_like(around)
    forces[...] = jnp.zeros_like(forces)
    moving = lax.fori_loop(0, SWEEPS, sweep, hydro)
    force = forces[...]
    mine = lanes_of((1, devices)) == w * narrow_count + n
    own_force = jnp.sum(jnp.where(mine, force, 0.0), axis=1, keepdims=True)
    force_ref[...] = jnp.broadcast_to(own_force, (CONT_DEV, 128))
    own_moving = jnp.sum(jnp.where(mine, moving, 0.0), axis=1, keepdims=True)
    row = lax.broadcasted_iota(jnp.int32, (16, 128), 0)
    centre = jnp.zeros((16, 128), F32)
    for k in range(ROWS_DEV):
        centre = jnp.where(row == k, meta_ref[GATHER.index((0, 0)), k], centre)
    moved_ref[...] = centre + time_step * own_moving
    velocity = part_ref[own] + near_ref[...]
    for place, copy in copies:
        copy.wait_recv()
        velocity = velocity + part_in[place]
    velocity_ref[...] = velocity
    for place, copy in copies:
        copy.wait_send()
    for half in (0, 1):
        wide_return[half].sent()
    for step in range(1, narrow_count):
        narrow_copy(step).wait_send()

    def finish(step, carry):
        wide_copy(step).wait_send()
        return carry

    lax.fori_loop(1, wide_count, finish, 0)


def local(
    wide_count,
    narrow_count,
    tractions,
    centers,
    node_offsets,
    occupied,
    anchors,
    near_list,
    contact_pairs,
    contact_gap,
    contact_angles,
):
    w, n = lax.axis_index("wide"), lax.axis_index("narrow")
    sizes = (wide_count, narrow_count)
    shape = jax.ShapeDtypeStruct
    dma = pltpu.SemaphoreType.DMA

    held, metas, cells = pl.pallas_call(
        functools.partial(gather_kernel, *sizes),
        out_shape=(shape((12, 16, NODES), F32), shape((12, 128), F32), shape((12, 128), jnp.int32)),
        in_specs=[VMEM_SPEC, SMEM_SPEC, SMEM_SPEC, SMEM_SPEC],
        out_specs=(VMEM_SPEC,) * 3,
        scratch_shapes=[
            pltpu.VMEM((16, NODES), F32),
            pltpu.VMEM((12, 16, NODES), F32),
            dma((12,)),
            dma((12,)),
        ],
        compiler_params=params(0),
        name="gather",
    )(tractions, centers, anchors, occupied)

    table_z = trig_table(2)
    wrapped_z = np.concatenate([table_z, table_z[:, :32]], axis=1).T.astype(np.float32).reshape(36, 8, GRID)
    table_x = trig_table(16)
    table_y = trig_table(128)
    turned_x = np.ascontiguousarray(table_x.T)
    turned_y = np.ascontiguousarray(table_y.T)
    tables = np.stack([*halves(table_x), *halves(turned_x), *halves(turned_y)])
    devices = wide_count * narrow_count
    velocity, force, moved = pl.pallas_call(
        functools.partial(flow_kernel, *sizes),
        out_shape=(shape((16, NODES), F32), shape((CONT_DEV, 128), F32), shape((16, 128), F32)),
        in_specs=[SMEM_SPEC] * 3 + [VMEM_SPEC] * 6 + [HBM_SPEC],
        out_specs=(VMEM_SPEC,) * 3,
        scratch_shapes=[
            pltpu.VMEM((16, NODES), F32),
            pltpu.VMEM((768, GRID), BF16),
            pltpu.VMEM((768, GRID), BF16),
            pltpu.VMEM((384, GRID), BF16),
            pltpu.VMEM((384, GRID), BF16),
            pltpu.VMEM((12, 256, GRID), F32),
            pltpu.VMEM((12, 128, GRID), F32),
            pltpu.VMEM((6, 16, NODES), F32),
            pltpu.VMEM((6, 16, NODES), F32),
            pltpu.VMEM((6, 16, NODES), F32),
            pltpu.VMEM((8, 128), F32),
            pltpu.VMEM((8, 8, 128), F32),
            pltpu.VMEM((8, 128), F32),
            pltpu.VMEM((32, 8, 128), F32),
            pltpu.VMEM((CONT_DEV, EDGE_ROWS, devices), F32),
            pltpu.VMEM((NODES, devices), F32),
            pltpu.VMEM((EDGE_ROWS, devices), F32),
            pltpu.VMEM((EDGE_ROWS, devices), F32),
            pltpu.VMEM((CONT_DEV, devices), F32),
            pltpu.VMEM((CONT_DEV, devices), F32),
            dma((6,)),
            dma((6,)),
            dma((8,)),
            dma((8,)),
            dma((32,)),
            dma((32,)),
            pltpu.VMEM((2, 768, NODES), BF16),
            pltpu.VMEM((2, 768, NODES), BF16),
            pltpu.VMEM((768, GRID), F32),
            pltpu.VMEM((GRID * 8, 128), F32),
            pltpu.VMEM((32, 2, 8, 384), F32),
            pltpu.VMEM((32, 2, 8, 384), F32),
            pltpu.VMEM((8, 2, 32, 384), F32),
            pltpu.VMEM((8, 2, 32, 384), F32),
            pltpu.VMEM((8, 2, 32, 384), F32),
            pltpu.VMEM((8, 2, 32, 384), F32),
            pltpu.VMEM((32, 2, 8, 384), F32),
            pltpu.VMEM((32, 2, 8, 384), F32),
            pltpu.VMEM((256, 1024), F32),
            pltpu.VMEM((256, 768), F32),
            pltpu.VMEM((6, 256, 256), BF16),
            pltpu.VMEM((2, 1024, 768), BF16),
            pltpu.VMEM((2, 768, 1024), BF16),
            pltpu.VMEM((3, NODES, 128), F32),
            pltpu.VMEM((3, 8, NODES), F32),
            pltpu.VMEM((NODES, 8), F32),
            pltpu.VMEM((8, NODES), F32),
            pltpu.VMEM((8, 8, NODES), F32),
            pltpu.VMEM((8, NODES), F32),
            pltpu.VMEM((32, 8, NODES), F32),
            dma((2, 2, 32)),
            dma((2, 2, 32)),
            dma((2, 2, 8)),
            dma((2, 2, 8)),
            dma,
            dma((8,)),
            dma((8,)),
            dma((32,)),
            dma((32,)),
        ],
        compiler_params=params(1, 56),
        name="flow",
    )(
        near_list,
        metas,
        cells,
        held,
        node_offsets,
        wrapped_z,
        contact_pairs,
        contact_gap,
        contact_angles,
        tables,
    )
    return (
        velocity[:12].reshape(2, 2, 3, NODES),
        force[:, 0],
        moved[:12, 0].reshape(2, 2, 3),
    )


def solution(mesh):
    placed = (
        P("wide", "narrow", None, None),
        P("wide", "narrow", None),
        P(),
        P("wide", "narrow"),
        P("wide", "narrow", None),
        P("wide", "narrow", None),
        P(None, ("wide", "narrow")),
        P(("wide", "narrow")),
        P(None, ("wide", "narrow")),
    )
    return jax.shard_map(
        functools.partial(local, mesh.shape["wide"], mesh.shape["narrow"]),
        mesh=mesh,
        in_specs=placed,
        out_specs=(
            P("wide", "narrow", None, None),
            P(("wide", "narrow")),
            P("wide", "narrow", None),
        ),
        check_vma=False,
    )
```

```python
import functools

import jax
import jax.numpy as jnp
import ml_dtypes
import numpy as np
from jax import lax
from jax.experimental import pallas as pl
from jax.experimental.pallas import tpu as pltpu
from jax.sharding import PartitionSpec as P

NODES = 256
GRID = 256
BLOCK = 16
NEAR = 2
SWEEPS = 6
SLOTS_DEV = 4
ROWS_DEV = 3 * SLOTS_DEV
CONT_DEV = 32
EDGE_ROWS = 112

soften = 1.0
screen = 0.0625
near_scale = 0.05
spread_norm = 0.17958712212516656
mobility = 0.2
time_step = 0.5
relaxation = 0.35
ewald_split = 0.5

MESH = pl.DeviceIdType.MESH
F32 = jnp.float32
BF16 = jnp.bfloat16
VMEM_SPEC = pl.BlockSpec(memory_space=pltpu.VMEM)
HBM_SPEC = pl.BlockSpec(memory_space=pltpu.HBM)
SMEM_SPEC = pl.BlockSpec(memory_space=pltpu.SMEM)


def params(collective_id=None, limit=40):
    if collective_id is None:
        return pltpu.CompilerParams(vmem_limit_bytes=limit * 2**20)
    return pltpu.CompilerParams(
        vmem_limit_bytes=limit * 2**20, collective_id=collective_id, has_side_effects=True
    )


def trig_table(group):
    cell = np.arange(GRID)
    rows = []
    for first in range(0, GRID // 2, group):
        for half in (0, 1):
            for k in range(first, first + group):
                angle = 2.0 * np.pi / GRID * (k * cell % GRID)
                if half == 0:
                    rows.append(np.cos(angle))
                elif k == 0:
                    rows.append(np.cos(np.pi * cell))
                else:
                    rows.append(np.sin(angle))
    return np.stack(rows)


def halves(table):
    high = table.astype(np.float32).astype(ml_dtypes.bfloat16)
    low = (table - high.astype(np.float64)).astype(np.float32).astype(ml_dtypes.bfloat16)
    return high, low


def split(values):
    high = values.astype(BF16)
    return high, (values - high.astype(F32)).astype(BF16)


def dot(a, b, contract=((1,), (0,))):
    return lax.dot_general(a, b, (contract, ((), ())), preferred_element_type=F32)


def dot3(a, b):
    return dot(
        jnp.concatenate([a[0], a[0], a[1]], axis=1), jnp.concatenate([b[0], b[1], b[0]], axis=0)
    )


def lanes_of(shape):
    return lax.broadcasted_iota(jnp.int32, shape, len(shape) - 1)


def roll(values, shift):
    return pltpu.roll(values, shift, len(values.shape) - 1)


def pack_lanes(u0, u1, u2, u3):
    lane = lanes_of(u0.shape)
    r1, r2, r3 = roll(u1, 96), roll(u2, 64), roll(u3, 32)
    return (
        jnp.where(lane < 96, u0, r1),
        jnp.where(lane < 64, r1, r2),
        jnp.where(lane < 32, r2, r3),
    )


def unpack_lanes(p0, p1, p2):
    lane = lanes_of(p0.shape)
    return (
        p0,
        roll(jnp.where(lane < 64, p1, p0), 32),
        roll(jnp.where(lane < 32, p2, p1), 64),
        roll(p2, 96),
    )


def hail(wide_count, narrow_count, offsets):
    w, n = lax.axis_index("wide"), lax.axis_index("narrow")
    for dw, dn in offsets:
        pl.semaphore_signal(
            pltpu.get_barrier_semaphore(),
            inc=1,
            device_id=(
                lax.rem(w + dw + wide_count, wide_count),
                lax.rem(n + dn + narrow_count, narrow_count),
            ),
            device_id_type=MESH,
        )


def hear(offsets):
    pl.semaphore_wait(pltpu.get_barrier_semaphore(), len(offsets))


GATHER = [(dw, dn) for dw in (-2, -1, 0, 1) for dn in (-1, 0, 1)]


def gather_kernel(
    wide_count,
    narrow_count,
    tractions_ref,
    centres_ref,
    anchors_ref,
    occupied_ref,
    out_ref,
    meta_ref,
    cells_ref,
    own_ref,
    held,
    send_sem,
    recv_sem,
):
    w, n = lax.axis_index("wide"), lax.axis_index("narrow")
    reach = [(dw, dn) for dw in (-2, -1, 0, 1, 2) for dn in (-1, 0, 1) if (dw, dn) != (0, 0)]
    hail(wide_count, narrow_count, reach)
    slots = [(a, b) for a in (0, 1) for b in (0, 1)]
    numbers = [centres_ref[a, b, c] for a, b in slots for c in range(3)]
    numbers += [anchors_ref[a, b, c].astype(F32) for a, b in slots for c in range(3)]
    numbers += [occupied_ref[a, b].astype(F32) for a, b in slots]
    lane = lanes_of((1, NODES))
    line = jnp.zeros((1, NODES), F32)
    for place, number in enumerate(numbers):
        line = jnp.where(lane == place, number, line)
    for s, (a, b) in enumerate(slots):
        own_ref[3 * s : 3 * s + 3, :] = tractions_ref[a, b]
    own_ref[12:16, :] = jnp.broadcast_to(line, (4, NODES))
    hear(reach)
    copies = []
    for place, (dw, dn) in enumerate(GATHER):
        if (dw, dn) == (0, 0):
            continue
        copy = pltpu.make_async_remote_copy(
            src_ref=own_ref,
            dst_ref=held.at[place],
            send_sem=send_sem.at[place],
            recv_sem=recv_sem.at[place],
            device_id=(
                lax.rem(w - dw + wide_count, wide_count),
                lax.rem(n - dn + narrow_count, narrow_count),
            ),
            device_id_type=MESH,
        )
        copy.start()
        copies.append((place, copy))
    own = GATHER.index((0, 0))
    out_ref[own] = own_ref[...]
    meta_ref[own : own + 1, :] = own_ref[12:13, 0:128]
    cells_ref[own : own + 1, :] = own_ref[12:13, 0:128].astype(jnp.int32)
    for place, copy in copies:
        copy.wait_recv()
        out_ref[place] = held[place]
        meta_ref[place : place + 1, :] = held[place, 12:13, 0:128]
        cells_ref[place : place + 1, :] = held[place, 12:13, 0:128].astype(jnp.int32)
    for place, copy in copies:
        copy.wait_send()


def near_field(slots, sizes, list_ref, meta_ref, held_ref, off_ref, out_ref, offcol, source, columns):
    wide_count, narrow_count = sizes
    w, n = lax.axis_index("wide"), lax.axis_index("narrow")
    own = GATHER.index((0, 0))
    columns[...] = jnp.zeros_like(columns)
    for s in slots:
        for j in range(1 + NEAR):
            if j == 0:
                place, within = own, s
            else:
                entry = list_ref[s // 2, s % 2, j - 1]
                holder = entry // SLOTS_DEV
                within = entry % SLOTS_DEV
                row = lax.rem(holder // narrow_count - w + 1 + wide_count, wide_count)
                column = lax.rem(lax.rem(holder, narrow_count) - n + 1 + narrow_count, narrow_count)
                place = (jnp.minimum(row, 2) + 1) * 3 + jnp.minimum(column, 2)
            for c in range(3):
                if j == 0:
                    shift = 0.0
                else:
                    e = meta_ref[own, 3 * s + c] - meta_ref[place, 3 * within + c]
                    shift = e - jnp.where(e >= 128.0, 256.0, jnp.where(e < -128.0, -256.0, 0.0))
                source[j, c : c + 1, :] = shift - off_ref[c : c + 1, :]
                source[j, 3 + c : 4 + c, :] = held_ref[place, pl.ds(within * 3 + c, 1), :]

        def chunk(i, carry):
            for part in (0, 1):
                rows = pl.ds(pl.multiple_of(i * 16 + part * 8, 8), 8)
                sums = [jnp.zeros((8, 128), F32) for _ in range(3)]
                at = [offcol[c, rows, :] for c in range(3)]
                for j in range(1 + NEAR):
                    for half in (0, 1):
                        lanes = slice(half * 128, half * 128 + 128)
                        d = [at[c] + source[j, c : c + 1, lanes] for c in range(3)]
                        f = [source[j, 3 + c : 4 + c, lanes] for c in range(3)]
                        r2 = d[0] * d[0] + d[1] * d[1] + d[2] * d[2]
                        inverse = lax.rsqrt(r2 + soften)
                        weight = jnp.exp(r2 * (-screen)) * (inverse * inverse * inverse)
                        along = (d[0] * f[0] + d[1] * f[1] + d[2] * f[2]) * weight
                        diagonal = (r2 + 2.0 * soften) * weight
                        for c in range(3):
                            sums[c] = sums[c] + (diagonal * f[c] + d[c] * along)
                for c in range(3):
                    columns[rows, c : c + 1] = jnp.sum(sums[c], axis=1, keepdims=True)
            return carry

        lax.fori_loop(0, NODES // 16, chunk, 0)
        result = jnp.transpose(columns[...])
        alive = jnp.where(meta_ref[own, 24 + s] > 0.5, near_scale, 0.0)
        out_ref[3 * s : 3 * s + 3, :] = alive * result[0:3, :]


def columns_of(off_ref, offcol):
    padded = jnp.concatenate([off_ref[...], jnp.zeros((5, NODES), F32)], axis=0)
    turned = jnp.transpose(padded)
    for c in range(3):
        offcol[c] = jnp.broadcast_to(turned[:, c : c + 1], (NODES, 128))


def sphere_weights(sizes, dw, dn, s, meta_ref, cells_ref, off_ref, offcol, tz_ref):
    wide_count, narrow_count = sizes
    w, n = lax.axis_index("wide"), lax.axis_index("narrow")
    size_x, size_y = GRID // wide_count, GRID // narrow_count
    place = (dw + 2) * 3 + dn + 1
    anchor = [cells_ref[place, 12 + 3 * s + c] for c in range(3)]
    centre = [meta_ref[place, 3 * s + c] for c in range(3)]
    alive = jnp.where(meta_ref[place, 24 + s] > 0.5, spread_norm, 0.0)
    low_x = anchor[0] - size_x * lax.rem(w + dw + wide_count, wide_count) + size_x * dw
    low_y = anchor[1] - size_y * lax.rem(n + dn + narrow_count, narrow_count) + size_y * dn
    low_z = anchor[2] % 8

    def weights(cell, position, base, low, factor):
        distance = position - (base + cell).astype(F32)
        inside = (cell >= low) & (cell < low + BLOCK)
        return jnp.where(inside, jnp.exp(-distance * distance) * factor, 0.0)

    def rows(c, low, count, factor):
        cell = lax.broadcasted_iota(jnp.int32, (count, NODES), 0)
        return weights(cell, centre[c] + off_ref[c : c + 1, :], anchor[c] - low, low, factor)

    lane = lanes_of((NODES, 128))
    wz = weights(lane % 32, centre[2] + offcol[2], anchor[2] - low_z, low_z, 1.0)
    high = wz.astype(BF16).astype(F32)
    left = jnp.where(lane < 64, high, jnp.where(lane < 96, wz - high, 0.0)).astype(BF16)
    tile = anchor[2] // 8
    t_high, t_low = split(jnp.concatenate([tz_ref[tile + t] for t in range(4)], axis=0))
    right = jnp.concatenate([t_high, t_low, t_high, jnp.zeros((32, GRID), BF16)], axis=0)
    along_z = split(dot(left, right))
    return place, rows(0, low_x, size_x, alive), rows(1, low_y, 16 if dn else size_y, 1.0), along_z


def pair_loop(body, dn, unroll=1):
    def step(index, carry):
        body(index // 2 - 2, dn, index % 2)
        return carry

    lax.fori_loop(0, 6, step, 0, unroll=unroll)


def spread(sizes, meta_ref, cells_ref, held_ref, off_ref, tz_ref, out_ref, offcol, a_high, a_low, total, turned):
    total[...] = jnp.zeros_like(total)

    def pair(dw, dn, which):
        span = 16 if dn else 32
        sums = []
        for member in (0, 1):
            s = 2 * which + member
            place, wx, wy, along_z = sphere_weights(sizes, dw, dn, s, meta_ref, cells_ref, off_ref, offcol, tz_ref)
            planar = jnp.concatenate(
                [wy * held_ref[place, pl.ds(s * 3 + c, 1), :] for c in range(3)], axis=0
            )
            size = 3 * span
            for x in range(8):
                high, low = split(planar * wx[x : x + 1, :])
                a_high[member, x * size : x * size + size, :] = high
                a_low[member, x * size : x * size + size, :] = low
            rows = slice(0, 8 * size)
            sums.append(dot3((a_high[member, rows, :], a_low[member, rows, :]), along_z))
        both = sums[0] + sums[1]
        if dn == 0:
            total[...] += both
        else:
            for block in range(24):
                total[block * 32 : block * 32 + 16, :] += both[block * 16 : block * 16 + 16]

    pair_loop(pair, -1)
    pair_loop(pair, 0)
    for x in range(8):
        block = jnp.concatenate([total[x * 96 : x * 96 + 96, :], jnp.zeros((32, GRID), F32)], axis=0)
        turned[pl.ds(x, GRID, stride=8), :] = jnp.transpose(block)
    values = turned[...].reshape(64, 4, 8, 128)
    packed = pack_lanes(*[values[:, j] for j in range(4)])
    for g in range(3):
        out_ref[:, :, :, g * 128 : g * 128 + 128] = packed[g].reshape(32, 2, 8, 128)


def mean_weights(sizes, meta_ref, cells_ref, off_ref, tz_ref, offcol, full, half):
    def pair(dw, dn, which):
        span = 16 if dn else 32
        for member in (0, 1):
            s = 2 * which + member
            place, wx, wy, along_z = sphere_weights(
                sizes, dw, dn, s, meta_ref, cells_ref, off_ref, offcol, tz_ref
            )
            wy = wy * (1.0 / NODES)
            left = split(jnp.concatenate([wy * wx[x : x + 1, :] for x in range(8)], axis=0))
            target = half if dn else full
            target[(dw + 2) * 4 + s] = dot3(left, along_z)

    pair_loop(pair, -1)
    pair_loop(pair, 0)


def mean_velocities(values, full, half, rows_ref):
    rows_ref[...] = jnp.zeros_like(rows_ref)
    for dn in (-1, 0):
        span = 16 if dn else 32

        def sphere(index, carry):
            source = half if dn else full
            tiles = [jnp.zeros((8, GRID), F32) for _ in range(3)]
            for x in range(8):
                for y in range(0, span, 8):
                    weight = source[index, x * span + y : x * span + y + 8, :]
                    for c in range(3):
                        at = x * 96 + c * 32 + y
                        tiles[c] = tiles[c] + values[at : at + 8, :] * weight
            piece = (index // 4) * 2 + dn + 1
            for c in range(3):
                rows_ref[piece, pl.ds((index % 4) * 3 + c, 1), :] = jnp.sum(tiles[c], axis=0, keepdims=True)
            return carry

        lax.fori_loop(0, 12, sphere, 0)


def unpack_mesh(mesh_ref, values, m_high, m_low, h_high, h_low, turned):
    groups = [mesh_ref[:, :, :, g * 128 : g * 128 + 128].reshape(64, 8, 128) for g in range(3)]
    unpacked = unpack_lanes(*groups)
    turned[...] = jnp.stack(unpacked, axis=1).reshape(GRID * 8, 128)
    for x in range(8):
        block = jnp.transpose(turned[pl.ds(x, GRID, stride=8), :])[:96]
        values[x * 96 : x * 96 + 96, :] = block
        high, low = split(block)
        m_high[x * 96 : x * 96 + 96, :] = high
        m_low[x * 96 : x * 96 + 96, :] = low
        for c in range(3):
            target = slice(x * 48 + c * 16, x * 48 + c * 16 + 16)
            h_high[target, :] = high[c * 32 : c * 32 + 16]
            h_low[target, :] = low[c * 32 : c * 32 + 16]


def interpolate(
    sizes, lower, meta_ref, cells_ref, off_ref, tz_ref, out_ref, offcol, m_high, m_low, h_high, h_low
):
    def pair(dw, dn, which):
        span = 16 if dn else 32
        size = 3 * span
        for member in (0, 1):
            s = 2 * which + member
            place, wx, wy, along_z = sphere_weights(sizes, dw, dn, s, meta_ref, cells_ref, off_ref, offcol, tz_ref)
            left = (h_high[...], h_low[...]) if dn else (m_high[...], m_low[...])
            turn = ((1,), (1,))
            found = dot(
                jnp.concatenate([left[0], left[0], left[1]], axis=1),
                jnp.concatenate([along_z[0], along_z[1], along_z[0]], axis=1),
                turn,
            )
            summed = found[0:size] * wx[0:1, :]
            for x in range(1, 8):
                summed = summed + found[x * size : x * size + size] * wx[x : x + 1, :]
            owner = (dw + 2) * 2 + dn + 1
            for c in range(3):
                out_ref[owner, pl.ds(s * 3 + c, 1), :] = jnp.sum(
                    summed[c * span : c * span + span] * wy, axis=0, keepdims=True
                )

    pair_loop(pair, lower, 2)


AROUND = [(dw, dn) for dw in (-1, 0, 1) for dn in (-1, 0, 1)]
PARTIAL = [(dw, dn) for dw in (-2, -1, 0) for dn in (-1, 0)]


def shift_narrow(values, dn, narrow_count):
    if dn == 0:
        return values
    place = lanes_of(values.shape) % narrow_count
    edge = 0 if dn == 1 else narrow_count - 1
    total = values.shape[-1]
    return jnp.where(
        place == edge,
        roll(values, (dn - dn * narrow_count) % total),
        roll(values, dn % total),
    )


def shift_wide(values, dw, narrow_count):
    if dw == 0:
        return values
    return roll(values, (dw * narrow_count) % values.shape[-1])


class Exchange:
    def __init__(self, axis, count, source, target, half, send_sem, recv_sem, me, other):
        self.__dict__.update(locals())

    def copy_to(self, step):
        to = lax.rem(self.me + step, self.count)
        return pltpu.make_async_remote_copy(
            src_ref=self.source.at[to, self.half],
            dst_ref=self.target.at[self.me, self.half],
            send_sem=self.send_sem.at[step],
            recv_sem=self.recv_sem.at[step],
            device_id=(to, self.other) if self.axis == "wide" else (self.other, to),
            device_id_type=MESH,
        )

    def begin(self):
        def step(index, carry):
            self.copy_to(index).start()
            return carry

        lax.fori_loop(1, self.count, step, 0)
        self.target[self.me, self.half] = self.source[self.me, self.half]

    def arrive(self):
        def step(index, carry):
            self.copy_to(index).wait_recv()
            return carry

        lax.fori_loop(1, self.count, step, 0)

    def sent(self):
        def step(index, carry):
            self.copy_to(index).wait_send()
            return carry

        lax.fori_loop(1, self.count, step, 0)


def flow_kernel(
    wide_count,
    narrow_count,
    list_ref,
    meta_ref,
    cells_ref,
    held_ref,
    off_ref,
    tz_ref,
    pairs_ref,
    gap_ref,
    angles_ref,
    tables,
    velocity_ref,
    force_ref,
    moved_ref,
    near_ref,
    m_high,
    m_low,
    h_high,
    h_low,
    full_means,
    half_means,
    mean_rows,
    part_ref,
    part_in,
    tile_out,
    tile_in,
    table_out,
    table_in,
    edges,
    fields,
    around,
    loads,
    relatives,
    forces,
    part_send,
    part_recv,
    tile_send,
    tile_recv,
    spread_send,
    spread_recv,
    a_high,
    a_low,
    total,
    turned,
    mesh_ref,
    wide_in,
    narrow_out,
    narrow_in,
    narrow_back,
    narrow_home,
    wide_back,
    wide_home,
    lines,
    spectrum,
    t_x,
    t_yf,
    t_yi,
    offcol,
    source,
    columns,
    own_line,
    lines_in,
    column_out,
    column_in,
    wide_send,
    wide_recv,
    narrow_send,
    narrow_recv,
    table_sem,
    line_send,
    line_recv,
    column_send,
    column_recv,
):
    w, n = lax.axis_index("wide"), lax.axis_index("narrow")
    load = pltpu.make_async_copy(tables, t_x, table_sem)
    load.start()
    reach = (
        [(step, 0) for step in range(1, wide_count)]
        + [(0, step) for step in range(1, narrow_count)]
        + [(-2, -1), (-1, -1), (2, 1), (1, 1)]
    )
    sizes = (wide_count, narrow_count)
    hail(*sizes, reach)
    columns_of(off_ref, offcol)
    spread(sizes, meta_ref, cells_ref, held_ref, off_ref, tz_ref, mesh_ref, offcol, a_high, a_low, total, turned)
    hear(reach)

    def exchanges(axis, source, target, way):
        if axis == "wide":
            fixed = (wide_count, w, n, wide_send, wide_recv)
        else:
            fixed = (narrow_count, n, w, narrow_send, narrow_recv)
        count, me, other, send_sem, recv_sem = fixed
        return [
            Exchange(
                axis, count, source, target, half, send_sem.at[way, half], recv_sem.at[way, half], me, other
            )
            for half in (0, 1)
        ]

    wide_go = exchanges("wide", mesh_ref, wide_in, 0)
    narrow_go = exchanges("narrow", narrow_out, narrow_in, 0)
    narrow_return = exchanges("narrow", narrow_back, narrow_home, 1)
    wide_return = exchanges("wide", wide_back, wide_home, 1)
    for half in (0, 1):
        wide_go[half].begin()

    ids = pairs_ref[...]
    within = (ids % SLOTS_DEV).astype(F32)
    holder = ids // SLOTS_DEV
    row_w = lax.rem(holder // narrow_count - w + 1 + wide_count, wide_count)
    row_n = lax.rem(lax.rem(holder, narrow_count) - n + 1 + narrow_count, narrow_count)
    seconds = ((row_w * 3 + row_n) * SLOTS_DEV).astype(F32) + within
    polar, azimuth = angles_ref[0:1, :], angles_ref[1:2, :]
    across = jnp.sin(polar)
    parts = [
        within[0:1],
        seconds[1:2],
        across * jnp.cos(azimuth),
        across * jnp.sin(azimuth),
        jnp.cos(polar),
        gap_ref[...].reshape(1, CONT_DEV),
    ]
    line = jnp.concatenate(parts + [jnp.zeros((1, 64), F32)], axis=1)
    own_line[...] = jnp.where(lax.broadcasted_iota(jnp.int32, (8, NODES), 0) == n, line, 0.0)

    def line_copy(step):
        return pltpu.make_async_remote_copy(
            src_ref=own_line,
            dst_ref=lines_in.at[step],
            send_sem=line_send.at[step],
            recv_sem=line_recv.at[step],
            device_id=(w, lax.rem(n + step, narrow_count)),
            device_id_type=MESH,
        )

    def column_copy(step):
        return pltpu.make_async_remote_copy(
            src_ref=column_out,
            dst_ref=column_in.at[w],
            send_sem=column_send.at[step],
            recv_sem=column_recv.at[step],
            device_id=(lax.rem(w + step, wide_count), n),
            device_id_type=MESH,
        )

    for step in range(1, narrow_count):
        line_copy(step).start()
    near_ref[...] = jnp.zeros_like(near_ref)
    near_field(
        (0, 1), sizes, list_ref, meta_ref, held_ref, off_ref, near_ref, offcol, source, columns
    )
    mean_weights(sizes, meta_ref, cells_ref, off_ref, tz_ref, offcol, full_means, half_means)
    load.wait()
    t_yf[...] = jnp.zeros_like(t_yf)
    for part in (0, 1):
        for piece in range(8):
            for c in range(3):
                t_yf[part, piece * 128 + c * 32 : piece * 128 + c * 32 + 32, c * 256 : c * 256 + 256] = t_x[
                    4 + part, piece * 32 : piece * 32 + 32, :
                ]
        for piece in range(8):
            for c in range(3):
                block = t_yf[part, piece * 128 : piece * 128 + 128, c * 256 : c * 256 + 256]
                t_yi[part, c * 256 : c * 256 + 256, piece * 128 : piece * 128 + 128] = jnp.transpose(
                    block.astype(F32)
                ).astype(BF16)
    for half in (0, 1):
        wide_go[half].arrive()
        block = split(wide_in[:, half].reshape(GRID, 384))
        along = dot3((t_x[0], t_x[1]), block)
        narrow_out[:, half] = along.reshape(narrow_count, 32, 384)
        narrow_go[half].begin()
    column = own_line[...]
    for step in range(1, narrow_count):
        line_copy(step).wait_recv()
        column = column + lines_in[step]
    column_out[...] = column
    column_in[w] = column

    def begin_column(step, carry):
        column_copy(step).start()
        return carry

    lax.fori_loop(1, wide_count, begin_column, 0)
    row = lax.broadcasted_iota(jnp.int32, (32, 1), 0)
    k_x = (n * 16 + row % 16).astype(F32)
    nyquist_x = jnp.where((row >= 16) & (k_x < 0.5), 128.0, 0.0)
    lane = lax.broadcasted_iota(jnp.int32, (1, GRID), 1)
    k_y = (lane % 128).astype(F32)
    nyquist_y = jnp.where((lane >= 128) & (k_y < 0.5), 128.0, 0.0)
    square_xy = k_x * k_x + nyquist_x * nyquist_x + (k_y * k_y + nyquist_y * nyquist_y)
    scale_x = jnp.where(k_x < 0.5, 1.0, 2.0)
    scale_y = jnp.where(k_y < 0.5, 1.0, 2.0)
    scale_xy = scale_x * scale_y
    damping = (ewald_split * np.pi / GRID) ** 2
    constant = GRID * GRID / (4.0 * np.pi * np.pi) / float(GRID) ** 3
    turn_x = jnp.where(row < 16, k_x, -k_x)
    turn_y = jnp.where(lane < 128, k_y, -k_y)

    def derive_x(values):
        return turn_x * jnp.concatenate([values[16:], values[:16]], axis=0)

    def derive_y(values):
        return turn_y * jnp.concatenate([values[:, 128:], values[:, :128]], axis=1)

    def filtered(index, group):
        k_z = (w * 4 + group * 2 + index).astype(F32)
        bases = [pl.multiple_of(group * 128 + half * 64 + index * 32, 32) for half in (0, 1)]
        fields = [
            [spectrum[pl.ds(bases[half], 32), c * 256 : c * 256 + 256] for c in range(3)]
            for half in (0, 1)
        ]
        flows = []
        nyquists_z = [jnp.zeros_like(k_z), jnp.where(k_z < 0.5, 128.0, 0.0)]
        scale_z = jnp.where(k_z < 0.5, 1.0, 2.0)
        turn_z = (k_z, -k_z)
        for half in (0, 1):
            values = fields[half]
            flows.append(derive_x(values[0]) + derive_y(values[1]) + turn_z[half] * fields[1 - half][2])
        for half in (0, 1):
            values = fields[half]
            nyquist_z = nyquists_z[half]
            square = square_xy + (k_z * k_z + nyquist_z * nyquist_z)
            safe = jnp.maximum(square, 1.0)
            inverse = 1.0 / safe
            factor = jnp.where(square > 0.5, jnp.exp(-damping * square) * inverse, 0.0)
            factor = factor * (scale_xy * (scale_z * constant))
            edge = (nyquist_x * values[0] + nyquist_y * values[1] + nyquist_z * values[2]) * inverse
            flow = [flows[half] * inverse, flows[1 - half] * inverse]
            gradient = [derive_x(flow[0]), derive_y(flow[0]), None]
            gradient[2] = turn_z[half] * (flows[1 - half] * inverse)
            nyquist = (nyquist_x, nyquist_y, nyquist_z)
            for c in range(3):
                spectrum[pl.ds(bases[half], 32), c * 256 : c * 256 + 256] = factor * (
                    values[c] + gradient[c] - nyquist[c] * edge
                )
        return group

    for half in (0, 1):
        narrow_go[half].arrive()
        for piece in range(8):
            groups = [narrow_in[piece, half, :, g * 128 : g * 128 + 128] for g in range(3)]
            unpacked = unpack_lanes(*groups)
            for j in range(4):
                lines[half * 128 + j * 32 : half * 128 + j * 32 + 32, piece * 128 : piece * 128 + 128] = unpacked[j]
        rows = slice(half * 128, half * 128 + 128)
        spectrum[rows, :] = dot3(split(lines[rows, :]), (t_yf[0], t_yf[1]))
        lax.fori_loop(0, 2, filtered, half)
        lines[rows, :] = dot3(split(spectrum[rows, :]), (t_yi[0], t_yi[1]))
        for target in range(8):
            groups = [
                lines[half * 128 + j * 32 : half * 128 + j * 32 + 32, target * 128 : target * 128 + 128]
                for j in range(4)
            ]
            packed = pack_lanes(*groups)
            for g in range(3):
                narrow_back[target, half, :, g * 128 : g * 128 + 128] = packed[g]
        narrow_return[half].begin()
    for half in (0, 1):
        narrow_return[half].arrive()
        block = split(narrow_home[:, half].reshape(GRID, 384))
        along = dot3((t_x[2], t_x[3]), block)
        wide_back[:, half] = along.reshape(wide_count, 8, 384)
        wide_return[half].begin()
    near_field(
        (2, 3), sizes, list_ref, meta_ref, held_ref, off_ref, near_ref, offcol, source, columns
    )
    def end_column(step, carry):
        column_copy(step).wait()
        return carry

    lax.fori_loop(1, wide_count, end_column, 0)
    for step in range(1, narrow_count):
        line_copy(step).wait_send()
    fields[...] = jnp.transpose(column_in[...].reshape(wide_count * narrow_count, NODES))
    sphere = lax.broadcasted_iota(jnp.int32, (EDGE_ROWS, 1), 0)
    component = sphere % 3
    sphere = (sphere // 3).astype(F32)

    def incidence(i, carry):
        first, second = fields[pl.ds(i, 1), :] + 4.0 * SLOTS_DEV, fields[pl.ds(32 + i, 1), :]
        normal = [fields[pl.ds(64 + 32 * c + i, 1), :] for c in range(3)]
        along = jnp.where(component == 0, normal[0], jnp.where(component == 1, normal[1], normal[2]))
        sign = jnp.where(sphere == first, 1.0, 0.0) - jnp.where(sphere == second, 1.0, 0.0)
        edges[i] = sign * along
        return carry

    lax.fori_loop(0, CONT_DEV, incidence, 0)
    for group in (wide_go, narrow_go, narrow_return):
        for half in (0, 1):
            group[half].sent()
    for half in (0, 1):
        wide_return[half].arrive()
    unpack_mesh(wide_home, total, m_high, m_low, h_high, h_low, turned)
    mean_velocities(total, full_means, half_means, mean_rows)

    def device(dw, dn):
        return (
            lax.rem(w + dw + wide_count, wide_count),
            lax.rem(n + dn + narrow_count, narrow_count),
        )

    devices = wide_count * narrow_count
    own = PARTIAL.index((0, 0))
    means = [jnp.sum(mean_rows[p], axis=1, keepdims=True) for p in range(6)]
    means[own] = means[own] + jnp.sum(near_ref[...], axis=1, keepdims=True) * (1.0 / NODES)
    column = jnp.concatenate(means + [jnp.zeros((32, 1), F32)], axis=0)
    line = jnp.transpose(jnp.broadcast_to(column, (128, 128)))[:8]
    tile_out[...] = jnp.where(lax.broadcasted_iota(jnp.int32, (8, 128), 0) == n, line, 0.0)

    def narrow_copy(step):
        to = lax.rem(n + step, narrow_count)
        return pltpu.make_async_remote_copy(
            src_ref=tile_out,
            dst_ref=tile_in.at[step],
            send_sem=tile_send.at[step],
            recv_sem=tile_recv.at[step],
            device_id=(w, to),
            device_id_type=MESH,
        )

    def wide_copy(step):
        to = lax.rem(w + step, wide_count)
        return pltpu.make_async_remote_copy(
            src_ref=table_out,
            dst_ref=table_in.at[w],
            send_sem=spread_send.at[step],
            recv_sem=spread_recv.at[step],
            device_id=(to, n),
            device_id_type=MESH,
        )

    for step in range(1, narrow_count):
        narrow_copy(step).start()
    part_ref[...] = jnp.zeros_like(part_ref)
    fixed = (meta_ref, cells_ref, off_ref, tz_ref, part_ref, offcol, m_high, m_low, h_high, h_low)
    interpolate(sizes, -1, *fixed)
    tile = tile_out[...]
    for step in range(1, narrow_count):
        narrow_copy(step).wait_recv()
        tile = tile + tile_in[step]
    table_out[...] = tile
    table_in[w] = tile

    def begin(step, carry):
        wide_copy(step).start()
        return carry

    lax.fori_loop(1, wide_count, begin, 0)

    interpolate(sizes, 0, *fixed)
    copies = []
    for place, (dw, dn) in enumerate(PARTIAL):
        if (dw, dn) == (0, 0):
            continue
        copy = pltpu.make_async_remote_copy(
            src_ref=part_ref.at[place],
            dst_ref=part_in.at[place],
            send_sem=part_send.at[place],
            recv_sem=part_recv.at[place],
            device_id=device(dw, dn),
            device_id_type=MESH,
        )
        copy.start()
        copies.append((place, copy))
    def end(step, carry):
        wide_copy(step).wait_recv()
        return carry

    lax.fori_loop(1, wide_count, end, 0)
    spread_means = jnp.transpose(table_in[...].reshape(devices, 128))
    hydro = jnp.zeros((16, devices), F32)
    for p, (dw, dn) in enumerate(PARTIAL):
        moved_means = shift_wide(spread_means[p * 16 : p * 16 + 16], dw, narrow_count)
        hydro = hydro + shift_narrow(moved_means, dn, narrow_count)

    gap = fields[160:192, :]

    def totals():
        def one_contact(i, sums):
            return sums + edges[i] * forces[pl.ds(i, 1), :]

        loads[...] = lax.fori_loop(
            0, CONT_DEV, one_contact, jnp.zeros((EDGE_ROWS, devices), F32), unroll=4
        )
        result = jnp.zeros((ROWS_DEV, devices), F32)
        for dn in (-1, 0, 1):
            inner = jnp.zeros((ROWS_DEV, devices), F32)
            for dw in (-1, 0, 1):
                start = AROUND.index((dw, dn)) * ROWS_DEV
                inner = inner + shift_wide(loads[start : start + ROWS_DEV, :], dw, narrow_count)
            result = result + shift_narrow(inner, dn, narrow_count)
        return jnp.concatenate([result, jnp.zeros((16 - ROWS_DEV, devices), F32)], axis=0)

    def sweep(turn, moving):
        for dn in (-1, 0, 1):
            beside = shift_narrow(moving, -dn, narrow_count)
            for dw in (-1, 0, 1):
                start = AROUND.index((dw, dn)) * ROWS_DEV
                around[start : start + ROWS_DEV, :] = shift_wide(beside, -dw, narrow_count)[:ROWS_DEV]

        def eight_contacts(block, carry):
            rows = [
                jnp.sum(edges[block * 8 + i] * around[...], axis=0, keepdims=True) for i in range(8)
            ]
            at = pl.ds(pl.multiple_of(block * 8, 8), 8)
            relatives[at, :] = jnp.concatenate(rows, axis=0)
            return carry

        lax.fori_loop(0, CONT_DEV // 8, eight_contacts, 0)
        forces[...] = jnp.maximum(
            forces[...]
            - relaxation * (gap + time_step * relatives[...]) / (2.0 * time_step * mobility),
            0.0,
        )
        return hydro + mobility * totals()

    around[...] = jnp.zeros_like(around)
    forces[...] = jnp.zeros_like(forces)
    moving = lax.fori_loop(0, SWEEPS, sweep, hydro)
    force = forces[...]
    mine = lanes_of((1, devices)) == w * narrow_count + n
    own_force = jnp.sum(jnp.where(mine, force, 0.0), axis=1, keepdims=True)
    force_ref[...] = jnp.broadcast_to(own_force, (CONT_DEV, 128))
    own_moving = jnp.sum(jnp.where(mine, moving, 0.0), axis=1, keepdims=True)
    row = lax.broadcasted_iota(jnp.int32, (16, 128), 0)
    centre = jnp.zeros((16, 128), F32)
    for k in range(ROWS_DEV):
        centre = jnp.where(row == k, meta_ref[GATHER.index((0, 0)), k], centre)
    moved_ref[...] = centre + time_step * own_moving
    velocity = part_ref[own] + near_ref[...]
    for place, copy in copies:
        copy.wait_recv()
        velocity = velocity + part_in[place]
    velocity_ref[...] = velocity
    for place, copy in copies:
        copy.wait_send()
    for half in (0, 1):
        wide_return[half].sent()
    for step in range(1, narrow_count):
        narrow_copy(step).wait_send()

    def finish(step, carry):
        wide_copy(step).wait_send()
        return carry

    lax.fori_loop(1, wide_count, finish, 0)


def local(
    wide_count,
    narrow_count,
    tractions,
    centers,
    node_offsets,
    occupied,
    anchors,
    near_list,
    contact_pairs,
    contact_gap,
    contact_angles,
):
    w, n = lax.axis_index("wide"), lax.axis_index("narrow")
    sizes = (wide_count, narrow_count)
    shape = jax.ShapeDtypeStruct
    dma = pltpu.SemaphoreType.DMA

    held, metas, cells = pl.pallas_call(
        functools.partial(gather_kernel, *sizes),
        out_shape=(shape((12, 16, NODES), F32), shape((12, 128), F32), shape((12, 128), jnp.int32)),
        in_specs=[VMEM_SPEC, SMEM_SPEC, SMEM_SPEC, SMEM_SPEC],
        out_specs=(VMEM_SPEC,) * 3,
        scratch_shapes=[
            pltpu.VMEM((16, NODES), F32),
            pltpu.VMEM((12, 16, NODES), F32),
            dma((12,)),
            dma((12,)),
        ],
        compiler_params=params(0),
        name="gather",
    )(tractions, centers, anchors, occupied)

    table_z = trig_table(2)
    wrapped_z = np.concatenate([table_z, table_z[:, :32]], axis=1).T.astype(np.float32).reshape(36, 8, GRID)
    table_x = trig_table(16)
    table_y = trig_table(128)
    turned_x = np.ascontiguousarray(table_x.T)
    turned_y = np.ascontiguousarray(table_y.T)
    tables = np.stack([*halves(table_x), *halves(turned_x), *halves(turned_y)])
    devices = wide_count * narrow_count
    velocity, force, moved = pl.pallas_call(
        functools.partial(flow_kernel, *sizes),
        out_shape=(shape((16, NODES), F32), shape((CONT_DEV, 128), F32), shape((16, 128), F32)),
        in_specs=[SMEM_SPEC] * 3 + [VMEM_SPEC] * 6 + [HBM_SPEC],
        out_specs=(VMEM_SPEC,) * 3,
        scratch_shapes=[
            pltpu.VMEM((16, NODES), F32),
            pltpu.VMEM((768, GRID), BF16),
            pltpu.VMEM((768, GRID), BF16),
            pltpu.VMEM((384, GRID), BF16),
            pltpu.VMEM((384, GRID), BF16),
            pltpu.VMEM((12, 256, GRID), F32),
            pltpu.VMEM((12, 128, GRID), F32),
            pltpu.VMEM((6, 16, NODES), F32),
            pltpu.VMEM((6, 16, NODES), F32),
            pltpu.VMEM((6, 16, NODES), F32),
            pltpu.VMEM((8, 128), F32),
            pltpu.VMEM((8, 8, 128), F32),
            pltpu.VMEM((8, 128), F32),
            pltpu.VMEM((32, 8, 128), F32),
            pltpu.VMEM((CONT_DEV, EDGE_ROWS, devices), F32),
            pltpu.VMEM((NODES, devices), F32),
            pltpu.VMEM((EDGE_ROWS, devices), F32),
            pltpu.VMEM((EDGE_ROWS, devices), F32),
            pltpu.VMEM((CONT_DEV, devices), F32),
            pltpu.VMEM((CONT_DEV, devices), F32),
            dma((6,)),
            dma((6,)),
            dma((8,)),
            dma((8,)),
            dma((32,)),
            dma((32,)),
            pltpu.VMEM((2, 768, NODES), BF16),
            pltpu.VMEM((2, 768, NODES), BF16),
            pltpu.VMEM((768, GRID), F32),
            pltpu.VMEM((GRID * 8, 128), F32),
            pltpu.VMEM((32, 2, 8, 384), F32),
            pltpu.VMEM((32, 2, 8, 384), F32),
            pltpu.VMEM((8, 2, 32, 384), F32),
            pltpu.VMEM((8, 2, 32, 384), F32),
            pltpu.VMEM((8, 2, 32, 384), F32),
            pltpu.VMEM((8, 2, 32, 384), F32),
            pltpu.VMEM((32, 2, 8, 384), F32),
            pltpu.VMEM((32, 2, 8, 384), F32),
            pltpu.VMEM((256, 1024), F32),
            pltpu.VMEM((256, 768), F32),
            pltpu.VMEM((6, 256, 256), BF16),
            pltpu.VMEM((2, 1024, 768), BF16),
            pltpu.VMEM((2, 768, 1024), BF16),
            pltpu.VMEM((3, NODES, 128), F32),
            pltpu.VMEM((3, 8, NODES), F32),
            pltpu.VMEM((NODES, 8), F32),
            pltpu.VMEM((8, NODES), F32),
            pltpu.VMEM((8, 8, NODES), F32),
            pltpu.VMEM((8, NODES), F32),
            pltpu.VMEM((32, 8, NODES), F32),
            dma((2, 2, 32)),
            dma((2, 2, 32)),
            dma((2, 2, 8)),
            dma((2, 2, 8)),
            dma,
            dma((8,)),
            dma((8,)),
            dma((32,)),
            dma((32,)),
        ],
        compiler_params=params(1, 56),
        name="flow",
    )(
        near_list,
        metas,
        cells,
        held,
        node_offsets,
        wrapped_z,
        contact_pairs,
        contact_gap,
        contact_angles,
        tables,
    )
    return (
        velocity[:12].reshape(2, 2, 3, NODES),
        force[:, 0],
        moved[:12, 0].reshape(2, 2, 3),
    )


def solution(mesh):
    placed = (
        P("wide", "narrow", None, None),
        P("wide", "narrow", None),
        P(),
        P("wide", "narrow"),
        P("wide", "narrow", None),
        P("wide", "narrow", None),
        P(None, ("wide", "narrow")),
        P(("wide", "narrow")),
        P(None, ("wide", "narrow")),
    )
    return jax.shard_map(
        functools.partial(local, mesh.shape["wide"], mesh.shape["narrow"]),
        mesh=mesh,
        in_specs=placed,
        out_specs=(
            P("wide", "narrow", None, None),
            P(("wide", "narrow")),
            P("wide", "narrow", None),
        ),
        check_vma=False,
    )
```

```python
import functools

import jax
import jax.numpy as jnp
import ml_dtypes
import numpy as np
from jax import lax
from jax.experimental import pallas as pl
from jax.experimental.pallas import tpu as pltpu
from jax.sharding import PartitionSpec as P

NODES = 256
GRID = 256
BLOCK = 16
NEAR = 2
SWEEPS = 6
SLOTS_DEV = 4
ROWS_DEV = 3 * SLOTS_DEV
CONT_DEV = 32
EDGE_ROWS = 112

soften = 1.0
screen = 0.0625
near_scale = 0.05
spread_norm = 0.17958712212516656
mobility = 0.2
time_step = 0.5
relaxation = 0.35
ewald_split = 0.5

MESH = pl.DeviceIdType.MESH
F32 = jnp.float32
BF16 = jnp.bfloat16
VMEM_SPEC = pl.BlockSpec(memory_space=pltpu.VMEM)
HBM_SPEC = pl.BlockSpec(memory_space=pltpu.HBM)
SMEM_SPEC = pl.BlockSpec(memory_space=pltpu.SMEM)


def params(collective_id=None, limit=40):
    if collective_id is None:
        return pltpu.CompilerParams(vmem_limit_bytes=limit * 2**20)
    return pltpu.CompilerParams(
        vmem_limit_bytes=limit * 2**20, collective_id=collective_id, has_side_effects=True
    )


def trig_table(group):
    cell = np.arange(GRID)
    rows = []
    for first in range(0, GRID // 2, group):
        for half in (0, 1):
            for k in range(first, first + group):
                angle = 2.0 * np.pi / GRID * (k * cell % GRID)
                if half == 0:
                    rows.append(np.cos(angle))
                elif k == 0:
                    rows.append(np.cos(np.pi * cell))
                else:
                    rows.append(np.sin(angle))
    return np.stack(rows)


def halves(table):
    high = table.astype(np.float32).astype(ml_dtypes.bfloat16)
    low = (table - high.astype(np.float64)).astype(np.float32).astype(ml_dtypes.bfloat16)
    return high, low


def split(values):
    high = values.astype(BF16)
    return high, (values - high.astype(F32)).astype(BF16)


def dot(a, b, contract=((1,), (0,))):
    return lax.dot_general(a, b, (contract, ((), ())), preferred_element_type=F32)


def dot3(a, b):
    return dot(
        jnp.concatenate([a[0], a[0], a[1]], axis=1), jnp.concatenate([b[0], b[1], b[0]], axis=0)
    )


def lanes_of(shape):
    return lax.broadcasted_iota(jnp.int32, shape, len(shape) - 1)


def roll(values, shift):
    return pltpu.roll(values, shift, len(values.shape) - 1)


def pack_lanes(u0, u1, u2, u3):
    lane = lanes_of(u0.shape)
    r1, r2, r3 = roll(u1, 96), roll(u2, 64), roll(u3, 32)
    return (
        jnp.where(lane < 96, u0, r1),
        jnp.where(lane < 64, r1, r2),
        jnp.where(lane < 32, r2, r3),
    )


def unpack_lanes(p0, p1, p2):
    lane = lanes_of(p0.shape)
    return (
        p0,
        roll(jnp.where(lane < 64, p1, p0), 32),
        roll(jnp.where(lane < 32, p2, p1), 64),
        roll(p2, 96),
    )


def hail(wide_count, narrow_count, offsets):
    w, n = lax.axis_index("wide"), lax.axis_index("narrow")
    for dw, dn in offsets:
        pl.semaphore_signal(
            pltpu.get_barrier_semaphore(),
            inc=1,
            device_id=(
                lax.rem(w + dw + wide_count, wide_count),
                lax.rem(n + dn + narrow_count, narrow_count),
            ),
            device_id_type=MESH,
        )


def hear(offsets):
    pl.semaphore_wait(pltpu.get_barrier_semaphore(), len(offsets))


GATHER = [(dw, dn) for dw in (-2, -1, 0, 1) for dn in (-1, 0, 1)]


def gather_kernel(
    wide_count,
    narrow_count,
    tractions_ref,
    centres_ref,
    anchors_ref,
    occupied_ref,
    out_ref,
    meta_ref,
    cells_ref,
    own_ref,
    held,
    send_sem,
    recv_sem,
):
    w, n = lax.axis_index("wide"), lax.axis_index("narrow")
    reach = [(dw, dn) for dw in (-2, -1, 0, 1, 2) for dn in (-1, 0, 1) if (dw, dn) != (0, 0)]
    hail(wide_count, narrow_count, reach)
    slots = [(a, b) for a in (0, 1) for b in (0, 1)]
    numbers = [centres_ref[a, b, c] for a, b in slots for c in range(3)]
    numbers += [anchors_ref[a, b, c].astype(F32) for a, b in slots for c in range(3)]
    numbers += [occupied_ref[a, b].astype(F32) for a, b in slots]
    lane = lanes_of((1, NODES))
    line = jnp.zeros((1, NODES), F32)
    for place, number in enumerate(numbers):
        line = jnp.where(lane == place, number, line)
    for s, (a, b) in enumerate(slots):
        own_ref[3 * s : 3 * s + 3, :] = tractions_ref[a, b]
    own_ref[12:16, :] = jnp.broadcast_to(line, (4, NODES))
    hear(reach)
    copies = []
    for place, (dw, dn) in enumerate(GATHER):
        if (dw, dn) == (0, 0):
            continue
        copy = pltpu.make_async_remote_copy(
            src_ref=own_ref,
            dst_ref=held.at[place],
            send_sem=send_sem.at[place],
            recv_sem=recv_sem.at[place],
            device_id=(
                lax.rem(w - dw + wide_count, wide_count),
                lax.rem(n - dn + narrow_count, narrow_count),
            ),
            device_id_type=MESH,
        )
        copy.start()
        copies.append((place, copy))
    own = GATHER.index((0, 0))
    out_ref[own] = own_ref[...]
    meta_ref[own : own + 1, :] = own_ref[12:13, 0:128]
    cells_ref[own : own + 1, :] = own_ref[12:13, 0:128].astype(jnp.int32)
    for place, copy in copies:
        copy.wait_recv()
        out_ref[place] = held[place]
        meta_ref[place : place + 1, :] = held[place, 12:13, 0:128]
        cells_ref[place : place + 1, :] = held[place, 12:13, 0:128].astype(jnp.int32)
    for place, copy in copies:
        copy.wait_send()


def near_field(sizes, list_ref, meta_ref, held_ref, off_ref, out_ref, offcol, source, columns):
    wide_count, narrow_count = sizes
    w, n = lax.axis_index("wide"), lax.axis_index("narrow")
    own = GATHER.index((0, 0))
    out_ref[...] = jnp.zeros_like(out_ref)
    columns[...] = jnp.zeros_like(columns)
    for s in range(SLOTS_DEV):
        for j in range(1 + NEAR):
            if j == 0:
                place, within = own, s
            else:
                entry = list_ref[s // 2, s % 2, j - 1]
                holder = entry // SLOTS_DEV
                within = entry % SLOTS_DEV
                row = lax.rem(holder // narrow_count - w + 1 + wide_count, wide_count)
                column = lax.rem(lax.rem(holder, narrow_count) - n + 1 + narrow_count, narrow_count)
                place = (jnp.minimum(row, 2) + 1) * 3 + jnp.minimum(column, 2)
            for c in range(3):
                if j == 0:
                    shift = 0.0
                else:
                    e = meta_ref[own, 3 * s + c] - meta_ref[place, 3 * within + c]
                    shift = e - jnp.where(e >= 128.0, 256.0, jnp.where(e < -128.0, -256.0, 0.0))
                source[j, c : c + 1, :] = shift - off_ref[c : c + 1, :]
                source[j, 3 + c : 4 + c, :] = held_ref[place, pl.ds(within * 3 + c, 1), :]

        def chunk(i, carry):
            for part in (0, 1):
                rows = pl.ds(pl.multiple_of(i * 16 + part * 8, 8), 8)
                sums = [jnp.zeros((8, 128), F32) for _ in range(3)]
                at = [offcol[c, rows, :] for c in range(3)]
                for j in range(1 + NEAR):
                    for half in (0, 1):
                        lanes = slice(half * 128, half * 128 + 128)
                        d = [at[c] + source[j, c : c + 1, lanes] for c in range(3)]
                        f = [source[j, 3 + c : 4 + c, lanes] for c in range(3)]
                        r2 = d[0] * d[0] + d[1] * d[1] + d[2] * d[2]
                        inverse = lax.rsqrt(r2 + soften)
                        weight = jnp.exp(r2 * (-screen)) * (inverse * inverse * inverse)
                        along = (d[0] * f[0] + d[1] * f[1] + d[2] * f[2]) * weight
                        diagonal = (r2 + 2.0 * soften) * weight
                        for c in range(3):
                            sums[c] = sums[c] + (diagonal * f[c] + d[c] * along)
                for c in range(3):
                    columns[rows, c : c + 1] = jnp.sum(sums[c], axis=1, keepdims=True)
            return carry

        lax.fori_loop(0, NODES // 16, chunk, 0)
        result = jnp.transpose(columns[...])
        alive = jnp.where(meta_ref[own, 24 + s] > 0.5, near_scale, 0.0)
        out_ref[3 * s : 3 * s + 3, :] = alive * result[0:3, :]


def columns_of(off_ref, offcol):
    padded = jnp.concatenate([off_ref[...], jnp.zeros((5, NODES), F32)], axis=0)
    turned = jnp.transpose(padded)
    for c in range(3):
        offcol[c] = jnp.broadcast_to(turned[:, c : c + 1], (NODES, 128))


def sphere_weights(sizes, dw, dn, s, meta_ref, cells_ref, off_ref, offcol, tz_ref):
    wide_count, narrow_count = sizes
    w, n = lax.axis_index("wide"), lax.axis_index("narrow")
    size_x, size_y = GRID // wide_count, GRID // narrow_count
    place = (dw + 2) * 3 + dn + 1
    anchor = [cells_ref[place, 12 + 3 * s + c] for c in range(3)]
    centre = [meta_ref[place, 3 * s + c] for c in range(3)]
    alive = jnp.where(meta_ref[place, 24 + s] > 0.5, spread_norm, 0.0)
    low_x = anchor[0] - size_x * lax.rem(w + dw + wide_count, wide_count) + size_x * dw
    low_y = anchor[1] - size_y * lax.rem(n + dn + narrow_count, narrow_count) + size_y * dn
    low_z = anchor[2] % 8

    def weights(cell, position, base, low, factor):
        distance = position - (base + cell).astype(F32)
        inside = (cell >= low) & (cell < low + BLOCK)
        return jnp.where(inside, jnp.exp(-distance * distance) * factor, 0.0)

    def rows(c, low, count, factor):
        cell = lax.broadcasted_iota(jnp.int32, (count, NODES), 0)
        return weights(cell, centre[c] + off_ref[c : c + 1, :], anchor[c] - low, low, factor)

    lane = lanes_of((NODES, 128))
    wz = weights(lane % 32, centre[2] + offcol[2], anchor[2] - low_z, low_z, 1.0)
    high = wz.astype(BF16).astype(F32)
    left = jnp.where(lane < 64, high, jnp.where(lane < 96, wz - high, 0.0)).astype(BF16)
    tile = anchor[2] // 8
    t_high, t_low = split(jnp.concatenate([tz_ref[tile + t] for t in range(4)], axis=0))
    right = jnp.concatenate([t_high, t_low, t_high, jnp.zeros((32, GRID), BF16)], axis=0)
    along_z = split(dot(left, right))
    return place, rows(0, low_x, size_x, alive), rows(1, low_y, 16 if dn else size_y, 1.0), along_z


def pair_loop(body, dn, unroll=1):
    def step(index, carry):
        body(index // 2 - 2, dn, index % 2)
        return carry

    lax.fori_loop(0, 6, step, 0, unroll=unroll)


def spread(sizes, meta_ref, cells_ref, held_ref, off_ref, tz_ref, out_ref, offcol, a_high, a_low, total, turned):
    total[...] = jnp.zeros_like(total)

    def pair(dw, dn, which):
        span = 16 if dn else 32
        sums = []
        for member in (0, 1):
            s = 2 * which + member
            place, wx, wy, along_z = sphere_weights(sizes, dw, dn, s, meta_ref, cells_ref, off_ref, offcol, tz_ref)
            planar = jnp.concatenate(
                [wy * held_ref[place, pl.ds(s * 3 + c, 1), :] for c in range(3)], axis=0
            )
            size = 3 * span
            for x in range(8):
                high, low = split(planar * wx[x : x + 1, :])
                a_high[member, x * size : x * size + size, :] = high
                a_low[member, x * size : x * size + size, :] = low
            rows = slice(0, 8 * size)
            sums.append(dot3((a_high[member, rows, :], a_low[member, rows, :]), along_z))
        both = sums[0] + sums[1]
        if dn == 0:
            total[...] += both
        else:
            for block in range(24):
                total[block * 32 : block * 32 + 16, :] += both[block * 16 : block * 16 + 16]

    pair_loop(pair, -1)
    pair_loop(pair, 0)
    for x in range(8):
        block = jnp.concatenate([total[x * 96 : x * 96 + 96, :], jnp.zeros((32, GRID), F32)], axis=0)
        turned[pl.ds(x, GRID, stride=8), :] = jnp.transpose(block)
    values = turned[...].reshape(64, 4, 8, 128)
    packed = pack_lanes(*[values[:, j] for j in range(4)])
    for g in range(3):
        out_ref[:, :, :, g * 128 : g * 128 + 128] = packed[g].reshape(32, 2, 8, 128)


def mean_weights(sizes, meta_ref, cells_ref, off_ref, tz_ref, offcol, full, half):
    def pair(dw, dn, which):
        span = 16 if dn else 32
        for member in (0, 1):
            s = 2 * which + member
            place, wx, wy, along_z = sphere_weights(
                sizes, dw, dn, s, meta_ref, cells_ref, off_ref, offcol, tz_ref
            )
            wy = wy * (1.0 / NODES)
            left = split(jnp.concatenate([wy * wx[x : x + 1, :] for x in range(8)], axis=0))
            target = half if dn else full
            target[(dw + 2) * 4 + s] = dot3(left, along_z)

    pair_loop(pair, -1)
    pair_loop(pair, 0)


def mean_velocities(values, full, half, rows_ref):
    rows_ref[...] = jnp.zeros_like(rows_ref)
    for dn in (-1, 0):
        span = 16 if dn else 32

        def sphere(index, carry):
            source = half if dn else full
            tiles = [jnp.zeros((8, GRID), F32) for _ in range(3)]
            for x in range(8):
                for y in range(0, span, 8):
                    weight = source[index, x * span + y : x * span + y + 8, :]
                    for c in range(3):
                        at = x * 96 + c * 32 + y
                        tiles[c] = tiles[c] + values[at : at + 8, :] * weight
            piece = (index // 4) * 2 + dn + 1
            for c in range(3):
                rows_ref[piece, pl.ds((index % 4) * 3 + c, 1), :] = jnp.sum(tiles[c], axis=0, keepdims=True)
            return carry

        lax.fori_loop(0, 12, sphere, 0)


def unpack_mesh(mesh_ref, values, m_high, m_low, h_high, h_low, turned):
    groups = [mesh_ref[:, :, :, g * 128 : g * 128 + 128].reshape(64, 8, 128) for g in range(3)]
    unpacked = unpack_lanes(*groups)
    turned[...] = jnp.stack(unpacked, axis=1).reshape(GRID * 8, 128)
    for x in range(8):
        block = jnp.transpose(turned[pl.ds(x, GRID, stride=8), :])[:96]
        values[x * 96 : x * 96 + 96, :] = block
        high, low = split(block)
        m_high[x * 96 : x * 96 + 96, :] = high
        m_low[x * 96 : x * 96 + 96, :] = low
        for c in range(3):
            target = slice(x * 48 + c * 16, x * 48 + c * 16 + 16)
            h_high[target, :] = high[c * 32 : c * 32 + 16]
            h_low[target, :] = low[c * 32 : c * 32 + 16]


def interpolate(
    sizes, lower, meta_ref, cells_ref, off_ref, tz_ref, out_ref, offcol, m_high, m_low, h_high, h_low
):
    def pair(dw, dn, which):
        span = 16 if dn else 32
        size = 3 * span
        for member in (0, 1):
            s = 2 * which + member
            place, wx, wy, along_z = sphere_weights(sizes, dw, dn, s, meta_ref, cells_ref, off_ref, offcol, tz_ref)
            left = (h_high[...], h_low[...]) if dn else (m_high[...], m_low[...])
            turn = ((1,), (1,))
            found = dot(
                jnp.concatenate([left[0], left[0], left[1]], axis=1),
                jnp.concatenate([along_z[0], along_z[1], along_z[0]], axis=1),
                turn,
            )
            summed = found[0:size] * wx[0:1, :]
            for x in range(1, 8):
                summed = summed + found[x * size : x * size + size] * wx[x : x + 1, :]
            owner = (dw + 2) * 2 + dn + 1
            for c in range(3):
                out_ref[owner, pl.ds(s * 3 + c, 1), :] = jnp.sum(
                    summed[c * span : c * span + span] * wy, axis=0, keepdims=True
                )

    pair_loop(pair, lower, 2)


AROUND = [(dw, dn) for dw in (-1, 0, 1) for dn in (-1, 0, 1)]
PARTIAL = [(dw, dn) for dw in (-2, -1, 0) for dn in (-1, 0)]


def shift_narrow(values, dn, narrow_count):
    if dn == 0:
        return values
    place = lanes_of(values.shape) % narrow_count
    edge = 0 if dn == 1 else narrow_count - 1
    total = values.shape[-1]
    return jnp.where(
        place == edge,
        roll(values, (dn - dn * narrow_count) % total),
        roll(values, dn % total),
    )


def shift_wide(values, dw, narrow_count):
    if dw == 0:
        return values
    return roll(values, (dw * narrow_count) % values.shape[-1])


class Exchange:
    def __init__(self, axis, count, source, target, half, send_sem, recv_sem, me, other):
        self.__dict__.update(locals())

    def copy_to(self, step):
        to = lax.rem(self.me + step, self.count)
        return pltpu.make_async_remote_copy(
            src_ref=self.source.at[to, self.half],
            dst_ref=self.target.at[self.me, self.half],
            send_sem=self.send_sem.at[step],
            recv_sem=self.recv_sem.at[step],
            device_id=(to, self.other) if self.axis == "wide" else (self.other, to),
            device_id_type=MESH,
        )

    def begin(self):
        def step(index, carry):
            self.copy_to(index).start()
            return carry

        lax.fori_loop(1, self.count, step, 0)
        self.target[self.me, self.half] = self.source[self.me, self.half]

    def arrive(self):
        def step(index, carry):
            self.copy_to(index).wait_recv()
            return carry

        lax.fori_loop(1, self.count, step, 0)

    def sent(self):
        def step(index, carry):
            self.copy_to(index).wait_send()
            return carry

        lax.fori_loop(1, self.count, step, 0)


def flow_kernel(
    wide_count,
    narrow_count,
    list_ref,
    meta_ref,
    cells_ref,
    held_ref,
    off_ref,
    tz_ref,
    pairs_ref,
    gap_ref,
    angles_ref,
    tables,
    velocity_ref,
    force_ref,
    moved_ref,
    near_ref,
    m_high,
    m_low,
    h_high,
    h_low,
    full_means,
    half_means,
    mean_rows,
    part_ref,
    part_in,
    tile_out,
    tile_in,
    table_out,
    table_in,
    edges,
    fields,
    around,
    loads,
    relatives,
    forces,
    part_send,
    part_recv,
    tile_send,
    tile_recv,
    spread_send,
    spread_recv,
    a_high,
    a_low,
    total,
    turned,
    mesh_ref,
    wide_in,
    narrow_out,
    narrow_in,
    narrow_back,
    narrow_home,
    wide_back,
    wide_home,
    lines,
    spectrum,
    t_x,
    t_yf,
    t_yi,
    offcol,
    source,
    columns,
    own_line,
    lines_in,
    column_out,
    column_in,
    wide_send,
    wide_recv,
    narrow_send,
    narrow_recv,
    table_sem,
    line_send,
    line_recv,
    column_send,
    column_recv,
):
    w, n = lax.axis_index("wide"), lax.axis_index("narrow")
    load = pltpu.make_async_copy(tables, t_x, table_sem)
    load.start()
    reach = (
        [(step, 0) for step in range(1, wide_count)]
        + [(0, step) for step in range(1, narrow_count)]
        + [(-2, -1), (-1, -1), (2, 1), (1, 1)]
    )
    sizes = (wide_count, narrow_count)
    hail(*sizes, reach)
    columns_of(off_ref, offcol)
    spread(sizes, meta_ref, cells_ref, held_ref, off_ref, tz_ref, mesh_ref, offcol, a_high, a_low, total, turned)
    hear(reach)

    def exchanges(axis, source, target, way):
        if axis == "wide":
            fixed = (wide_count, w, n, wide_send, wide_recv)
        else:
            fixed = (narrow_count, n, w, narrow_send, narrow_recv)
        count, me, other, send_sem, recv_sem = fixed
        return [
            Exchange(
                axis, count, source, target, half, send_sem.at[way, half], recv_sem.at[way, half], me, other
            )
            for half in (0, 1)
        ]

    wide_go = exchanges("wide", mesh_ref, wide_in, 0)
    narrow_go = exchanges("narrow", narrow_out, narrow_in, 0)
    narrow_return = exchanges("narrow", narrow_back, narrow_home, 1)
    wide_return = exchanges("wide", wide_back, wide_home, 1)
    for half in (0, 1):
        wide_go[half].begin()

    ids = pairs_ref[...]
    within = (ids % SLOTS_DEV).astype(F32)
    holder = ids // SLOTS_DEV
    row_w = lax.rem(holder // narrow_count - w + 1 + wide_count, wide_count)
    row_n = lax.rem(lax.rem(holder, narrow_count) - n + 1 + narrow_count, narrow_count)
    seconds = ((row_w * 3 + row_n) * SLOTS_DEV).astype(F32) + within
    polar, azimuth = angles_ref[0:1, :], angles_ref[1:2, :]
    across = jnp.sin(polar)
    parts = [
        within[0:1],
        seconds[1:2],
        across * jnp.cos(azimuth),
        across * jnp.sin(azimuth),
        jnp.cos(polar),
        gap_ref[...].reshape(1, CONT_DEV),
    ]
    line = jnp.concatenate(parts + [jnp.zeros((1, 64), F32)], axis=1)
    own_line[...] = jnp.where(lax.broadcasted_iota(jnp.int32, (8, NODES), 0) == n, line, 0.0)

    def line_copy(step):
        return pltpu.make_async_remote_copy(
            src_ref=own_line,
            dst_ref=lines_in.at[step],
            send_sem=line_send.at[step],
            recv_sem=line_recv.at[step],
            device_id=(w, lax.rem(n + step, narrow_count)),
            device_id_type=MESH,
        )

    def column_copy(step):
        return pltpu.make_async_remote_copy(
            src_ref=column_out,
            dst_ref=column_in.at[w],
            send_sem=column_send.at[step],
            recv_sem=column_recv.at[step],
            device_id=(lax.rem(w + step, wide_count), n),
            device_id_type=MESH,
        )

    for step in range(1, narrow_count):
        line_copy(step).start()
    mean_weights(sizes, meta_ref, cells_ref, off_ref, tz_ref, offcol, full_means, half_means)
    load.wait()
    t_yf[...] = jnp.zeros_like(t_yf)
    for part in (0, 1):
        for piece in range(8):
            for c in range(3):
                t_yf[part, piece * 128 + c * 32 : piece * 128 + c * 32 + 32, c * 256 : c * 256 + 256] = t_x[
                    4 + part, piece * 32 : piece * 32 + 32, :
                ]
        for piece in range(8):
            for c in range(3):
                block = t_yf[part, piece * 128 : piece * 128 + 128, c * 256 : c * 256 + 256]
                t_yi[part, c * 256 : c * 256 + 256, piece * 128 : piece * 128 + 128] = jnp.transpose(
                    block.astype(F32)
                ).astype(BF16)
    for half in (0, 1):
        wide_go[half].arrive()
        block = split(wide_in[:, half].reshape(GRID, 384))
        along = dot3((t_x[0], t_x[1]), block)
        narrow_out[:, half] = along.reshape(narrow_count, 32, 384)
        narrow_go[half].begin()
    column = own_line[...]
    for step in range(1, narrow_count):
        line_copy(step).wait_recv()
        column = column + lines_in[step]
    column_out[...] = column
    column_in[w] = column

    def begin_column(step, carry):
        column_copy(step).start()
        return carry

    lax.fori_loop(1, wide_count, begin_column, 0)
    row = lax.broadcasted_iota(jnp.int32, (32, 1), 0)
    k_x = (n * 16 + row % 16).astype(F32)
    nyquist_x = jnp.where((row >= 16) & (k_x < 0.5), 128.0, 0.0)
    lane = lax.broadcasted_iota(jnp.int32, (1, GRID), 1)
    k_y = (lane % 128).astype(F32)
    nyquist_y = jnp.where((lane >= 128) & (k_y < 0.5), 128.0, 0.0)
    square_xy = k_x * k_x + nyquist_x * nyquist_x + (k_y * k_y + nyquist_y * nyquist_y)
    scale_x = jnp.where(k_x < 0.5, 1.0, 2.0)
    scale_y = jnp.where(k_y < 0.5, 1.0, 2.0)
    scale_xy = scale_x * scale_y
    damping = (ewald_split * np.pi / GRID) ** 2
    constant = GRID * GRID / (4.0 * np.pi * np.pi) / float(GRID) ** 3
    turn_x = jnp.where(row < 16, k_x, -k_x)
    turn_y = jnp.where(lane < 128, k_y, -k_y)

    def derive_x(values):
        return turn_x * jnp.concatenate([values[16:], values[:16]], axis=0)

    def derive_y(values):
        return turn_y * jnp.concatenate([values[:, 128:], values[:, :128]], axis=1)

    def filtered(index, group):
        k_z = (w * 4 + group * 2 + index).astype(F32)
        bases = [pl.multiple_of(group * 128 + half * 64 + index * 32, 32) for half in (0, 1)]
        fields = [
            [spectrum[pl.ds(bases[half], 32), c * 256 : c * 256 + 256] for c in range(3)]
            for half in (0, 1)
        ]
        flows = []
        nyquists_z = [jnp.zeros_like(k_z), jnp.where(k_z < 0.5, 128.0, 0.0)]
        scale_z = jnp.where(k_z < 0.5, 1.0, 2.0)
        turn_z = (k_z, -k_z)
        for half in (0, 1):
            values = fields[half]
            flows.append(derive_x(values[0]) + derive_y(values[1]) + turn_z[half] * fields[1 - half][2])
        for half in (0, 1):
            values = fields[half]
            nyquist_z = nyquists_z[half]
            square = square_xy + (k_z * k_z + nyquist_z * nyquist_z)
            safe = jnp.maximum(square, 1.0)
            inverse = 1.0 / safe
            factor = jnp.where(square > 0.5, jnp.exp(-damping * square) * inverse, 0.0)
            factor = factor * (scale_xy * (scale_z * constant))
            edge = (nyquist_x * values[0] + nyquist_y * values[1] + nyquist_z * values[2]) * inverse
            flow = [flows[half] * inverse, flows[1 - half] * inverse]
            gradient = [derive_x(flow[0]), derive_y(flow[0]), None]
            gradient[2] = turn_z[half] * (flows[1 - half] * inverse)
            nyquist = (nyquist_x, nyquist_y, nyquist_z)
            for c in range(3):
                spectrum[pl.ds(bases[half], 32), c * 256 : c * 256 + 256] = factor * (
                    values[c] + gradient[c] - nyquist[c] * edge
                )
        return group

    for half in (0, 1):
        narrow_go[half].arrive()
        for piece in range(8):
            groups = [narrow_in[piece, half, :, g * 128 : g * 128 + 128] for g in range(3)]
            unpacked = unpack_lanes(*groups)
            for j in range(4):
                lines[half * 128 + j * 32 : half * 128 + j * 32 + 32, piece * 128 : piece * 128 + 128] = unpacked[j]
        rows = slice(half * 128, half * 128 + 128)
        spectrum[rows, :] = dot3(split(lines[rows, :]), (t_yf[0], t_yf[1]))
        lax.fori_loop(0, 2, filtered, half)
        lines[rows, :] = dot3(split(spectrum[rows, :]), (t_yi[0], t_yi[1]))
        for target in range(8):
            groups = [
                lines[half * 128 + j * 32 : half * 128 + j * 32 + 32, target * 128 : target * 128 + 128]
                for j in range(4)
            ]
            packed = pack_lanes(*groups)
            for g in range(3):
                narrow_back[target, half, :, g * 128 : g * 128 + 128] = packed[g]
        narrow_return[half].begin()
    for half in (0, 1):
        narrow_return[half].arrive()
        block = split(narrow_home[:, half].reshape(GRID, 384))
        along = dot3((t_x[2], t_x[3]), block)
        wide_back[:, half] = along.reshape(wide_count, 8, 384)
        wide_return[half].begin()
    near_field(
        (wide_count, narrow_count), list_ref, meta_ref, held_ref, off_ref, near_ref, offcol, source, columns
    )
    def end_column(step, carry):
        column_copy(step).wait()
        return carry

    lax.fori_loop(1, wide_count, end_column, 0)
    for step in range(1, narrow_count):
        line_copy(step).wait_send()
    fields[...] = jnp.transpose(column_in[...].reshape(wide_count * narrow_count, NODES))
    sphere = lax.broadcasted_iota(jnp.int32, (EDGE_ROWS, 1), 0)
    component = sphere % 3
    sphere = (sphere // 3).astype(F32)

    def incidence(i, carry):
        first, second = fields[pl.ds(i, 1), :] + 4.0 * SLOTS_DEV, fields[pl.ds(32 + i, 1), :]
        normal = [fields[pl.ds(64 + 32 * c + i, 1), :] for c in range(3)]
        along = jnp.where(component == 0, normal[0], jnp.where(component == 1, normal[1], normal[2]))
        sign = jnp.where(sphere == first, 1.0, 0.0) - jnp.where(sphere == second, 1.0, 0.0)
        edges[i] = sign * along
        return carry

    lax.fori_loop(0, CONT_DEV, incidence, 0)
    for group in (wide_go, narrow_go, narrow_return):
        for half in (0, 1):
            group[half].sent()
    for half in (0, 1):
        wide_return[half].arrive()
    unpack_mesh(wide_home, total, m_high, m_low, h_high, h_low, turned)
    mean_velocities(total, full_means, half_means, mean_rows)

    def device(dw, dn):
        return (
            lax.rem(w + dw + wide_count, wide_count),
            lax.rem(n + dn + narrow_count, narrow_count),
        )

    devices = wide_count * narrow_count
    own = PARTIAL.index((0, 0))
    means = [jnp.sum(mean_rows[p], axis=1, keepdims=True) for p in range(6)]
    means[own] = means[own] + jnp.sum(near_ref[...], axis=1, keepdims=True) * (1.0 / NODES)
    column = jnp.concatenate(means + [jnp.zeros((32, 1), F32)], axis=0)
    line = jnp.transpose(jnp.broadcast_to(column, (128, 128)))[:8]
    tile_out[...] = jnp.where(lax.broadcasted_iota(jnp.int32, (8, 128), 0) == n, line, 0.0)

    def narrow_copy(step):
        to = lax.rem(n + step, narrow_count)
        return pltpu.make_async_remote_copy(
            src_ref=tile_out,
            dst_ref=tile_in.at[step],
            send_sem=tile_send.at[step],
            recv_sem=tile_recv.at[step],
            device_id=(w, to),
            device_id_type=MESH,
        )

    def wide_copy(step):
        to = lax.rem(w + step, wide_count)
        return pltpu.make_async_remote_copy(
            src_ref=table_out,
            dst_ref=table_in.at[w],
            send_sem=spread_send.at[step],
            recv_sem=spread_recv.at[step],
            device_id=(to, n),
            device_id_type=MESH,
        )

    for step in range(1, narrow_count):
        narrow_copy(step).start()
    part_ref[...] = jnp.zeros_like(part_ref)
    fixed = (meta_ref, cells_ref, off_ref, tz_ref, part_ref, offcol, m_high, m_low, h_high, h_low)
    interpolate(sizes, -1, *fixed)
    tile = tile_out[...]
    for step in range(1, narrow_count):
        narrow_copy(step).wait_recv()
        tile = tile + tile_in[step]
    table_out[...] = tile
    table_in[w] = tile

    def begin(step, carry):
        wide_copy(step).start()
        return carry

    lax.fori_loop(1, wide_count, begin, 0)

    interpolate(sizes, 0, *fixed)
    copies = []
    for place, (dw, dn) in enumerate(PARTIAL):
        if (dw, dn) == (0, 0):
            continue
        copy = pltpu.make_async_remote_copy(
            src_ref=part_ref.at[place],
            dst_ref=part_in.at[place],
            send_sem=part_send.at[place],
            recv_sem=part_recv.at[place],
            device_id=device(dw, dn),
            device_id_type=MESH,
        )
        copy.start()
        copies.append((place, copy))
    def end(step, carry):
        wide_copy(step).wait_recv()
        return carry

    lax.fori_loop(1, wide_count, end, 0)
    spread_means = jnp.transpose(table_in[...].reshape(devices, 128))
    hydro = jnp.zeros((16, devices), F32)
    for p, (dw, dn) in enumerate(PARTIAL):
        moved_means = shift_wide(spread_means[p * 16 : p * 16 + 16], dw, narrow_count)
        hydro = hydro + shift_narrow(moved_means, dn, narrow_count)

    gap = fields[160:192, :]

    def totals():
        def one_contact(i, sums):
            return sums + edges[i] * forces[pl.ds(i, 1), :]

        loads[...] = lax.fori_loop(
            0, CONT_DEV, one_contact, jnp.zeros((EDGE_ROWS, devices), F32), unroll=4
        )
        result = jnp.zeros((ROWS_DEV, devices), F32)
        for dn in (-1, 0, 1):
            inner = jnp.zeros((ROWS_DEV, devices), F32)
            for dw in (-1, 0, 1):
                start = AROUND.index((dw, dn)) * ROWS_DEV
                inner = inner + shift_wide(loads[start : start + ROWS_DEV, :], dw, narrow_count)
            result = result + shift_narrow(inner, dn, narrow_count)
        return jnp.concatenate([result, jnp.zeros((16 - ROWS_DEV, devices), F32)], axis=0)

    def sweep(turn, moving):
        for dn in (-1, 0, 1):
            beside = shift_narrow(moving, -dn, narrow_count)
            for dw in (-1, 0, 1):
                start = AROUND.index((dw, dn)) * ROWS_DEV
                around[start : start + ROWS_DEV, :] = shift_wide(beside, -dw, narrow_count)[:ROWS_DEV]

        def eight_contacts(block, carry):
            rows = [
                jnp.sum(edges[block * 8 + i] * around[...], axis=0, keepdims=True) for i in range(8)
            ]
            at = pl.ds(pl.multiple_of(block * 8, 8), 8)
            relatives[at, :] = jnp.concatenate(rows, axis=0)
            return carry

        lax.fori_loop(0, CONT_DEV // 8, eight_contacts, 0)
        forces[...] = jnp.maximum(
            forces[...]
            - relaxation * (gap + time_step * relatives[...]) / (2.0 * time_step * mobility),
            0.0,
        )
        return hydro + mobility * totals()

    around[...] = jnp.zeros_like(around)
    forces[...] = jnp.zeros_like(forces)
    moving = lax.fori_loop(0, SWEEPS, sweep, hydro)
    force = forces[...]
    mine = lanes_of((1, devices)) == w * narrow_count + n
    own_force = jnp.sum(jnp.where(mine, force, 0.0), axis=1, keepdims=True)
    force_ref[...] = jnp.broadcast_to(own_force, (CONT_DEV, 128))
    own_moving = jnp.sum(jnp.where(mine, moving, 0.0), axis=1, keepdims=True)
    row = lax.broadcasted_iota(jnp.int32, (16, 128), 0)
    centre = jnp.zeros((16, 128), F32)
    for k in range(ROWS_DEV):
        centre = jnp.where(row == k, meta_ref[GATHER.index((0, 0)), k], centre)
    moved_ref[...] = centre + time_step * own_moving
    velocity = part_ref[own] + near_ref[...]
    for place, copy in copies:
        copy.wait_recv()
        velocity = velocity + part_in[place]
    velocity_ref[...] = velocity
    for place, copy in copies:
        copy.wait_send()
    for half in (0, 1):
        wide_return[half].sent()
    for step in range(1, narrow_count):
        narrow_copy(step).wait_send()

    def finish(step, carry):
        wide_copy(step).wait_send()
        return carry

    lax.fori_loop(1, wide_count, finish, 0)


def local(
    wide_count,
    narrow_count,
    tractions,
    centers,
    node_offsets,
    occupied,
    anchors,
    near_list,
    contact_pairs,
    contact_gap,
    contact_angles,
):
    w, n = lax.axis_index("wide"), lax.axis_index("narrow")
    sizes = (wide_count, narrow_count)
    shape = jax.ShapeDtypeStruct
    dma = pltpu.SemaphoreType.DMA

    held, metas, cells = pl.pallas_call(
        functools.partial(gather_kernel, *sizes),
        out_shape=(shape((12, 16, NODES), F32), shape((12, 128), F32), shape((12, 128), jnp.int32)),
        in_specs=[VMEM_SPEC, SMEM_SPEC, SMEM_SPEC, SMEM_SPEC],
        out_specs=(VMEM_SPEC,) * 3,
        scratch_shapes=[
            pltpu.VMEM((16, NODES), F32),
            pltpu.VMEM((12, 16, NODES), F32),
            dma((12,)),
            dma((12,)),
        ],
        compiler_params=params(0),
        name="gather",
    )(tractions, centers, anchors, occupied)

    table_z = trig_table(2)
    wrapped_z = np.concatenate([table_z, table_z[:, :32]], axis=1).T.astype(np.float32).reshape(36, 8, GRID)
    table_x = trig_table(16)
    table_y = trig_table(128)
    turned_x = np.ascontiguousarray(table_x.T)
    turned_y = np.ascontiguousarray(table_y.T)
    tables = np.stack([*halves(table_x), *halves(turned_x), *halves(turned_y)])
    devices = wide_count * narrow_count
    velocity, force, moved = pl.pallas_call(
        functools.partial(flow_kernel, *sizes),
        out_shape=(shape((16, NODES), F32), shape((CONT_DEV, 128), F32), shape((16, 128), F32)),
        in_specs=[SMEM_SPEC] * 3 + [VMEM_SPEC] * 6 + [HBM_SPEC],
        out_specs=(VMEM_SPEC,) * 3,
        scratch_shapes=[
            pltpu.VMEM((16, NODES), F32),
            pltpu.VMEM((768, GRID), BF16),
            pltpu.VMEM((768, GRID), BF16),
            pltpu.VMEM((384, GRID), BF16),
            pltpu.VMEM((384, GRID), BF16),
            pltpu.VMEM((12, 256, GRID), F32),
            pltpu.VMEM((12, 128, GRID), F32),
            pltpu.VMEM((6, 16, NODES), F32),
            pltpu.VMEM((6, 16, NODES), F32),
            pltpu.VMEM((6, 16, NODES), F32),
            pltpu.VMEM((8, 128), F32),
            pltpu.VMEM((8, 8, 128), F32),
            pltpu.VMEM((8, 128), F32),
            pltpu.VMEM((32, 8, 128), F32),
            pltpu.VMEM((CONT_DEV, EDGE_ROWS, devices), F32),
            pltpu.VMEM((NODES, devices), F32),
            pltpu.VMEM((EDGE_ROWS, devices), F32),
            pltpu.VMEM((EDGE_ROWS, devices), F32),
            pltpu.VMEM((CONT_DEV, devices), F32),
            pltpu.VMEM((CONT_DEV, devices), F32),
            dma((6,)),
            dma((6,)),
            dma((8,)),
            dma((8,)),
            dma((32,)),
            dma((32,)),
            pltpu.VMEM((2, 768, NODES), BF16),
            pltpu.VMEM((2, 768, NODES), BF16),
            pltpu.VMEM((768, GRID), F32),
            pltpu.VMEM((GRID * 8, 128), F32),
            pltpu.VMEM((32, 2, 8, 384), F32),
            pltpu.VMEM((32, 2, 8, 384), F32),
            pltpu.VMEM((8, 2, 32, 384), F32),
            pltpu.VMEM((8, 2, 32, 384), F32),
            pltpu.VMEM((8, 2, 32, 384), F32),
            pltpu.VMEM((8, 2, 32, 384), F32),
            pltpu.VMEM((32, 2, 8, 384), F32),
            pltpu.VMEM((32, 2, 8, 384), F32),
            pltpu.VMEM((256, 1024), F32),
            pltpu.VMEM((256, 768), F32),
            pltpu.VMEM((6, 256, 256), BF16),
            pltpu.VMEM((2, 1024, 768), BF16),
            pltpu.VMEM((2, 768, 1024), BF16),
            pltpu.VMEM((3, NODES, 128), F32),
            pltpu.VMEM((3, 8, NODES), F32),
            pltpu.VMEM((NODES, 8), F32),
            pltpu.VMEM((8, NODES), F32),
            pltpu.VMEM((8, 8, NODES), F32),
            pltpu.VMEM((8, NODES), F32),
            pltpu.VMEM((32, 8, NODES), F32),
            dma((2, 2, 32)),
            dma((2, 2, 32)),
            dma((2, 2, 8)),
            dma((2, 2, 8)),
            dma,
            dma((8,)),
            dma((8,)),
            dma((32,)),
            dma((32,)),
        ],
        compiler_params=params(1, 40),
        name="flow",
    )(
        near_list,
        metas,
        cells,
        held,
        node_offsets,
        wrapped_z,
        contact_pairs,
        contact_gap,
        contact_angles,
        tables,
    )
    return (
        velocity[:12].reshape(2, 2, 3, NODES),
        force[:, 0],
        moved[:12, 0].reshape(2, 2, 3),
    )


def solution(mesh):
    placed = (
        P("wide", "narrow", None, None),
        P("wide", "narrow", None),
        P(),
        P("wide", "narrow"),
        P("wide", "narrow", None),
        P("wide", "narrow", None),
        P(None, ("wide", "narrow")),
        P(("wide", "narrow")),
        P(None, ("wide", "narrow")),
    )
    return jax.shard_map(
        functools.partial(local, mesh.shape["wide"], mesh.shape["narrow"]),
        mesh=mesh,
        in_specs=placed,
        out_specs=(
            P("wide", "narrow", None, None),
            P(("wide", "narrow")),
            P("wide", "narrow", None),
        ),
        check_vma=False,
    )
```
